128 devices in a mesh: dp: 16 (over x_lo, z, core), ctx: 8 (over x_hi, y).
Axes of the slice: x: 4 (x_hi: 2, x_lo: 2; x = x_hi * 2 + x_lo), y: 4, z: 4, core: 2. Of those that a mesh axis runs over, the one named last changes fastest.
Arguments:
- hidden_rows: bfloat16 [16, 2048, 8192], P('dp', 'ctx'), may hold values from -6 to 6
- inner_rows: bfloat16 [16, 2048, 8192], P('dp', 'ctx'), may hold values from -6 to 6
- weight_proj: bfloat16 [8192, 320], P('dp'), may hold values from -0.03125 to 0.03125
- decay_log: float32 [64], replicated, as said below
- step_bias: float32 [64], replicated, may hold values from -0.5 to 0.5
- skip_gain: float32 [64], replicated, may hold values from 0.5 to 1.5
- grad_output: bfloat16 [16, 2048, 8192], P('dp', 'ctx'), may hold values from -6 to 6
Outputs:
- ssd_output: bfloat16 [16, 2048, 8192], P('dp', 'ctx')
- grad_inner: bfloat16 [16, 2048, 8192], P('dp', 'ctx')
- grad_hidden: bfloat16 [16, 2048, 8192], P('dp', 'ctx')
- grad_weight: float32 [8192, 320], P('dp')
The draws below stay inside these ranges and needn't reach their ends.
Inputs may be any that keep to these rules, and one draw needn't show every extreme that they name: -exp(decay_log) is each head's decay rate per unit of step size.
All inputs are finite; a program needn't handle non-finite values.
Results may differ from the reference program's by a relative error of at most 0.005.
Values may be sent and summed in bfloat16 or wider, within the bound.
A program may use at most 384 MiB of HBM per device.

```python
import math
from functools import partial
import jax
import jax.numpy as jnp
from jax import lax

D = 8192
H = 64
P_SIZE = 128
N = 128
BLOCK = 128
SEQ = 2048
BATCH = 16
COLS = 320


def draw_decay_log(key, part):
    key_one, key_two, key_three = jax.random.split(jax.random.fold_in(key, 11), 3)
    slow_share = 5
    head_picks = jax.random.randint(key_one, (H,), 0, 10)
    is_slow = head_picks < slow_share
    slow_rates = jax.random.uniform(key_two, (H,), minval=0.3, maxval=1.5) / SEQ
    fast_rates = jnp.exp(jax.random.uniform(key_three, (H,), minval=math.log(0.03), maxval=math.log(0.12)))
    return jnp.log(jnp.where(is_slow, slow_rates, fast_rates)).astype(jnp.float32)


def steps_of(stream_key, extent, cuts, least, high):
    def one(axis_at, blocks):
        heights = jax.random.uniform(jax.random.fold_in(jax.random.fold_in(stream_key, 6), axis_at), (blocks,), jnp.float32, least / len(cuts), high / len(cuts))
        return jnp.repeat(jnp.exp(heights), extent[axis_at] // blocks).reshape((-1,) + (1,) * (len(extent) - axis_at - 1))

    loudness = one(*cuts[0])
    for cut in cuts[1:]:
        loudness = loudness * one(*cut)
    return loudness


def gaussian(stream_key, extent, deviation, reach, cuts=(), dtype=jnp.bfloat16):
    drawn = jax.random.normal(stream_key, extent, jnp.float32) * deviation
    if len(cuts) > 0:
        drawn = steps_of(stream_key, extent, cuts, -0.22, 0.18) * drawn
    return jnp.clip(drawn, min=-reach, max=reach).astype(dtype)


def setup_inputs(seed: int = 0) -> dict:
    key_list = jax.random.split(jax.random.key(seed), 8)
    return {
        "hidden_rows": gaussian(key_list[0], (BATCH, SEQ, D), 1.0, 6.0, ((0, 16), (1, 8))),
        "inner_rows": gaussian(key_list[1], (BATCH, SEQ, H * P_SIZE), 1.0, 6.0, ((0, 16), (1, 8))),
        "weight_proj": gaussian(key_list[2], (D, COLS), (4 * D) ** -0.5, 0.03125, ((0, 16),)),
        "decay_log": draw_decay_log(jax.random.fold_in(key_list[7], 71), 0),
        "step_bias": jnp.clip(jax.random.uniform(key_list[4], (H,), jnp.float32, -0.5, 0.5), -0.5, 0.5),
        "skip_gain": jnp.clip(jax.random.uniform(key_list[5], (H,), jnp.float32, 0.5, 1.5), 0.5, 1.5),
        "grad_output": gaussian(key_list[6], (BATCH, SEQ, H * P_SIZE), 1.0, 6.0, ((0, 16), (1, 8))),
    }


highest = lax.Precision.HIGHEST

def split_proj(projected, step_bias, decay_log):
    key_rows = projected[:, :N]
    query_rows = projected[:, N:2 * N] * N ** (-0.5)
    step_sizes = jax.nn.softplus(projected[:, 2 * N:] + step_bias[None, :])
    log_decay = -jnp.exp(decay_log)[None, :] * step_sizes
    return (key_rows, query_rows, step_sizes, log_decay)

def block_step(skip_gain, carry_state, block):
    key_rows, query_rows, step_sizes, log_decay, value_rows = block
    block_len = key_rows.shape[0]
    values = value_rows.astype(jnp.float32).reshape(block_len, carry_state.shape[0], carry_state.shape[1])
    running = jnp.cumsum(log_decay.T, axis=1)
    causal = jnp.arange(block_len)[:, None] >= jnp.arange(block_len)[None, :]
    log_gaps = running[:, :, None] - running[:, None, :]
    decays = jnp.where(causal[None], jnp.exp(jnp.where(causal[None], log_gaps, 0.0)), 0.0)
    scores = jnp.dot(query_rows, key_rows.T, precision=highest)
    mixing = decays * scores[None] * step_sizes.T[:, None, :]
    within = jnp.einsum('hts,shp->thp', mixing, values, precision=highest)
    carried = jnp.einsum('tn,hpn->thp', query_rows, carry_state, precision=highest) * jnp.exp(running).T[:, :, None]
    tail_weight = jnp.exp(running[:, -1:] - running) * step_sizes.T
    new_state = jnp.exp(running[:, -1])[:, None, None] * carry_state + jnp.einsum('hs,shp,sn->hpn', tail_weight, values, key_rows, precision=highest)
    output = within + carried + skip_gain[None, :, None] * values
    return (new_state, output.reshape(block_len, -1))

def to_blocks(array, num_blocks):
    return array.reshape((num_blocks, -1) + array.shape[1:])

def run_blocks(projected, value_rows, state_start, decay_log, step_bias, skip_gain):
    key_rows, query_rows, step_sizes, log_decay = split_proj(projected, step_bias, decay_log)
    num_blocks = projected.shape[0] // BLOCK
    blocks = tuple((to_blocks(item, num_blocks) for item in (key_rows, query_rows, step_sizes, log_decay, value_rows)))
    final_state, outputs = lax.scan(partial(block_step, skip_gain), state_start, blocks)
    return (outputs.reshape(projected.shape[0], -1), final_state)

def reference(hidden_rows, inner_rows, weight_proj, decay_log, step_bias, skip_gain, grad_output):

    def one_sequence(grad_total, items):
        token_rows, value_rows, cotangent = items
        projected = jnp.dot(token_rows, weight_proj, preferred_element_type=jnp.float32)
        state_start = jnp.zeros((decay_log.shape[0], P_SIZE, N), jnp.float32)

        def forward(proj_in, values_in):
            return run_blocks(proj_in, values_in, state_start, decay_log, step_bias, skip_gain)[0]
        output, pullback = jax.vjp(forward, projected, value_rows)
        grad_proj, grad_values = pullback(cotangent.astype(jnp.float32))
        grad_low = grad_proj.astype(jnp.bfloat16)
        grad_tokens = jnp.dot(grad_low, weight_proj.T, preferred_element_type=jnp.float32).astype(jnp.bfloat16)
        grad_total = grad_total + jnp.dot(token_rows.T, grad_low, preferred_element_type=jnp.float32)
        return (grad_total, (output.astype(jnp.bfloat16), grad_values.astype(jnp.bfloat16), grad_tokens))
    zero_grad = jnp.zeros(weight_proj.shape, jnp.float32)
    grad_weight, outputs = lax.scan(one_sequence, zero_grad, (hidden_rows, inner_rows, grad_output))
    ssd_output, grad_inner, grad_hidden = outputs
    return (ssd_output, grad_inner, grad_hidden, grad_weight)
```

```python
from functools import partial

import jax
import jax.numpy as jnp
from jax import lax
from jax.experimental import pallas as pl
from jax.experimental.pallas import tpu as pltpu
from jax.sharding import PartitionSpec as P

PS = 128
NS = 128
CHUNK = 2
LAG = 2
MESH = pl.DeviceIdType.MESH
highest = lax.Precision.HIGHEST
f32 = jnp.float32
bf16 = jnp.bfloat16
NN = (((1,), (0,)), ((), ()))
NT = (((1,), (1,)), ((), ()))
TN = (((0,), (0,)), ((), ()))


def dot(a, b, dims=NN):
    return lax.dot_general(a, b, dims, preferred_element_type=f32)


def dot_high(a, b, dims=NN):
    return lax.dot_general(a, b, dims, preferred_element_type=f32, precision=highest)


def split(a):
    high = a.astype(bf16)
    return high, (a - high.astype(f32)).astype(bf16)


def scan_kernel(
    pieces, heads, gain_ref, proj_ref, head_ref, x_ref, dy_ref, y_ref, dx_ref, grad_ref,
    run, run_t, step_t, step_c, key_t, query_t, key_hl, query_hl, scores,
    acc_diff, acc_cross, acc_const, dq, dk, dscores,
    state_in, state_out, grad_in, grad_out, sf, rf, sb, rb,
):
    k = lax.axis_index("ctx")
    last = pieces - 1
    tokens = proj_ref.shape[0]
    half = tokens // 2
    chunks = heads // CHUNK
    right = lax.rem(k + 1, pieces)
    left = lax.rem(k + pieces - 1, pieces)

    barrier = pltpu.get_barrier_semaphore()
    for neighbour in (left, right):
        pl.semaphore_signal(barrier, inc=1, device_id={"ctx": neighbour}, device_id_type=MESH)

    rows = lax.broadcasted_iota(jnp.int32, (tokens, tokens), 0)
    cols = lax.broadcasted_iota(jnp.int32, (tokens, tokens), 1)
    key = proj_ref[:, :NS]
    query = proj_ref[:, NS : 2 * NS] * NS ** (-0.5)
    bias = head_ref[0:1, :]
    rate = jnp.exp(head_ref[1:2, :])
    pre = proj_ref[:, 2 * NS :] + bias
    steps = jnp.maximum(pre, 0.0) + jnp.log1p(jnp.exp(-jnp.abs(pre)))
    running = dot_high((rows >= cols).astype(f32), -rate * steps)
    run[...] = running
    run_t[...] = running.T
    step_c[...] = steps
    step_t[...] = steps.T
    key_t[...] = key.T
    query_t[...] = query.T
    high, low = split(key)
    key_hl[:, :NS] = high
    key_hl[:, NS:] = low
    high, low = split(query)
    query_hl[:, :NS] = high
    query_hl[:, NS:] = low
    scores[...] = dot_high(query, key, NT)
    dq[...] = jnp.zeros_like(dq)
    dk[...] = jnp.zeros_like(dk)
    dscores[...] = jnp.zeros_like(dscores)
    acc_diff[...] = jnp.zeros_like(acc_diff)
    acc_cross[...] = jnp.zeros_like(acc_cross)
    acc_const[...] = jnp.zeros_like(acc_const)

    @pl.when(k == 0)
    def _():
        state_in[...] = jnp.zeros_like(state_in)

    @pl.when(k == last)
    def _():
        grad_in[...] = jnp.zeros_like(grad_in)

    pl.semaphore_wait(barrier, 2)

    def copy_fwd(j):
        part = pl.ds(j * CHUNK, CHUNK)
        return pltpu.make_async_remote_copy(
            src_ref=state_out.at[part], dst_ref=state_in.at[part],
            send_sem=sf.at[j], recv_sem=rf.at[j],
            device_id={"ctx": right}, device_id_type=MESH,
        )

    def copy_bwd(j):
        part = pl.ds(j * CHUNK, CHUNK)
        return pltpu.make_async_remote_copy(
            src_ref=grad_out.at[part], dst_ref=grad_in.at[part],
            send_sem=sb.at[j], recv_sem=rb.at[j],
            device_id={"ctx": left}, device_id_type=MESH,
        )

    def columns(h):
        return pl.ds(pl.multiple_of(h * PS, PS), PS)

    def forward(j):
        local = []
        for u in range(CHUNK):
            h = j * CHUNK + u
            r_row = run_t[pl.ds(h, 1), :]
            r_end = r_row[:, tokens - 1 : tokens]
            weight = jnp.exp(r_end - r_row) * step_t[pl.ds(h, 1), :]
            high, low = split(key_t[...] * weight)
            x = x_ref[:, columns(h)]
            local.append((h, jnp.exp(r_end), dot(high, x) + dot(low, x)))

        @pl.when(k > 0)
        def _():
            copy_fwd(j).wait_recv()

        @pl.when(k < last)
        def _():
            for h, decay, state in local:
                state_out[h] = (decay * state_in[h].astype(f32) + state).astype(bf16)
            copy_fwd(j).start()

    def backward(j):
        local = []
        for u in range(CHUNK):
            h = j * CHUNK + u
            r_row = run_t[pl.ds(h, 1), :]
            r_end = r_row[:, tokens - 1 : tokens]
            high, low = split(query_t[...] * jnp.exp(r_row))
            dy = dy_ref[:, columns(h)]
            local.append((h, jnp.exp(r_end), dot(high, dy) + dot(low, dy)))

        @pl.when(k < last)
        def _():
            copy_bwd(j).wait_recv()

        @pl.when(k > 0)
        def _():
            for h, decay, state in local:
                grad_out[h] = (decay * grad_in[h].astype(f32) + state).astype(bf16)
            copy_bwd(j).start()

    def compute(h):
        lane = lax.broadcasted_iota(jnp.int32, (tokens, NS), 1)
        mine = lane == h
        r_col = jnp.sum(jnp.where(mine, run[...], 0.0), axis=1, keepdims=True)
        s_col = jnp.sum(jnp.where(mine, step_c[...], 0.0), axis=1, keepdims=True)
        r_row = run_t[pl.ds(h, 1), :]
        s_row = step_t[pl.ds(h, 1), :]
        r_end = r_row[:, tokens - 1 : tokens]
        x = x_ref[:, columns(h)]
        dy = dy_ref[:, columns(h)]
        gain = gain_ref[h]

        def decays(begin, width):
            t = lax.broadcasted_iota(jnp.int32, (half, width), 0) + begin
            s = lax.broadcasted_iota(jnp.int32, (half, width), 1)
            gaps = r_col[begin : begin + half] - r_row[:, :width]
            return jnp.exp(jnp.where(t >= s, gaps, -1e30)) * s_row[:, :width]

        top = decays(0, half)
        bottom = decays(half, tokens)
        mix_top = (top * scores[:half, :half]).astype(bf16)
        mix_bottom = (bottom * scores[half:, :]).astype(bf16)
        dscores[:half, :half] += top * dot(dy[:half], x[:half], NT)
        dscores[half:, :] += bottom * dot(dy[half:], x, NT)
        y = jnp.concatenate([dot(mix_top, x[:half]), dot(mix_bottom, x)], axis=0)
        dx = dot(mix_bottom, dy[half:], TN)
        dx = jnp.concatenate([dx[:half] + dot(mix_top, dy[:half], TN), dx[half:]], axis=0)

        state = state_in[h]
        grad = grad_in[h]
        from_start = jnp.exp(r_col)
        to_end = jnp.exp(r_end - r_col) * s_col
        y += from_start * dot(query_hl[...], jnp.concatenate([state, state], axis=0))
        carried = to_end * dot(key_hl[...], jnp.concatenate([grad, grad], axis=0))
        dx += carried
        dq[...] += from_start * dot(dy, state, NT)
        dk[...] += to_end * dot(x, grad, NT)
        xf = x.astype(f32)
        dyf = dy.astype(f32)
        y_ref[:, columns(h)] = (y + gain * xf).astype(bf16)
        dx_ref[:, columns(h)] = (dx + gain * dyf).astype(bf16)
        cross = xf * dx
        acc_cross[...] = jnp.where(mine, jnp.sum(cross, axis=1, keepdims=True), acc_cross[...])
        acc_diff[...] = jnp.where(
            mine, jnp.sum(dyf * y - cross, axis=1, keepdims=True), acc_diff[...]
        )
        inner = jnp.sum(grad.astype(f32) * state.astype(f32), axis=0, keepdims=True)
        inner = jnp.sum(inner, axis=1, keepdims=True)
        outer = jnp.sum(jnp.sum(xf * carried, axis=0, keepdims=True), axis=1, keepdims=True)
        const = jnp.exp(r_end) * inner + outer
        acc_const[...] = jnp.where(mine[:8], const, acc_const[...])

    start_f = LAG * k
    start_b = LAG * (last - k)
    start_c = jnp.maximum(start_f, start_b)

    def iteration(i, carry):
        jf = i - start_f
        jb = i - start_b
        jc = i - start_c

        @pl.when((jf >= 0) & (jf < chunks))
        def _():
            forward(jf)

        @pl.when((jb >= 0) & (jb < chunks))
        def _():
            backward(jb)

        @pl.when((jc >= 0) & (jc < chunks))
        def _():
            for u in range(CHUNK):
                compute(jc * CHUNK + u)

        return carry

    lax.fori_loop(0, chunks + LAG * last, iteration, 0)

    @pl.when(k < last)
    def _():
        def wait(j, carry):
            copy_fwd(j).wait_send()
            return carry

        lax.fori_loop(0, chunks, wait, 0)

    @pl.when(k > 0)
    def _():
        def wait(j, carry):
            copy_bwd(j).wait_send()
            return carry

        lax.fori_loop(0, chunks, wait, 0)

    key = proj_ref[:, :NS]
    query = proj_ref[:, NS : 2 * NS] * NS ** (-0.5)
    pre = proj_ref[:, 2 * NS :] + head_ref[0:1, :]
    d_log = dot_high((cols >= rows).astype(f32), acc_diff[...]) + acc_const[0:1, :]
    slope = 1.0 / (1.0 + jnp.exp(-pre))
    ratio = jnp.where(pre < -20.0, 1.0, slope / step_c[...])
    dk_all = dk[...] + dot_high(dscores[...].T, query)
    dq_all = dq[...] + dot_high(dscores[...], key)
    grad_ref[:, :NS] = dk_all.astype(bf16)
    grad_ref[:, NS : 2 * NS] = (dq_all * NS ** (-0.5)).astype(bf16)
    rate = jnp.exp(head_ref[1:2, :])
    grad_ref[:, 2 * NS :] = (acc_cross[...] * ratio - rate * d_log * slope).astype(bf16)


def scan_pass(pieces, gain, proj, head, x, dy):
    tokens, width = x.shape
    heads = width // PS
    chunks = heads // CHUNK
    vm = pl.BlockSpec(memory_space=pltpu.VMEM)
    big = (heads, NS, PS)
    return pl.pallas_call(
        partial(scan_kernel, pieces, heads),
        out_shape=(
            jax.ShapeDtypeStruct(x.shape, bf16),
            jax.ShapeDtypeStruct(x.shape, bf16),
            jax.ShapeDtypeStruct((tokens, 3 * NS), bf16),
        ),
        in_specs=[pl.BlockSpec(memory_space=pltpu.SMEM), vm, vm, vm, vm],
        out_specs=(vm, vm, vm),
        scratch_shapes=[
            pltpu.VMEM((tokens, NS), f32),
            pltpu.VMEM((NS, tokens), f32),
            pltpu.VMEM((NS, tokens), f32),
            pltpu.VMEM((tokens, NS), f32),
            pltpu.VMEM((NS, tokens), f32),
            pltpu.VMEM((NS, tokens), f32),
            pltpu.VMEM((tokens, 2 * NS), bf16),
            pltpu.VMEM((tokens, 2 * NS), bf16),
            pltpu.VMEM((tokens, tokens), f32),
            pltpu.VMEM((tokens, NS), f32),
            pltpu.VMEM((tokens, NS), f32),
            pltpu.VMEM((8, NS), f32),
            pltpu.VMEM((tokens, NS), f32),
            pltpu.VMEM((tokens, NS), f32),
            pltpu.VMEM((tokens, tokens), f32),
            pltpu.VMEM(big, bf16),
            pltpu.VMEM(big, bf16),
            pltpu.VMEM(big, bf16),
            pltpu.VMEM(big, bf16),
            pltpu.SemaphoreType.DMA((chunks,)),
            pltpu.SemaphoreType.DMA((chunks,)),
            pltpu.SemaphoreType.DMA((chunks,)),
            pltpu.SemaphoreType.DMA((chunks,)),
        ],
        compiler_params=pltpu.CompilerParams(
            collective_id=0, has_side_effects=True, vmem_limit_bytes=48 * 2**20
        ),
    )(gain, proj, head, x, dy)


def shards(pieces, hidden_rows, inner_rows, weight_proj, decay_log, step_bias, skip_gain, grad_output):
    token_rows = hidden_rows.reshape(-1, hidden_rows.shape[-1])
    value_rows = inner_rows.reshape(-1, inner_rows.shape[-1])
    cotangent = grad_output.reshape(value_rows.shape)
    cols = weight_proj.shape[1]
    heads = decay_log.shape[0]
    whole = lax.all_gather(weight_proj, "dp", axis=0, tiled=True)
    padded = jnp.pad(whole, ((0, 0), (0, 3 * NS - cols)))
    projected = jnp.dot(token_rows, padded, preferred_element_type=f32)
    head = jnp.pad(jnp.stack([step_bias, decay_log]), ((0, 6), (0, NS - heads)))
    output, grad_values, grad_low = scan_pass(
        pieces, skip_gain, projected, head, value_rows, cotangent
    )
    ssd_output = output.reshape(inner_rows.shape)
    grad_inner = grad_values.reshape(inner_rows.shape)
    grad_low = grad_low[:, :cols]
    grad_tokens = dot(grad_low, whole, NT)
    grad_hidden = grad_tokens.astype(bf16).reshape(hidden_rows.shape)
    grad_shard = lax.psum_scatter(
        dot(token_rows, grad_low, TN), "dp", scatter_dimension=0, tiled=True
    )
    grad_weight = lax.psum(grad_shard, "ctx")
    return (ssd_output, grad_inner, grad_hidden, grad_weight)


def solution(mesh):
    rows = P("dp", "ctx", None)
    return jax.shard_map(
        partial(shards, mesh.shape["ctx"]),
        mesh=mesh,
        in_specs=(rows, rows, P("dp", None), P(), P(), P(), rows),
        out_specs=(rows, rows, rows, P("dp", None)),
        check_vma=False,
    )
```

```python
from functools import partial

import jax
import jax.numpy as jnp
from jax import lax
from jax.experimental import pallas as pl
from jax.experimental.pallas import tpu as pltpu
from jax.sharding import PartitionSpec as P

PS = 128
NS = 128
CHUNK = 2
LAG = 2
MESH = pl.DeviceIdType.MESH
highest = lax.Precision.HIGHEST
f32 = jnp.float32
bf16 = jnp.bfloat16
NN = (((1,), (0,)), ((), ()))
NT = (((1,), (1,)), ((), ()))
TN = (((0,), (0,)), ((), ()))


def dot(a, b, dims=NN):
    return lax.dot_general(a, b, dims, preferred_element_type=f32)


def dot_high(a, b, dims=NN):
    return lax.dot_general(a, b, dims, preferred_element_type=f32, precision=highest)


def split(a):
    high = a.astype(bf16)
    return high, (a - high.astype(f32)).astype(bf16)


def scan_kernel(
    pieces, heads, gain_ref, proj_ref, head_ref, x_ref, dy_ref, y_ref, dx_ref, grad_ref,
    run, run_t, step_t, step_c, key_t, query_t, key_hl, query_hl, scores,
    acc_diff, acc_cross, acc_const, dq, dk, dscores,
    state_in, state_out, grad_in, grad_out, sf, rf, sb, rb,
):
    k = lax.axis_index("ctx")
    last = pieces - 1
    tokens = proj_ref.shape[0]
    half = tokens // 2
    chunks = heads // CHUNK
    right = lax.rem(k + 1, pieces)
    left = lax.rem(k + pieces - 1, pieces)

    barrier = pltpu.get_barrier_semaphore()
    for neighbour in (left, right):
        pl.semaphore_signal(barrier, inc=1, device_id={"ctx": neighbour}, device_id_type=MESH)

    rows = lax.broadcasted_iota(jnp.int32, (tokens, tokens), 0)
    cols = lax.broadcasted_iota(jnp.int32, (tokens, tokens), 1)
    key = proj_ref[:, :NS]
    query = proj_ref[:, NS : 2 * NS] * NS ** (-0.5)
    bias = head_ref[0:1, :]
    rate = jnp.exp(head_ref[1:2, :])
    pre = proj_ref[:, 2 * NS :] + bias
    steps = jnp.maximum(pre, 0.0) + jnp.log1p(jnp.exp(-jnp.abs(pre)))
    running = dot_high((rows >= cols).astype(f32), -rate * steps)
    run[...] = running
    run_t[...] = running.T
    step_c[...] = steps
    step_t[...] = steps.T
    key_t[...] = key.T
    query_t[...] = query.T
    high, low = split(key)
    key_hl[:, :NS] = high
    key_hl[:, NS:] = low
    high, low = split(query)
    query_hl[:, :NS] = high
    query_hl[:, NS:] = low
    scores[...] = dot_high(query, key, NT)
    dq[...] = jnp.zeros_like(dq)
    dk[...] = jnp.zeros_like(dk)
    dscores[...] = jnp.zeros_like(dscores)
    acc_diff[...] = jnp.zeros_like(acc_diff)
    acc_cross[...] = jnp.zeros_like(acc_cross)
    acc_const[...] = jnp.zeros_like(acc_const)

    @pl.when(k == 0)
    def _():
        state_in[...] = jnp.zeros_like(state_in)

    @pl.when(k == last)
    def _():
        grad_in[...] = jnp.zeros_like(grad_in)

    pl.semaphore_wait(barrier, 2)

    def copy_fwd(j):
        part = pl.ds(j * CHUNK, CHUNK)
        return pltpu.make_async_remote_copy(
            src_ref=state_out.at[part], dst_ref=state_in.at[part],
            send_sem=sf.at[j], recv_sem=rf.at[j],
            device_id={"ctx": right}, device_id_type=MESH,
        )

    def copy_bwd(j):
        part = pl.ds(j * CHUNK, CHUNK)
        return pltpu.make_async_remote_copy(
            src_ref=grad_out.at[part], dst_ref=grad_in.at[part],
            send_sem=sb.at[j], recv_sem=rb.at[j],
            device_id={"ctx": left}, device_id_type=MESH,
        )

    def columns(h):
        return pl.ds(pl.multiple_of(h * PS, PS), PS)

    def forward(j):
        local = []
        for u in range(CHUNK):
            h = j * CHUNK + u
            r_row = run_t[pl.ds(h, 1), :]
            r_end = r_row[:, tokens - 1 : tokens]
            weight = jnp.exp(r_end - r_row) * step_t[pl.ds(h, 1), :]
            high, low = split(key_t[...] * weight)
            x = x_ref[:, columns(h)]
            local.append((h, jnp.exp(r_end), dot(high, x) + dot(low, x)))

        @pl.when(k > 0)
        def _():
            copy_fwd(j).wait_recv()

        @pl.when(k < last)
        def _():
            for h, decay, state in local:
                state_out[h] = (decay * state_in[h].astype(f32) + state).astype(bf16)
            copy_fwd(j).start()

    def backward(j):
        local = []
        for u in range(CHUNK):
            h = j * CHUNK + u
            r_row = run_t[pl.ds(h, 1), :]
            r_end = r_row[:, tokens - 1 : tokens]
            high, low = split(query_t[...] * jnp.exp(r_row))
            dy = dy_ref[:, columns(h)]
            local.append((h, jnp.exp(r_end), dot(high, dy) + dot(low, dy)))

        @pl.when(k < last)
        def _():
            copy_bwd(j).wait_recv()

        @pl.when(k > 0)
        def _():
            for h, decay, state in local:
                grad_out[h] = (decay * grad_in[h].astype(f32) + state).astype(bf16)
            copy_bwd(j).start()

    def compute(h):
        lane = lax.broadcasted_iota(jnp.int32, (tokens, NS), 1)
        mine = lane == h
        r_col = jnp.sum(jnp.where(mine, run[...], 0.0), axis=1, keepdims=True)
        s_col = jnp.sum(jnp.where(mine, step_c[...], 0.0), axis=1, keepdims=True)
        r_row = run_t[pl.ds(h, 1), :]
        s_row = step_t[pl.ds(h, 1), :]
        r_end = r_row[:, tokens - 1 : tokens]
        x = x_ref[:, columns(h)]
        dy = dy_ref[:, columns(h)]
        gain = gain_ref[h]

        def decays(begin, width):
            t = lax.broadcasted_iota(jnp.int32, (half, width), 0) + begin
            s = lax.broadcasted_iota(jnp.int32, (half, width), 1)
            gaps = r_col[begin : begin + half] - r_row[:, :width]
            return jnp.exp(jnp.where(t >= s, gaps, -1e30)) * s_row[:, :width]

        top = decays(0, half)
        bottom = decays(half, tokens)
        mix_top = (top * scores[:half, :half]).astype(bf16)
        mix_bottom = (bottom * scores[half:, :]).astype(bf16)
        dscores[:half, :half] += top * dot(dy[:half], x[:half], NT)
        dscores[half:, :] += bottom * dot(dy[half:], x, NT)
        y = jnp.concatenate([dot(mix_top, x[:half]), dot(mix_bottom, x)], axis=0)
        dx = dot(mix_bottom, dy[half:], TN)
        dx = jnp.concatenate([dx[:half] + dot(mix_top, dy[:half], TN), dx[half:]], axis=0)

        state = state_in[h]
        grad = grad_in[h]
        from_start = jnp.exp(r_col)
        to_end = jnp.exp(r_end - r_col) * s_col
        y += from_start * dot(query_hl[...], jnp.concatenate([state, state], axis=0))
        carried = to_end * dot(key_hl[...], jnp.concatenate([grad, grad], axis=0))
        dx += carried
        dq[...] += from_start * dot(dy, state, NT)
        dk[...] += to_end * dot(x, grad, NT)
        xf = x.astype(f32)
        dyf = dy.astype(f32)
        y_ref[:, columns(h)] = (y + gain * xf).astype(bf16)
        dx_ref[:, columns(h)] = (dx + gain * dyf).astype(bf16)
        cross = xf * dx
        acc_cross[...] = jnp.where(mine, jnp.sum(cross, axis=1, keepdims=True), acc_cross[...])
        acc_diff[...] = jnp.where(
            mine, jnp.sum(dyf * y - cross, axis=1, keepdims=True), acc_diff[...]
        )
        inner = jnp.sum(grad.astype(f32) * state.astype(f32), axis=0, keepdims=True)
        inner = jnp.sum(inner, axis=1, keepdims=True)
        outer = jnp.sum(jnp.sum(xf * carried, axis=0, keepdims=True), axis=1, keepdims=True)
        const = jnp.exp(r_end) * inner + outer
        acc_const[...] = jnp.where(mine[:8], const, acc_const[...])

    start_f = LAG * k
    start_b = LAG * (last - k)
    start_c = jnp.maximum(start_f, start_b)

    def iteration(i, carry):
        jf = i - start_f
        jb = i - start_b
        jc = i - start_c

        @pl.when((jf >= 0) & (jf < chunks))
        def _():
            forward(jf)

        @pl.when((jb >= 0) & (jb < chunks))
        def _():
            backward(jb)

        @pl.when((jc >= 0) & (jc < chunks))
        def _():
            for u in range(CHUNK):
                compute(jc * CHUNK + u)

        return carry

    lax.fori_loop(0, chunks + LAG * last, iteration, 0)

    @pl.when(k < last)
    def _():
        def wait(j, carry):
            copy_fwd(j).wait_send()
            return carry

        lax.fori_loop(0, chunks, wait, 0)

    @pl.when(k > 0)
    def _():
        def wait(j, carry):
            copy_bwd(j).wait_send()
            return carry

        lax.fori_loop(0, chunks, wait, 0)

    key = proj_ref[:, :NS]
    query = proj_ref[:, NS : 2 * NS] * NS ** (-0.5)
    pre = proj_ref[:, 2 * NS :] + head_ref[0:1, :]
    d_log = dot_high((cols >= rows).astype(f32), acc_diff[...]) + acc_const[0:1, :]
    slope = 1.0 / (1.0 + jnp.exp(-pre))
    ratio = jnp.where(pre < -20.0, 1.0, slope / step_c[...])
    dk_all = dk[...] + dot_high(dscores[...].T, query)
    dq_all = dq[...] + dot_high(dscores[...], key)
    grad_ref[:, :NS] = dk_all.astype(bf16)
    grad_ref[:, NS : 2 * NS] = (dq_all * NS ** (-0.5)).astype(bf16)
    rate = jnp.exp(head_ref[1:2, :])
    grad_ref[:, 2 * NS :] = (acc_cross[...] * ratio - rate * d_log * slope).astype(bf16)


def scan_pass(pieces, gain, proj, head, x, dy):
    tokens, width = x.shape
    heads = width // PS
    chunks = heads // CHUNK
    vm = pl.BlockSpec(memory_space=pltpu.VMEM)
    big = (heads, NS, PS)
    return pl.pallas_call(
        partial(scan_kernel, pieces, heads),
        out_shape=(
            jax.ShapeDtypeStruct(x.shape, bf16),
            jax.ShapeDtypeStruct(x.shape, bf16),
            jax.ShapeDtypeStruct((tokens, 3 * NS), bf16),
        ),
        in_specs=[pl.BlockSpec(memory_space=pltpu.SMEM), vm, vm, vm, vm],
        out_specs=(vm, vm, vm),
        scratch_shapes=[
            pltpu.VMEM((tokens, NS), f32),
            pltpu.VMEM((NS, tokens), f32),
            pltpu.VMEM((NS, tokens), f32),
            pltpu.VMEM((tokens, NS), f32),
            pltpu.VMEM((NS, tokens), f32),
            pltpu.VMEM((NS, tokens), f32),
            pltpu.VMEM((tokens, 2 * NS), bf16),
            pltpu.VMEM((tokens, 2 * NS), bf16),
            pltpu.VMEM((tokens, tokens), f32),
            pltpu.VMEM((tokens, NS), f32),
            pltpu.VMEM((tokens, NS), f32),
            pltpu.VMEM((8, NS), f32),
            pltpu.VMEM((tokens, NS), f32),
            pltpu.VMEM((tokens, NS), f32),
            pltpu.VMEM((tokens, tokens), f32),
            pltpu.VMEM(big, bf16),
            pltpu.VMEM(big, bf16),
            pltpu.VMEM(big, bf16),
            pltpu.VMEM(big, bf16),
            pltpu.SemaphoreType.DMA((chunks,)),
            pltpu.SemaphoreType.DMA((chunks,)),
            pltpu.SemaphoreType.DMA((chunks,)),
            pltpu.SemaphoreType.DMA((chunks,)),
        ],
        compiler_params=pltpu.CompilerParams(
            collective_id=0, has_side_effects=True, vmem_limit_bytes=48 * 2**20
        ),
    )(gain, proj, head, x, dy)


def weight_grad_kernel(
    h_ref, g_ref, out_ref, g_t, sib_send, sib_recv, own, low,
    slot_a0, slot_a1, slot_a2, sum_a0, sum_a1, sum_a2, low_a0, low_a1, low_a2,
    slot_b0, slot_b1, slot_b2, sum_b0, sum_b1, sum_b2,
    slot_c0, slot_c1, slot_c2, final, gathered,
    sib_s, sib_r, st_s, st_r, ga_s, ga_r,
):
    dp = lax.axis_index("dp")
    ctx = lax.axis_index("ctx")
    x_lo, z, core = dp // 8, lax.rem(dp // 2, 4), lax.rem(dp, 2)
    x_hi, y = ctx // 4, lax.rem(ctx, 4)
    x = x_hi * 2 + x_lo
    rows = out_ref.shape[0]
    depth = out_ref.shape[1]
    half = rows // 2
    lanes = depth // 4

    def device(x_lo=x_lo, z=z, core=core, x_hi=x_hi, y=y):
        return {"dp": x_lo * 8 + z * 2 + core, "ctx": x_hi * 4 + y}

    def ring(axis, d):
        if axis == "z":
            return device(z=lax.rem(z + d, 4)), (lax.rem(z + d, 4),)
        if axis == "y":
            return device(y=lax.rem(y + d, 4)), (lax.rem(y + d, 4),)
        to = lax.rem(x + d, 4)
        return device(x_lo=lax.rem(to, 2), x_hi=to // 2), (lax.rem(to, 2), to // 2)

    barrier = pltpu.get_barrier_semaphore()
    others = [(a, b) for a in range(2) for b in range(4) if a + b]
    peers = [device(core=1 - core)]
    peers += [ring("z", d)[0] for d in (1, 2, 3)]
    peers += [ring("x", d)[0] for d in (1, 3)]
    peers += [device(x_hi=lax.rem(x_hi + a, 2), y=lax.rem(y + b, 4)) for a, b in others]
    for peer in peers:
        pl.semaphore_signal(barrier, inc=1, device_id=peer, device_id_type=MESH)
    g_t[...] = g_ref[...].astype(f32).T.astype(bf16)
    pl.semaphore_wait(barrier, len(peers))

    def product(s, side):
        at = (s // 4) * 8 + lax.rem(s, 4) * 2 + side
        block = h_ref[:, pl.ds(pl.multiple_of(at * depth, depth), depth)]
        return dot(g_t[:rows, :], block)

    def sib(s):
        return pltpu.make_async_remote_copy(
            src_ref=sib_send.at[s], dst_ref=sib_recv.at[s],
            send_sem=sib_s.at[s], recv_sem=sib_r.at[s],
            device_id=device(core=1 - core), device_id_type=MESH,
        )

    def for_sibling(s, carry):
        p = product(s, 1 - core).astype(bf16)
        for b in range(4):
            for a in range(2):
                sib_send[s, b, a] = p[a * half : (a + 1) * half, b * lanes : (b + 1) * lanes]
        sib(s).start()
        return carry

    lax.fori_loop(0, 8, for_sibling, 0)

    def for_self(s, carry):
        p = product(s, core)
        sib(s).wait_recv()
        for b in range(4):
            for a in range(2):
                total = p[a * half : (a + 1) * half, b * lanes : (b + 1) * lanes]
                total += sib_recv[s, b, a].astype(f32)
                own[s // 4, lax.rem(s, 4), b, a] = total
                low[s // 4, lax.rem(s, 4), b, a] = total.astype(bf16)
        return carry

    lax.fori_loop(0, 8, for_self, 0)

    orders = (("z", "y", "x"), ("y", "x", "z"), ("x", "z", "y"))
    slots = ((slot_a0, slot_b0, slot_c0), (slot_a1, slot_b1, slot_c1), (slot_a2, slot_b2, slot_c2))

    def pick(left, axis, place):
        at = []
        for name in left:
            if name == axis:
                at.append(place[0])
            elif axis == "x" and name == "x_lo":
                at.append(place[0])
            elif axis == "x" and name == "x_hi":
                at.append(place[1])
            else:
                at.append(slice(None))
        return tuple(at)

    def rest(left, axis):
        gone = ("x_lo", "x_hi") if axis == "x" else (axis,)
        return tuple(name for name in left if name not in gone)

    everything = ("x_lo", "z", "y", "x_hi")

    def exchange(color, stage, source, left):
        axis = orders[color][stage]
        off, size = bands(half)[color]
        window = (pl.ds(off, size),) if stage == 0 else ()
        copies = []
        for d in (1, 2, 3):
            peer, place = ring(axis, d)
            n = color * 9 + stage * 3 + d - 1
            copies.append(
                pltpu.make_async_remote_copy(
                    src_ref=source.at[pick(left, axis, place) + window],
                    dst_ref=slots[color][stage].at[d - 1],
                    send_sem=st_s.at[n], recv_sem=st_r.at[n],
                    device_id=peer, device_id_type=MESH,
                )
            )
            copies[-1].start()
        return copies

    def my_place(axis):
        return {"z": (z,), "y": (y,), "x": (x_lo, x_hi)}[axis]

    pending = []
    left = [everything] * 3
    current = []
    for color in range(3):
        current.append(exchange(color, 0, low, everything))
    sums = (sum_a0, sum_a1, sum_a2)
    lows = (low_a0, low_a1, low_a2)
    for color in range(3):
        axis = orders[color][0]
        off, size = bands(half)[color]
        for copy in current[color]:
            copy.wait_recv()
        pending += current[color]
        total = own[pick(everything, axis, my_place(axis)) + (pl.ds(off, size),)]
        for d in range(3):
            total += slots[color][0][d].astype(f32)
        sums[color][...] = total
        lows[color][...] = total.astype(bf16)
        left[color] = rest(everything, axis)
        current[color] = exchange(color, 1, lows[color], left[color])
    finals = (sum_b0, sum_b1, sum_b2)
    for color in range(3):
        axis = orders[color][1]
        for copy in current[color]:
            copy.wait_recv()
        pending += current[color]
        total = sums[color][pick(left[color], axis, my_place(axis))]
        for d in range(3):
            total += slots[color][1][d].astype(f32)
        finals[color][...] = total
        left[color] = rest(left[color], axis)
        current[color] = exchange(color, 2, finals[color], left[color])
    gathers = []
    for color in range(3):
        axis = orders[color][2]
        off, size = bands(half)[color]
        for copy in current[color]:
            copy.wait_recv()
        pending += current[color]
        total = finals[color][pick(left[color], axis, my_place(axis))]
        for d in range(3):
            total += slots[color][2][d]
        final[pl.ds(off, size)] = total
        for m, (a, b) in enumerate(others):
            gathers.append(
                pltpu.make_async_remote_copy(
                    src_ref=final.at[pl.ds(off, size)],
                    dst_ref=gathered.at[x_hi, y, pl.ds(off, size)],
                    send_sem=ga_s.at[color * 7 + m], recv_sem=ga_r.at[color * 7 + m],
                    device_id=device(x_hi=lax.rem(x_hi + a, 2), y=lax.rem(y + b, 4)),
                    device_id_type=MESH,
                )
            )
            gathers[-1].start()
    for copy in gathers:
        copy.wait_recv()
    for a in range(2):
        for b in range(4):
            mine = (x_hi == a) & (y == b)
            part = jnp.where(mine, final[...], gathered[a, b])
            out_ref[a * half : (a + 1) * half, b * lanes : (b + 1) * lanes] = part
    for copy in pending + gathers:
        copy.wait_send()

    def sent(s, carry):
        sib(s).wait_send()
        return carry

    lax.fori_loop(0, 8, sent, 0)


def bands(half):
    third = half // 3 // 16 * 16
    return ((0, third), (third, third), (2 * third, half - 2 * third))


def weight_grad(token_rows, grad_low, cols, depth):
    half, lanes = cols // 2, depth // 4
    sizes = [size for _, size in bands(half)]
    vm = pl.BlockSpec(memory_space=pltpu.VMEM)
    dims = {"x_lo": 2, "z": 4, "y": 4, "x_hi": 2}
    kept = (
        (("x_lo", "y", "x_hi"), ("x_lo", "z", "x_hi"), ("z", "y")),
        (("x_lo", "x_hi"), ("z",), ("y",)),
        ((), (), ()),
    )

    def shape(stage, color):
        return tuple(dims[name] for name in kept[stage][color]) + (sizes[color], lanes)

    return pl.pallas_call(
        weight_grad_kernel,
        out_shape=jax.ShapeDtypeStruct((cols, depth), f32),
        in_specs=[vm, vm],
        out_specs=vm,
        scratch_shapes=[
            pltpu.VMEM((grad_low.shape[1], grad_low.shape[0]), bf16),
            pltpu.VMEM((8, 4, 2, half, lanes), bf16),
            pltpu.VMEM((8, 4, 2, half, lanes), bf16),
            pltpu.VMEM((2, 4, 4, 2, half, lanes), f32),
            pltpu.VMEM((2, 4, 4, 2, half, lanes), bf16),
        ]
        + [pltpu.VMEM((3,) + shape(0, c), bf16) for c in range(3)]
        + [pltpu.VMEM(shape(0, c), f32) for c in range(3)]
        + [pltpu.VMEM(shape(0, c), bf16) for c in range(3)]
        + [pltpu.VMEM((3,) + shape(1, c), bf16) for c in range(3)]
        + [pltpu.VMEM(shape(1, c), f32) for c in range(3)]
        + [pltpu.VMEM((3,) + shape(2, c), f32) for c in range(3)]
        + [
            pltpu.VMEM((half, lanes), f32),
            pltpu.VMEM((2, 4, half, lanes), f32),
            pltpu.SemaphoreType.DMA((8,)),
            pltpu.SemaphoreType.DMA((8,)),
            pltpu.SemaphoreType.DMA((27,)),
            pltpu.SemaphoreType.DMA((27,)),
            pltpu.SemaphoreType.DMA((21,)),
            pltpu.SemaphoreType.DMA((21,)),
        ],
        compiler_params=pltpu.CompilerParams(
            collective_id=1, has_side_effects=True, vmem_limit_bytes=48 * 2**20
        ),
    )(token_rows, grad_low)


def shards(pieces, hidden_rows, inner_rows, weight_proj, decay_log, step_bias, skip_gain, grad_output):
    token_rows = hidden_rows.reshape(-1, hidden_rows.shape[-1])
    value_rows = inner_rows.reshape(-1, inner_rows.shape[-1])
    cotangent = grad_output.reshape(value_rows.shape)
    cols = weight_proj.shape[1]
    heads = decay_log.shape[0]
    whole = lax.all_gather(weight_proj, "dp", axis=0, tiled=True)
    padded = jnp.pad(whole, ((0, 0), (0, 3 * NS - cols)))
    projected = jnp.dot(token_rows, padded, preferred_element_type=f32)
    head = jnp.pad(jnp.stack([step_bias, decay_log]), ((0, 6), (0, NS - heads)))
    output, grad_values, grad_low = scan_pass(
        pieces, skip_gain, projected, head, value_rows, cotangent
    )
    ssd_output = output.reshape(inner_rows.shape)
    grad_inner = grad_values.reshape(inner_rows.shape)
    grad_weight = weight_grad(token_rows, grad_low, cols, weight_proj.shape[0]).T
    grad_tokens = dot(grad_low[:, :cols], whole, NT)
    grad_hidden = grad_tokens.astype(bf16).reshape(hidden_rows.shape)
    return (ssd_output, grad_inner, grad_hidden, grad_weight)


def solution(mesh):
    rows = P("dp", "ctx", None)
    return jax.shard_map(
        partial(shards, mesh.shape["ctx"]),
        mesh=mesh,
        in_specs=(rows, rows, P("dp", None), P(), P(), P(), rows),
        out_specs=(rows, rows, rows, P("dp", None)),
        check_vma=False,
    )
```

```python
from functools import partial

import jax
import jax.numpy as jnp
from jax import lax
from jax.experimental import pallas as pl
from jax.experimental.pallas import tpu as pltpu
from jax.sharding import PartitionSpec as P

PS = 128
NS = 128
CHUNK = 2
LAG = 4
MESH = pl.DeviceIdType.MESH
highest = lax.Precision.HIGHEST
f32 = jnp.float32
bf16 = jnp.bfloat16
NN = (((1,), (0,)), ((), ()))
NT = (((1,), (1,)), ((), ()))
TN = (((0,), (0,)), ((), ()))


def dot(a, b, dims=NN):
    return lax.dot_general(a, b, dims, preferred_element_type=f32)


def dot_high(a, b, dims=NN):
    return lax.dot_general(a, b, dims, preferred_element_type=f32, precision=highest)


def split(a):
    high = a.astype(bf16)
    return high, (a - high.astype(f32)).astype(bf16)


def scan_kernel(
    pieces, heads, gain_ref, proj_ref, head_ref, x_ref, dy_ref, y_ref, dx_ref, grad_ref,
    run, run_t, step_t, step_c, key_t, query_t, key_hl, query_hl, scores,
    acc_diff, acc_cross, acc_const, dq, dk, dscores,
    state_in, state_out, grad_in, grad_out, sf, rf, sb, rb,
):
    k = lax.axis_index("ctx")
    last = pieces - 1
    tokens = proj_ref.shape[0]
    half = tokens // 2
    chunks = heads // CHUNK
    right = lax.rem(k + 1, pieces)
    left = lax.rem(k + pieces - 1, pieces)

    barrier = pltpu.get_barrier_semaphore()
    for neighbour in (left, right):
        pl.semaphore_signal(barrier, inc=1, device_id={"ctx": neighbour}, device_id_type=MESH)

    rows = lax.broadcasted_iota(jnp.int32, (tokens, tokens), 0)
    cols = lax.broadcasted_iota(jnp.int32, (tokens, tokens), 1)
    key = proj_ref[:, :NS]
    query = proj_ref[:, NS : 2 * NS] * NS ** (-0.5)
    bias = head_ref[0:1, :]
    rate = jnp.exp(head_ref[1:2, :])
    pre = proj_ref[:, 2 * NS :] + bias
    steps = jnp.maximum(pre, 0.0) + jnp.log1p(jnp.exp(-jnp.abs(pre)))
    running = dot_high((rows >= cols).astype(f32), -rate * steps)
    run[...] = running
    run_t[...] = running.T
    step_c[...] = steps
    step_t[...] = steps.T
    key_t[...] = key.T
    query_t[...] = query.T
    high, low = split(key)
    key_hl[:, :NS] = high
    key_hl[:, NS:] = low
    high, low = split(query)
    query_hl[:, :NS] = high
    query_hl[:, NS:] = low
    scores[...] = dot_high(query, key, NT)
    dq[...] = jnp.zeros_like(dq)
    dk[...] = jnp.zeros_like(dk)
    dscores[...] = jnp.zeros_like(dscores)
    acc_diff[...] = jnp.zeros_like(acc_diff)
    acc_cross[...] = jnp.zeros_like(acc_cross)
    acc_const[...] = jnp.zeros_like(acc_const)

    @pl.when(k == 0)
    def _():
        state_in[...] = jnp.zeros_like(state_in)

    @pl.when(k == last)
    def _():
        grad_in[...] = jnp.zeros_like(grad_in)

    pl.semaphore_wait(barrier, 2)

    def copy_fwd(j):
        part = pl.ds(j * CHUNK, CHUNK)
        return pltpu.make_async_remote_copy(
            src_ref=state_out.at[part], dst_ref=state_in.at[part],
            send_sem=sf.at[j], recv_sem=rf.at[j],
            device_id={"ctx": right}, device_id_type=MESH,
        )

    def copy_bwd(j):
        part = pl.ds(j * CHUNK, CHUNK)
        return pltpu.make_async_remote_copy(
            src_ref=grad_out.at[part], dst_ref=grad_in.at[part],
            send_sem=sb.at[j], recv_sem=rb.at[j],
            device_id={"ctx": left}, device_id_type=MESH,
        )

    def columns(h):
        return pl.ds(pl.multiple_of(h * PS, PS), PS)

    def forward(j):
        local = []
        for u in range(CHUNK):
            h = j * CHUNK + u
            r_row = run_t[pl.ds(h, 1), :]
            r_end = r_row[:, tokens - 1 : tokens]
            weight = jnp.exp(r_end - r_row) * step_t[pl.ds(h, 1), :]
            high, low = split(key_t[...] * weight)
            x = x_ref[:, columns(h)]
            local.append((h, jnp.exp(r_end), dot(high, x) + dot(low, x)))

        @pl.when(k > 0)
        def _():
            copy_fwd(j).wait_recv()

        @pl.when(k < last)
        def _():
            for h, decay, state in local:
                state_out[h] = (decay * state_in[h].astype(f32) + state).astype(bf16)
            copy_fwd(j).start()

    def backward(j):
        local = []
        for u in range(CHUNK):
            h = j * CHUNK + u
            r_row = run_t[pl.ds(h, 1), :]
            r_end = r_row[:, tokens - 1 : tokens]
            high, low = split(query_t[...] * jnp.exp(r_row))
            dy = dy_ref[:, columns(h)]
            local.append((h, jnp.exp(r_end), dot(high, dy) + dot(low, dy)))

        @pl.when(k < last)
        def _():
            copy_bwd(j).wait_recv()

        @pl.when(k > 0)
        def _():
            for h, decay, state in local:
                grad_out[h] = (decay * grad_in[h].astype(f32) + state).astype(bf16)
            copy_bwd(j).start()

    def compute(h):
        lane = lax.broadcasted_iota(jnp.int32, (tokens, NS), 1)
        mine = lane == h
        r_col = jnp.sum(jnp.where(mine, run[...], 0.0), axis=1, keepdims=True)
        s_col = jnp.sum(jnp.where(mine, step_c[...], 0.0), axis=1, keepdims=True)
        r_row = run_t[pl.ds(h, 1), :]
        s_row = step_t[pl.ds(h, 1), :]
        r_end = r_row[:, tokens - 1 : tokens]
        x = x_ref[:, columns(h)]
        dy = dy_ref[:, columns(h)]
        gain = gain_ref[h]

        def decays(begin, width):
            t = lax.broadcasted_iota(jnp.int32, (half, width), 0) + begin
            s = lax.broadcasted_iota(jnp.int32, (half, width), 1)
            gaps = r_col[begin : begin + half] - r_row[:, :width]
            return jnp.exp(jnp.where(t >= s, gaps, -1e30)) * s_row[:, :width]

        top = decays(0, half)
        bottom = decays(half, tokens)
        mix_top = (top * scores[:half, :half]).astype(bf16)
        mix_bottom = (bottom * scores[half:, :]).astype(bf16)
        dscores[:half, :half] += top * dot(dy[:half], x[:half], NT)
        dscores[half:, :] += bottom * dot(dy[half:], x, NT)
        y = jnp.concatenate([dot(mix_top, x[:half]), dot(mix_bottom, x)], axis=0)
        dx = dot(mix_bottom, dy[half:], TN)
        dx = jnp.concatenate([dx[:half] + dot(mix_top, dy[:half], TN), dx[half:]], axis=0)

        state = state_in[h]
        grad = grad_in[h]
        from_start = jnp.exp(r_col)
        to_end = jnp.exp(r_end - r_col) * s_col
        y += from_start * dot(query_hl[...], jnp.concatenate([state, state], axis=0))
        carried = to_end * dot(key_hl[...], jnp.concatenate([grad, grad], axis=0))
        dx += carried
        dq[...] += from_start * dot(dy, state, NT)
        dk[...] += to_end * dot(x, grad, NT)
        xf = x.astype(f32)
        dyf = dy.astype(f32)
        y_ref[:, columns(h)] = (y + gain * xf).astype(bf16)
        dx_ref[:, columns(h)] = (dx + gain * dyf).astype(bf16)
        cross = xf * dx
        acc_cross[...] = jnp.where(mine, jnp.sum(cross, axis=1, keepdims=True), acc_cross[...])
        acc_diff[...] = jnp.where(
            mine, jnp.sum(dyf * y - cross, axis=1, keepdims=True), acc_diff[...]
        )
        inner = jnp.sum(grad.astype(f32) * state.astype(f32), axis=0, keepdims=True)
        inner = jnp.sum(inner, axis=1, keepdims=True)
        outer = jnp.sum(jnp.sum(xf * carried, axis=0, keepdims=True), axis=1, keepdims=True)
        const = jnp.exp(r_end) * inner + outer
        acc_const[...] = jnp.where(mine[:8], const, acc_const[...])

    start_f = LAG * k
    start_b = LAG * (last - k)
    start_c = jnp.maximum(start_f, start_b)

    def iteration(i, carry):
        jf = i - start_f
        jb = i - start_b
        jc = i - start_c

        @pl.when((jf >= 0) & (jf < chunks))
        def _():
            forward(jf)

        @pl.when((jb >= 0) & (jb < chunks))
        def _():
            backward(jb)

        @pl.when((jc >= 0) & (jc < chunks))
        def _():
            for u in range(CHUNK):
                compute(jc * CHUNK + u)

        return carry

    lax.fori_loop(0, chunks + LAG * last, iteration, 0)

    @pl.when(k < last)
    def _():
        def wait(j, carry):
            copy_fwd(j).wait_send()
            return carry

        lax.fori_loop(0, chunks, wait, 0)

    @pl.when(k > 0)
    def _():
        def wait(j, carry):
            copy_bwd(j).wait_send()
            return carry

        lax.fori_loop(0, chunks, wait, 0)

    key = proj_ref[:, :NS]
    query = proj_ref[:, NS : 2 * NS] * NS ** (-0.5)
    pre = proj_ref[:, 2 * NS :] + head_ref[0:1, :]
    d_log = dot_high((cols >= rows).astype(f32), acc_diff[...]) + acc_const[0:1, :]
    slope = 1.0 / (1.0 + jnp.exp(-pre))
    ratio = jnp.where(pre < -20.0, 1.0, slope / step_c[...])
    dk_all = dk[...] + dot_high(dscores[...].T, query)
    dq_all = dq[...] + dot_high(dscores[...], key)
    grad_ref[:, :NS] = dk_all.astype(bf16)
    grad_ref[:, NS : 2 * NS] = (dq_all * NS ** (-0.5)).astype(bf16)
    rate = jnp.exp(head_ref[1:2, :])
    grad_ref[:, 2 * NS :] = (acc_cross[...] * ratio - rate * d_log * slope).astype(bf16)


def scan_pass(pieces, gain, proj, head, x, dy):
    tokens, width = x.shape
    heads = width // PS
    chunks = heads // CHUNK
    vm = pl.BlockSpec(memory_space=pltpu.VMEM)
    big = (heads, NS, PS)
    return pl.pallas_call(
        partial(scan_kernel, pieces, heads),
        out_shape=(
            jax.ShapeDtypeStruct(x.shape, bf16),
            jax.ShapeDtypeStruct(x.shape, bf16),
            jax.ShapeDtypeStruct((tokens, 3 * NS), bf16),
        ),
        in_specs=[pl.BlockSpec(memory_space=pltpu.SMEM), vm, vm, vm, vm],
        out_specs=(vm, vm, vm),
        scratch_shapes=[
            pltpu.VMEM((tokens, NS), f32),
            pltpu.VMEM((NS, tokens), f32),
            pltpu.VMEM((NS, tokens), f32),
            pltpu.VMEM((tokens, NS), f32),
            pltpu.VMEM((NS, tokens), f32),
            pltpu.VMEM((NS, tokens), f32),
            pltpu.VMEM((tokens, 2 * NS), bf16),
            pltpu.VMEM((tokens, 2 * NS), bf16),
            pltpu.VMEM((tokens, tokens), f32),
            pltpu.VMEM((tokens, NS), f32),
            pltpu.VMEM((tokens, NS), f32),
            pltpu.VMEM((8, NS), f32),
            pltpu.VMEM((tokens, NS), f32),
            pltpu.VMEM((tokens, NS), f32),
            pltpu.VMEM((tokens, tokens), f32),
            pltpu.VMEM(big, bf16),
            pltpu.VMEM(big, bf16),
            pltpu.VMEM(big, bf16),
            pltpu.VMEM(big, bf16),
            pltpu.SemaphoreType.DMA((chunks,)),
            pltpu.SemaphoreType.DMA((chunks,)),
            pltpu.SemaphoreType.DMA((chunks,)),
            pltpu.SemaphoreType.DMA((chunks,)),
        ],
        compiler_params=pltpu.CompilerParams(
            collective_id=0, has_side_effects=True, vmem_limit_bytes=48 * 2**20
        ),
    )(gain, proj, head, x, dy)


def weight_grad_kernel(
    h_ref, g_ref, out_ref, g_t, sib_send, sib_recv, own, low,
    slot_a0, slot_a1, slot_a2, sum_a0, sum_a1, sum_a2, low_a0, low_a1, low_a2,
    slot_b0, slot_b1, slot_b2, sum_b0, sum_b1, sum_b2,
    slot_c0, slot_c1, slot_c2, final, gathered,
    sib_s, sib_r, st_s, st_r, ga_s, ga_r,
):
    dp = lax.axis_index("dp")
    ctx = lax.axis_index("ctx")
    x_lo, z, core = dp // 8, lax.rem(dp // 2, 4), lax.rem(dp, 2)
    x_hi, y = ctx // 4, lax.rem(ctx, 4)
    x = x_hi * 2 + x_lo
    rows = out_ref.shape[0]
    depth = out_ref.shape[1]
    half = rows // 2
    lanes = depth // 4

    def device(x_lo=x_lo, z=z, core=core, x_hi=x_hi, y=y):
        return {"dp": x_lo * 8 + z * 2 + core, "ctx": x_hi * 4 + y}

    def ring(axis, d):
        if axis == "z":
            return device(z=lax.rem(z + d, 4)), (lax.rem(z + d, 4),)
        if axis == "y":
            return device(y=lax.rem(y + d, 4)), (lax.rem(y + d, 4),)
        to = lax.rem(x + d, 4)
        return device(x_lo=lax.rem(to, 2), x_hi=to // 2), (lax.rem(to, 2), to // 2)

    barrier = pltpu.get_barrier_semaphore()
    others = [(a, b) for a in range(2) for b in range(4) if a + b]
    peers = [device(core=1 - core)]
    peers += [ring("z", d)[0] for d in (1, 2, 3)]
    peers += [ring("x", d)[0] for d in (1, 3)]
    peers += [device(x_hi=lax.rem(x_hi + a, 2), y=lax.rem(y + b, 4)) for a, b in others]
    for peer in peers:
        pl.semaphore_signal(barrier, inc=1, device_id=peer, device_id_type=MESH)
    g_t[...] = g_ref[...].astype(f32).T.astype(bf16)
    pl.semaphore_wait(barrier, len(peers))

    def product(s, side):
        at = (s // 4) * 8 + lax.rem(s, 4) * 2 + side
        block = h_ref[:, pl.ds(pl.multiple_of(at * depth, depth), depth)]
        return dot(g_t[:rows, :], block)

    def sib(s):
        return pltpu.make_async_remote_copy(
            src_ref=sib_send.at[s], dst_ref=sib_recv.at[s],
            send_sem=sib_s.at[s], recv_sem=sib_r.at[s],
            device_id=device(core=1 - core), device_id_type=MESH,
        )

    def for_sibling(s, carry):
        p = product(s, 1 - core).astype(bf16)
        for b in range(4):
            for a in range(2):
                sib_send[s, b, a] = p[a * half : (a + 1) * half, b * lanes : (b + 1) * lanes]
        sib(s).start()
        return carry

    lax.fori_loop(0, 8, for_sibling, 0)

    def for_self(s, carry):
        p = product(s, core)
        sib(s).wait_recv()
        for b in range(4):
            for a in range(2):
                total = p[a * half : (a + 1) * half, b * lanes : (b + 1) * lanes]
                total += sib_recv[s, b, a].astype(f32)
                own[s // 4, lax.rem(s, 4), b, a] = total
                low[s // 4, lax.rem(s, 4), b, a] = total.astype(bf16)
        return carry

    lax.fori_loop(0, 8, for_self, 0)

    orders = (("z", "y", "x"), ("y", "x", "z"), ("x", "z", "y"))
    slots = ((slot_a0, slot_b0, slot_c0), (slot_a1, slot_b1, slot_c1), (slot_a2, slot_b2, slot_c2))

    def pick(left, axis, place):
        at = []
        for name in left:
            if name == axis:
                at.append(place[0])
            elif axis == "x" and name == "x_lo":
                at.append(place[0])
            elif axis == "x" and name == "x_hi":
                at.append(place[1])
            else:
                at.append(slice(None))
        return tuple(at)

    def rest(left, axis):
        gone = ("x_lo", "x_hi") if axis == "x" else (axis,)
        return tuple(name for name in left if name not in gone)

    everything = ("x_lo", "z", "y", "x_hi")

    def exchange(color, stage, source, left):
        axis = orders[color][stage]
        off, size = bands(half)[color]
        window = (pl.ds(off, size),) if stage == 0 else ()
        copies = []
        for d in (1, 2, 3):
            peer, place = ring(axis, d)
            n = color * 9 + stage * 3 + d - 1
            copies.append(
                pltpu.make_async_remote_copy(
                    src_ref=source.at[pick(left, axis, place) + window],
                    dst_ref=slots[color][stage].at[d - 1],
                    send_sem=st_s.at[n], recv_sem=st_r.at[n],
                    device_id=peer, device_id_type=MESH,
                )
            )
            copies[-1].start()
        return copies

    def my_place(axis):
        return {"z": (z,), "y": (y,), "x": (x_lo, x_hi)}[axis]

    pending = []
    left = [everything] * 3
    current = []
    for color in range(3):
        current.append(exchange(color, 0, low, everything))
    sums = (sum_a0, sum_a1, sum_a2)
    lows = (low_a0, low_a1, low_a2)
    for color in range(3):
        axis = orders[color][0]
        off, size = bands(half)[color]
        for copy in current[color]:
            copy.wait_recv()
        pending += current[color]
        total = own[pick(everything, axis, my_place(axis)) + (pl.ds(off, size),)]
        for d in range(3):
            total += slots[color][0][d].astype(f32)
        sums[color][...] = total
        lows[color][...] = total.astype(bf16)
        left[color] = rest(everything, axis)
        current[color] = exchange(color, 1, lows[color], left[color])
    finals = (sum_b0, sum_b1, sum_b2)
    for color in range(3):
        axis = orders[color][1]
        for copy in current[color]:
            copy.wait_recv()
        pending += current[color]
        total = sums[color][pick(left[color], axis, my_place(axis))]
        for d in range(3):
            total += slots[color][1][d].astype(f32)
        finals[color][...] = total
        left[color] = rest(left[color], axis)
        current[color] = exchange(color, 2, finals[color], left[color])
    gathers = []
    for color in range(3):
        axis = orders[color][2]
        off, size = bands(half)[color]
        for copy in current[color]:
            copy.wait_recv()
        pending += current[color]
        total = finals[color][pick(left[color], axis, my_place(axis))]
        for d in range(3):
            total += slots[color][2][d]
        final[pl.ds(off, size)] = total
        for m, (a, b) in enumerate(others):
            gathers.append(
                pltpu.make_async_remote_copy(
                    src_ref=final.at[pl.ds(off, size)],
                    dst_ref=gathered.at[x_hi, y, pl.ds(off, size)],
                    send_sem=ga_s.at[color * 7 + m], recv_sem=ga_r.at[color * 7 + m],
                    device_id=device(x_hi=lax.rem(x_hi + a, 2), y=lax.rem(y + b, 4)),
                    device_id_type=MESH,
                )
            )
            gathers[-1].start()
    for copy in gathers:
        copy.wait_recv()
    for a in range(2):
        for b in range(4):
            mine = (x_hi == a) & (y == b)
            part = jnp.where(mine, final[...], gathered[a, b])
            out_ref[a * half : (a + 1) * half, b * lanes : (b + 1) * lanes] = part
    for copy in pending + gathers:
        copy.wait_send()

    def sent(s, carry):
        sib(s).wait_send()
        return carry

    lax.fori_loop(0, 8, sent, 0)


def bands(half):
    third = half // 3 // 16 * 16
    return ((0, third), (third, third), (2 * third, half - 2 * third))


def weight_grad(token_rows, grad_low, cols, depth):
    half, lanes = cols // 2, depth // 4
    sizes = [size for _, size in bands(half)]
    vm = pl.BlockSpec(memory_space=pltpu.VMEM)
    dims = {"x_lo": 2, "z": 4, "y": 4, "x_hi": 2}
    kept = (
        (("x_lo", "y", "x_hi"), ("x_lo", "z", "x_hi"), ("z", "y")),
        (("x_lo", "x_hi"), ("z",), ("y",)),
        ((), (), ()),
    )

    def shape(stage, color):
        return tuple(dims[name] for name in kept[stage][color]) + (sizes[color], lanes)

    return pl.pallas_call(
        weight_grad_kernel,
        out_shape=jax.ShapeDtypeStruct((cols, depth), f32),
        in_specs=[vm, vm],
        out_specs=vm,
        scratch_shapes=[
            pltpu.VMEM((grad_low.shape[1], grad_low.shape[0]), bf16),
            pltpu.VMEM((8, 4, 2, half, lanes), bf16),
            pltpu.VMEM((8, 4, 2, half, lanes), bf16),
            pltpu.VMEM((2, 4, 4, 2, half, lanes), f32),
            pltpu.VMEM((2, 4, 4, 2, half, lanes), bf16),
        ]
        + [pltpu.VMEM((3,) + shape(0, c), bf16) for c in range(3)]
        + [pltpu.VMEM(shape(0, c), f32) for c in range(3)]
        + [pltpu.VMEM(shape(0, c), bf16) for c in range(3)]
        + [pltpu.VMEM((3,) + shape(1, c), bf16) for c in range(3)]
        + [pltpu.VMEM(shape(1, c), f32) for c in range(3)]
        + [pltpu.VMEM((3,) + shape(2, c), f32) for c in range(3)]
        + [
            pltpu.VMEM((half, lanes), f32),
            pltpu.VMEM((2, 4, half, lanes), f32),
            pltpu.SemaphoreType.DMA((8,)),
            pltpu.SemaphoreType.DMA((8,)),
            pltpu.SemaphoreType.DMA((27,)),
            pltpu.SemaphoreType.DMA((27,)),
            pltpu.SemaphoreType.DMA((21,)),
            pltpu.SemaphoreType.DMA((21,)),
        ],
        compiler_params=pltpu.CompilerParams(
            collective_id=1, has_side_effects=True, vmem_limit_bytes=48 * 2**20
        ),
    )(token_rows, grad_low)


def project_kernel(
    w_ref, h_ref, proj_ref, all_ref, st_s, st_r, sib_s, sib_r
):
    dp = lax.axis_index("dp")
    ctx = lax.axis_index("ctx")
    x_lo, z, core = dp // 8, lax.rem(dp // 2, 4), lax.rem(dp, 2)
    x_hi, y = ctx // 4, lax.rem(ctx, 4)
    x = x_hi * 2 + x_lo
    cols, depth = w_ref.shape
    half, lanes = cols // 2, depth // 4

    def device(x_lo=x_lo, z=z, core=core, x_hi=x_hi, y=y):
        return {"dp": x_lo * 8 + z * 2 + core, "ctx": x_hi * 4 + y}

    def ring(axis, d):
        if axis == "z":
            return device(z=lax.rem(z + d, 4))
        if axis == "y":
            return device(y=lax.rem(y + d, 4))
        to = lax.rem(x + d, 4)
        return device(x_lo=lax.rem(to, 2), x_hi=to // 2)

    barrier = pltpu.get_barrier_semaphore()
    peers = [device(core=1 - core)]
    peers += [ring(axis, d) for axis in "xyz" for d in (1, 2, 3)]
    for peer in peers:
        pl.semaphore_signal(barrier, inc=1, device_id=peer, device_id_type=MESH)
    for a in range(2):
        for b in range(4):
            @pl.when((x_hi == a) & (y == b))
            def _():
                all_ref[core, x_lo, z, b, a] = w_ref[
                    a * half : (a + 1) * half, b * lanes : (b + 1) * lanes
                ]
    proj_ref[...] = jnp.zeros_like(proj_ref)
    pl.semaphore_wait(barrier, len(peers))

    whole = slice(None)
    orders = ("xyz", "zxy", "yzx")

    def region(side, color, have, x_lo=x_lo, z=z, x_hi=x_hi, y=y):
        off, size = bands(half)[color]
        return all_ref.at[
            side,
            whole if "x" in have else x_lo,
            whole if "z" in have else z,
            whole if "y" in have else y,
            whole if "x" in have else x_hi,
            pl.ds(off, size),
        ]

    def exchange(color, stage):
        axis = orders[color][stage]
        copies = []
        for d in (1, 2, 3):
            n = color * 9 + stage * 3 + d - 1
            part = region(core, color, orders[color][:stage])
            copies.append(
                pltpu.make_async_remote_copy(
                    src_ref=part, dst_ref=part, send_sem=st_s.at[n], recv_sem=st_r.at[n],
                    device_id=ring(axis, d), device_id_type=MESH,
                )
            )
            copies[-1].start()
        return copies

    def origin(axis, d):
        if axis == "z":
            return {"z": lax.rem(z + 4 - d, 4)}
        if axis == "y":
            return {"y": lax.rem(y + 4 - d, 4)}
        at = lax.rem(x + 4 - d, 4)
        return {"x_lo": lax.rem(at, 2), "x_hi": at // 2}

    def to_sibling(color, d):
        place = origin(orders[color][2], d) if d else {}
        part = region(core, color, orders[color][:2], **place)
        copy = pltpu.make_async_remote_copy(
            src_ref=part, dst_ref=part,
            send_sem=sib_s.at[color * 4 + d], recv_sem=sib_r.at[color * 4 + d],
            device_id=device(core=1 - core), device_id_type=MESH,
        )
        copy.start()
        return copy

    pending, current, shared = [], [], []
    for color in range(3):
        current.append(exchange(color, 0))
    for stage in (1, 2):
        for color in range(3):
            for copy in current[color]:
                copy.wait_recv()
            pending += current[color]
            current[color] = exchange(color, stage)
            if stage == 2:
                shared.append(to_sibling(color, 0))
    for d in (1, 3, 2):
        for color in range(3):
            current[color][d - 1].wait_recv()
            shared.append(to_sibling(color, d))
    for color in range(3):
        pending += current[color]

    def add(s, side):
        at = (s // 4) * 8 + lax.rem(s, 4) * 2 + side
        block = h_ref[:, pl.ds(pl.multiple_of(at * depth, depth), depth)]
        weights = jnp.concatenate(
            [all_ref[side, s // 4, lax.rem(s, 4), b].reshape(cols, lanes) for b in range(4)],
            axis=1,
        )
        proj_ref[:, :cols] += dot(block, weights, NT)

    def mine(s, carry):
        add(s, core)
        return carry

    def other(s, carry):
        add(s, 1 - core)
        return carry

    lax.fori_loop(0, 8, mine, 0)
    for copy in shared:
        copy.wait_recv()
    lax.fori_loop(0, 8, other, 0)
    for copy in pending + shared:
        copy.wait_send()


def project(weight_t, token_rows):
    cols, depth = weight_t.shape
    vm = pl.BlockSpec(memory_space=pltpu.VMEM)
    return pl.pallas_call(
        project_kernel,
        out_shape=(
            jax.ShapeDtypeStruct((token_rows.shape[0], 3 * NS), f32),
            jax.ShapeDtypeStruct((2, 2, 4, 4, 2, cols // 2, depth // 4), bf16),
        ),
        in_specs=[vm, vm],
        out_specs=(vm, vm),
        scratch_shapes=[
            pltpu.SemaphoreType.DMA((27,)),
            pltpu.SemaphoreType.DMA((27,)),
            pltpu.SemaphoreType.DMA((12,)),
            pltpu.SemaphoreType.DMA((12,)),
        ],
        compiler_params=pltpu.CompilerParams(
            collective_id=2, has_side_effects=True, vmem_limit_bytes=40 * 2**20
        ),
    )(weight_t, token_rows)


def hidden_kernel(g_ref, w_ref, out_ref):
    cols = w_ref.shape[2] * w_ref.shape[3]
    weights = jnp.concatenate([w_ref[0, b].reshape(cols, -1) for b in range(4)], axis=1)
    out_ref[...] = dot(g_ref[:, :cols], weights).astype(bf16)


def hidden_grad(grad_low, weights):
    tokens = grad_low.shape[0]
    half, lanes = weights.shape[-2:]
    depth = 4 * lanes
    flat = weights.reshape(2 * 8, 4, 2, half, lanes)
    return pl.pallas_call(
        hidden_kernel,
        grid=(16,),
        out_shape=jax.ShapeDtypeStruct((tokens, 16 * depth), bf16),
        in_specs=[
            pl.BlockSpec(grad_low.shape, lambda i: (0, 0)),
            pl.BlockSpec((1, 4, 2, half, lanes), lambda i: (i, 0, 0, 0, 0)),
        ],
        out_specs=pl.BlockSpec((tokens, depth), lambda i: (0, (i % 8) * 2 + i // 8)),
    )(grad_low, flat)


def shards(pieces, hidden_rows, inner_rows, weight_proj, decay_log, step_bias, skip_gain, grad_output):
    token_rows = hidden_rows.reshape(-1, hidden_rows.shape[-1])
    value_rows = inner_rows.reshape(-1, inner_rows.shape[-1])
    cotangent = grad_output.reshape(value_rows.shape)
    cols = weight_proj.shape[1]
    heads = decay_log.shape[0]
    projected, weights = project(weight_proj.T, token_rows)
    head = jnp.pad(jnp.stack([step_bias, decay_log]), ((0, 6), (0, NS - heads)))
    output, grad_values, grad_low = scan_pass(
        pieces, skip_gain, projected, head, value_rows, cotangent
    )
    ssd_output = output.reshape(inner_rows.shape)
    grad_inner = grad_values.reshape(inner_rows.shape)
    grad_weight = weight_grad(token_rows, grad_low, cols, weight_proj.shape[0]).T
    grad_hidden = hidden_grad(grad_low, weights).reshape(hidden_rows.shape)
    return (ssd_output, grad_inner, grad_hidden, grad_weight)


def solution(mesh):
    rows = P("dp", "ctx", None)
    return jax.shard_map(
        partial(shards, mesh.shape["ctx"]),
        mesh=mesh,
        in_specs=(rows, rows, P("dp", None), P(), P(), P(), rows),
        out_specs=(rows, rows, rows, P("dp", None)),
        check_vma=False,
    )
```

```python
from functools import partial

import jax
import jax.numpy as jnp
from jax import lax
from jax.experimental import pallas as pl
from jax.experimental.pallas import tpu as pltpu
from jax.sharding import PartitionSpec as P

PS = 128
NS = 128
CHUNK = 2
LAG = 2
LAG_FAR = 4
MESH = pl.DeviceIdType.MESH
highest = lax.Precision.HIGHEST
f32 = jnp.float32
bf16 = jnp.bfloat16
NN = (((1,), (0,)), ((), ()))
NT = (((1,), (1,)), ((), ()))
TN = (((0,), (0,)), ((), ()))


def dot(a, b, dims=NN):
    return lax.dot_general(a, b, dims, preferred_element_type=f32)


def dot_high(a, b, dims=NN):
    return lax.dot_general(a, b, dims, preferred_element_type=f32, precision=highest)


def split(a):
    high = a.astype(bf16)
    return high, (a - high.astype(f32)).astype(bf16)

BANDS = 3
ORDER_SUM = ("zyx", "yxz", "xzy")
ORDER_GATHER = ("xyz", "zxy", "yzx")


def bands(half):
    third = half // 3 // 16 * 16
    return ((0, third), (third, third), (2 * third, half - 2 * third))


def remote(src, dst, send, recv, device):
    return pltpu.make_async_remote_copy(
        src_ref=src, dst_ref=dst, send_sem=send, recv_sem=recv,
        device_id=device, device_id_type=MESH,
    )


class Place:
    def __init__(self):
        dp, ctx = lax.axis_index("dp"), lax.axis_index("ctx")
        self.x_lo, self.z, self.core = dp // 8, lax.rem(dp // 2, 4), lax.rem(dp, 2)
        self.x_hi, self.y = ctx // 4, lax.rem(ctx, 4)
        self.x = self.x_hi * 2 + self.x_lo
        self.ctx = ctx

    def device(self, **other):
        at = {name: getattr(self, name) for name in ("x_lo", "z", "core", "x_hi", "y")}
        at.update(other)
        return {
            "dp": at["x_lo"] * 8 + at["z"] * 2 + at["core"],
            "ctx": at["x_hi"] * 4 + at["y"],
        }

    def along(self, axis, d):
        to = lax.rem(getattr(self, axis) + d, 4)
        return {"x_lo": lax.rem(to, 2), "x_hi": to // 2} if axis == "x" else {axis: to}

    def ring(self, axis, d):
        return self.device(**self.along(axis, d))

    def sibling(self):
        return self.device(core=1 - self.core)

    def piece(self, a, b):
        return self.device(x_hi=lax.rem(self.x_hi + a, 2), y=lax.rem(self.y + b, 4))

    def columns(self, s, side, depth):
        at = (s // 4) * 8 + lax.rem(s, 4) * 2 + side
        return pl.ds(pl.multiple_of(at * depth, depth), depth)


OTHERS = [(a, b) for a in range(2) for b in range(4) if a + b]


def loop(count, body):
    def step(i, carry):
        body(i)
        return carry

    lax.fori_loop(0, count, step, 0)


def gather_weights(me, w_ref, all_ref, send, recv):
    cols, depth = w_ref.shape
    half = cols // 2
    whole = slice(None)

    def region(color, have):
        off, size = bands(half)[color]
        return all_ref.at[
            whole if "x" in have else me.x_lo,
            whole if "z" in have else me.z,
            whole if "y" in have else me.y,
            whole if "x" in have else me.x_hi,
            pl.ds(off, size),
        ]

    def exchange(color, stage):
        axis = ORDER_GATHER[color][stage]
        part = region(color, ORDER_GATHER[color][:stage])
        copies = []
        for d in (1, 3, 2):
            n = color * 9 + stage * 3 + d - 1
            copies.append(remote(part, part, send.at[n], recv.at[n], me.ring(axis, d)))
            copies[-1].start()
        return copies

    pending = []
    current = [exchange(color, 0) for color in range(BANDS)]
    for stage in (1, 2, 3):
        for color in range(BANDS):
            for copy in current[color]:
                copy.wait_recv()
            pending += current[color]
            if stage < 3:
                current[color] = exchange(color, stage)
    return pending


def sum_start(me, low, slots, send, recv):
    return [sum_exchange(me, color, 0, low, "xzy", slots, send, recv) for color in range(BANDS)]


def pick(left, axis, place):
    at = []
    for name in ("x_lo", "z", "y", "x_hi"):
        if name[0] in left:
            at.append(place[name] if name[0] == axis else slice(None))
    return tuple(at)


def sum_exchange(me, color, stage, source, left, slots, send, recv):
    axis = ORDER_SUM[color][stage]
    off, size = bands(slots[0][2].shape[1] + slots[1][2].shape[1] + slots[2][2].shape[1])[color]
    window = (pl.ds(off, size),) if stage == 0 else ()
    copies = []
    for d in (1, 3, 2):
        n = color * 9 + stage * 3 + d - 1
        part = source.at[pick(left, axis, me.along(axis, d)) + window]
        copies.append(
            remote(part, slots[color][stage].at[d - 1], send.at[n], recv.at[n], me.ring(axis, d))
        )
        copies[-1].start()
    return copies


def sum_finish(me, current, own, slots, sums, lows, finals, final, gathered, out_ref, send, recv, ga_s, ga_r):
    half = final.shape[0]
    lanes = final.shape[1]
    pending = []

    def arrived(color, stage, source, left, window=()):
        axis = ORDER_SUM[color][stage]
        pending.extend(current[color])
        for copy in current[color]:
            copy.wait_recv()
        total = source[pick(left, axis, me.along(axis, 0)) + window]
        for d in range(3):
            total += slots[color][stage][d].astype(f32)
        return total

    for color in range(BANDS):
        off, size = bands(half)[color]
        total = arrived(color, 0, own, "xzy", (pl.ds(off, size),))
        sums[color][...] = total
        lows[color][...] = total.astype(bf16)
        left = ORDER_SUM[color][1:]
        current[color] = sum_exchange(me, color, 1, lows[color], left, slots, send, recv)
    for color in range(BANDS):
        finals[color][...] = arrived(color, 1, sums[color], ORDER_SUM[color][1:])
        left = ORDER_SUM[color][2:]
        current[color] = sum_exchange(me, color, 2, finals[color], left, slots, send, recv)
    gathers = []
    for color in range(BANDS):
        off, size = bands(half)[color]
        final[pl.ds(off, size)] = arrived(color, 2, finals[color], ORDER_SUM[color][2:])
        for m, (a, b) in enumerate(OTHERS):
            n = color * 7 + m
            gathers.append(
                remote(
                    final.at[pl.ds(off, size)], gathered.at[me.x_hi, me.y, pl.ds(off, size)],
                    ga_s.at[n], ga_r.at[n], me.piece(a, b),
                )
            )
            gathers[-1].start()
    for copy in gathers:
        copy.wait_recv()
    for a in range(2):
        for b in range(4):
            mine = (me.x_hi == a) & (me.y == b)
            part = jnp.where(mine, final[...], gathered[a, b])
            out_ref[a * half : (a + 1) * half, b * lanes : (b + 1) * lanes] = part
    return pending + gathers


def layer_kernel(
    heads, gain_ref, head_ref, w_ref, h_ref, x_hbm, dy_hbm,
    y_hbm, dx_hbm, hid_hbm, gw_ref,
    h_all, w_all, x_ref, dy_ref, part, proj_in, proj_ref,
    run, run_t, step_t, step_c, key_t, query_t, key_hl, query_hl, scores,
    acc_diff, acc_cross, acc_const, dq, dk, dscores,
    state_in, state_out, grad_in, grad_out,
    g_all, gt_all, own, low,
    slot_a0, slot_a1, slot_a2, sum_a0, sum_a1, sum_a2, low_a0, low_a1, low_a2,
    slot_b0, slot_b1, slot_b2, sum_b0, sum_b1, sum_b2,
    slot_c0, slot_c1, slot_c2, final, gathered, hid,
    load_h, load_xy, hs, hr, ag_s, ag_r, one_s, one_r, sf, rf, sb, rb,
    store_y, store_dx, st_s, st_r, ga_s, ga_r, hid_l, hid_s, hid_r,
):
    me = Place()
    k = me.ctx
    pieces = lax.axis_size("ctx")
    last = pieces - 1
    tokens = proj_ref.shape[0]
    half = tokens // 2
    chunks = heads // CHUNK
    cols, depth = w_ref.shape
    band, lanes = cols // 2, depth // 4
    right = {"ctx": lax.rem(k + 1, pieces)}
    left = {"ctx": lax.rem(k + pieces - 1, pieces)}

    barrier = pltpu.get_barrier_semaphore()
    peers = [me.sibling()]
    peers += [me.ring("z", d) for d in (1, 2, 3)]
    peers += [me.ring("x", d) for d in (1, 3)]
    peers += [me.piece(a, b) for a, b in OTHERS]
    for peer in peers:
        pl.semaphore_signal(barrier, inc=1, device_id=peer, device_id_type=MESH)

    def load(s):
        return pltpu.make_async_copy(
            h_ref.at[:, me.columns(s, me.core, depth)], h_all.at[s, me.core], load_h.at[s]
        )

    def lend(s):
        return remote(
            h_ref.at[:, me.columns(s, 1 - me.core, depth)], h_all.at[s, me.core],
            hs.at[s], hr.at[s], me.sibling(),
        )

    loop(8, lambda s: load(s).start())
    load_x = pltpu.make_async_copy(x_hbm, x_ref, load_xy.at[0])
    load_dy = pltpu.make_async_copy(dy_hbm, dy_ref, load_xy.at[1])
    for a in range(2):
        for b in range(4):
            @pl.when((me.x_hi == a) & (me.y == b))
            def _():
                w_all[me.x_lo, me.z, b, a] = w_ref[
                    a * band : (a + 1) * band, b * lanes : (b + 1) * lanes
                ]
    part[...] = jnp.zeros_like(part)
    pl.semaphore_wait(barrier, len(peers))
    loop(8, lambda s: lend(s).start())
    load_x.start()
    load_dy.start()

    @pl.when(k == 0)
    def _():
        state_in[...] = jnp.zeros_like(state_in)

    @pl.when(k == last)
    def _():
        grad_in[...] = jnp.zeros_like(grad_in)

    dq[...] = jnp.zeros_like(dq)
    dk[...] = jnp.zeros_like(dk)
    dscores[...] = jnp.zeros_like(dscores)
    acc_diff[...] = jnp.zeros_like(acc_diff)
    acc_cross[...] = jnp.zeros_like(acc_cross)
    acc_const[...] = jnp.zeros_like(acc_const)

    pending = gather_weights(me, w_ref, w_all, ag_s, ag_r)

    def weights(s):
        parts = [w_all[s // 4, lax.rem(s, 4), b].reshape(cols, lanes) for b in range(4)]
        return jnp.concatenate(parts, axis=1)

    def project(s):
        load(s).wait()
        lend(s).wait_recv()
        part[:, :cols] += dot(h_all[s].reshape(2 * tokens, depth), weights(s), NT)

    loop(8, project)
    mine = pl.ds(pl.multiple_of(me.core * tokens, tokens), tokens)
    theirs = pl.ds(pl.multiple_of((1 - me.core) * tokens, tokens), tokens)
    give = remote(part.at[theirs], proj_in, one_s.at[0], one_r.at[0], me.sibling())
    give.start()
    give.wait_recv()
    pending.append(give)
    proj_ref[...] = part[mine] + proj_in[...]

    rows = lax.broadcasted_iota(jnp.int32, (tokens, tokens), 0)
    columns_at = lax.broadcasted_iota(jnp.int32, (tokens, tokens), 1)
    key = proj_ref[:, :NS]
    query = proj_ref[:, NS : 2 * NS] * NS ** (-0.5)
    pre = proj_ref[:, 2 * NS :] + head_ref[0:1, :]
    rate = jnp.exp(head_ref[1:2, :])
    steps = jnp.maximum(pre, 0.0) + jnp.log1p(jnp.exp(-jnp.abs(pre)))
    running = dot_high((rows >= columns_at).astype(f32), -rate * steps)
    run[...] = running
    run_t[...] = running.T
    step_c[...] = steps
    step_t[...] = steps.T
    key_t[...] = key.T
    query_t[...] = query.T
    high, low_part = split(key)
    key_hl[:, :NS] = high
    key_hl[:, NS:] = low_part
    high, low_part = split(query)
    query_hl[:, :NS] = high
    query_hl[:, NS:] = low_part
    scores[...] = dot_high(query, key, NT)
    load_x.wait()
    load_dy.wait()

    def copy_fwd(j):
        chunk = pl.ds(j * CHUNK, CHUNK)
        return remote(state_out.at[chunk], state_in.at[chunk], sf.at[j], rf.at[j], right)

    def copy_bwd(j):
        chunk = pl.ds(j * CHUNK, CHUNK)
        return remote(grad_out.at[chunk], grad_in.at[chunk], sb.at[j], rb.at[j], left)

    def columns(h, count=1):
        return pl.ds(pl.multiple_of(h * PS, PS), count * PS)

    def forward(j):
        local = []
        for u in range(CHUNK):
            h = j * CHUNK + u
            r_row = run_t[pl.ds(h, 1), :]
            r_end = r_row[:, tokens - 1 : tokens]
            weight = jnp.exp(r_end - r_row) * step_t[pl.ds(h, 1), :]
            high, low_part = split(key_t[...] * weight)
            x = x_ref[:, columns(h)]
            local.append((h, jnp.exp(r_end), dot(high, x) + dot(low_part, x)))

        @pl.when(k > 0)
        def _():
            copy_fwd(j).wait_recv()

        @pl.when(k < last)
        def _():
            for h, decay, state in local:
                state_out[h] = (decay * state_in[h].astype(f32) + state).astype(bf16)
            copy_fwd(j).start()

    def backward(j):
        local = []
        for u in range(CHUNK):
            h = j * CHUNK + u
            r_row = run_t[pl.ds(h, 1), :]
            r_end = r_row[:, tokens - 1 : tokens]
            high, low_part = split(query_t[...] * jnp.exp(r_row))
            dy = dy_ref[:, columns(h)]
            local.append((h, jnp.exp(r_end), dot(high, dy) + dot(low_part, dy)))

        @pl.when(k < last)
        def _():
            copy_bwd(j).wait_recv()

        @pl.when(k > 0)
        def _():
            for h, decay, state in local:
                grad_out[h] = (decay * grad_in[h].astype(f32) + state).astype(bf16)
            copy_bwd(j).start()

    def one_head(h):
        lane = lax.broadcasted_iota(jnp.int32, (tokens, NS), 1)
        at_h = lane == h
        r_col = jnp.sum(jnp.where(at_h, run[...], 0.0), axis=1, keepdims=True)
        s_col = jnp.sum(jnp.where(at_h, step_c[...], 0.0), axis=1, keepdims=True)
        r_row = run_t[pl.ds(h, 1), :]
        s_row = step_t[pl.ds(h, 1), :]
        r_end = r_row[:, tokens - 1 : tokens]
        x = x_ref[:, columns(h)]
        dy = dy_ref[:, columns(h)]
        gain = gain_ref[h]

        def decays(begin, width):
            t = lax.broadcasted_iota(jnp.int32, (half, width), 0) + begin
            s = lax.broadcasted_iota(jnp.int32, (half, width), 1)
            gaps = r_col[begin : begin + half] - r_row[:, :width]
            return jnp.exp(jnp.where(t >= s, gaps, -1e30)) * s_row[:, :width]

        top = decays(0, half)
        bottom = decays(half, tokens)
        mix_top = (top * scores[:half, :half]).astype(bf16)
        mix_bottom = (bottom * scores[half:, :]).astype(bf16)
        ds_top = top * dot(dy[:half], x[:half], NT)
        ds_bottom = bottom * dot(dy[half:], x, NT)
        y = jnp.concatenate([dot(mix_top, x[:half]), dot(mix_bottom, x)], axis=0)
        dx = dot(mix_bottom, dy[half:], TN)
        dx = jnp.concatenate([dx[:half] + dot(mix_top, dy[:half], TN), dx[half:]], axis=0)

        state = state_in[h]
        grad = grad_in[h]
        from_start = jnp.exp(r_col)
        to_end = jnp.exp(r_end - r_col) * s_col
        y += from_start * dot(query_hl[...], jnp.concatenate([state, state], axis=0))
        carried = to_end * dot(key_hl[...], jnp.concatenate([grad, grad], axis=0))
        dx += carried
        dq_h = from_start * dot(dy, state, NT)
        dk_h = to_end * dot(x, grad, NT)
        xf = x.astype(f32)
        dyf = dy.astype(f32)
        y_out = (y + gain * xf).astype(bf16)
        dx_out = (dx + gain * dyf).astype(bf16)
        cross = xf * dx
        cross_h = jnp.sum(cross, axis=1, keepdims=True)
        diff_h = jnp.sum(dyf * y - cross, axis=1, keepdims=True)
        inner = jnp.sum(grad.astype(f32) * state.astype(f32), axis=0, keepdims=True)
        inner = jnp.sum(inner, axis=1, keepdims=True)
        outer = jnp.sum(jnp.sum(xf * carried, axis=0, keepdims=True), axis=1, keepdims=True)
        const_h = jnp.exp(r_end) * inner + outer
        return at_h, ds_top, ds_bottom, dq_h, dk_h, y_out, dx_out, cross_h, diff_h, const_h

    def keep_y(j):
        at = columns(j * CHUNK, CHUNK)
        return pltpu.make_async_copy(x_ref.at[:, at], y_hbm.at[:, at], store_y.at[j])

    def keep_dx(j):
        at = columns(j * CHUNK, CHUNK)
        return pltpu.make_async_copy(dy_ref.at[:, at], dx_hbm.at[:, at], store_dx.at[j])

    def compute(j):
        done = [one_head(j * CHUNK + u) for u in range(CHUNK)]
        ats, ds_tops, ds_bottoms, dqs, dks, ys, dxs, crosses, diffs, consts = zip(*done)
        dscores[:half, :half] += sum(ds_tops[1:], ds_tops[0])
        dscores[half:, :] += sum(ds_bottoms[1:], ds_bottoms[0])
        dq[...] += sum(dqs[1:], dqs[0])
        dk[...] += sum(dks[1:], dks[0])
        cross, diff, const = acc_cross[...], acc_diff[...], acc_const[...]
        for u in range(CHUNK):
            cross = jnp.where(ats[u], crosses[u], cross)
            diff = jnp.where(ats[u], diffs[u], diff)
            const = jnp.where(ats[u][:8], consts[u], const)
        acc_cross[...] = cross
        acc_diff[...] = diff
        acc_const[...] = const
        for u in range(CHUNK):
            x_ref[:, columns(j * CHUNK + u)] = ys[u]
            dy_ref[:, columns(j * CHUNK + u)] = dxs[u]
        keep_y(j).start()
        keep_dx(j).start()

    extra = LAG_FAR - LAG
    start_f = LAG * k + extra * (k // 4)
    start_b = LAG * (last - k) + extra * ((last - k) // 4)
    start_c = jnp.maximum(start_f, start_b)

    def iteration(i):
        jf = i - start_f
        jb = i - start_b
        jc = i - start_c

        @pl.when((jf >= 0) & (jf < chunks))
        def _():
            forward(jf)

        @pl.when((jb >= 0) & (jb < chunks))
        def _():
            backward(jb)

        @pl.when((jc >= 0) & (jc < chunks))
        def _():
            compute(jc)

    loop(chunks + LAG * last + extra, iteration)

    key = proj_ref[:, :NS]
    query = proj_ref[:, NS : 2 * NS] * NS ** (-0.5)
    pre = proj_ref[:, 2 * NS :] + head_ref[0:1, :]
    d_log = dot_high((columns_at >= rows).astype(f32), acc_diff[...]) + acc_const[0:1, :]
    slope = 1.0 / (1.0 + jnp.exp(-pre))
    ratio = jnp.where(pre < -20.0, 1.0, slope / step_c[...])
    dk_all = dk[...] + dot_high(dscores[...].T, query)
    dq_all = (dq[...] + dot_high(dscores[...], key)) * NS ** (-0.5)
    dz_all = acc_cross[...] * ratio - rate * d_log * slope
    g_mine = g_all.at[me.core]
    gt_mine = gt_all.at[me.core]
    for n, grads in enumerate((dk_all, dq_all, dz_all)):
        g_mine[:, n * NS : (n + 1) * NS] = grads.astype(bf16)
        gt_mine[n * NS : (n + 1) * NS, :] = grads.T.astype(bf16)
    give_t = remote(gt_mine, gt_mine, one_s.at[1], one_r.at[1], me.sibling())
    give_g = remote(g_mine, g_mine, one_s.at[2], one_r.at[2], me.sibling())
    give_t.start()
    give_g.start()
    pending += [give_t, give_g]
    give_t.wait_recv()

    def weight_grad(s):
        both = jnp.concatenate([gt_all[0, :cols], gt_all[1, :cols]], axis=1)
        p = dot(both, h_all[s].reshape(2 * tokens, depth))
        for b in range(4):
            for a in range(2):
                block = p[a * band : (a + 1) * band, b * lanes : (b + 1) * lanes]
                own[s // 4, lax.rem(s, 4), b, a] = block
                low[s // 4, lax.rem(s, 4), b, a] = block.astype(bf16)

    loop(8, weight_grad)
    slots = (
        (slot_a0, slot_b0, slot_c0), (slot_a1, slot_b1, slot_c1), (slot_a2, slot_b2, slot_c2)
    )
    current = sum_start(me, low, slots, st_s, st_r)
    give_g.wait_recv()

    def keep_hid(s):
        return pltpu.make_async_copy(
            hid.at[s, me.core], hid_hbm.at[:, me.columns(s, me.core, depth)], hid_l.at[s]
        )

    def give_hid(s):
        return remote(
            hid.at[s, 1 - me.core], hid_hbm.at[:, me.columns(s, me.core, depth)],
            hid_s.at[s], hid_r.at[s], me.sibling(),
        )

    def hidden(s):
        both = g_all[...].reshape(2 * tokens, 3 * NS)
        out = dot(both[:, :cols], weights(s)).astype(bf16)
        hid[s] = out.reshape(2, tokens, depth)
        keep_hid(s).start()
        give_hid(s).start()

    loop(8, hidden)
    pending += sum_finish(
        me, current, own, slots, (sum_a0, sum_a1, sum_a2), (low_a0, low_a1, low_a2),
        (sum_b0, sum_b1, sum_b2), final, gathered, gw_ref, st_s, st_r, ga_s, ga_r,
    )
    for copy in pending:
        copy.wait_send()

    def finish(s):
        lend(s).wait_send()
        keep_hid(s).wait()
        give_hid(s).wait_send()
        give_hid(s).wait_recv()

    loop(8, finish)

    def stored(j):
        keep_y(j).wait()
        keep_dx(j).wait()

    loop(chunks, stored)

    @pl.when(k < last)
    def _():
        loop(chunks, lambda j: copy_fwd(j).wait_send())

    @pl.when(k > 0)
    def _():
        loop(chunks, lambda j: copy_bwd(j).wait_send())


def layer(gain, head, weight_t, h, x, dy):
    tokens, width = x.shape
    heads = width // PS
    chunks = heads // CHUNK
    cols, depth = weight_t.shape
    half, lanes = cols // 2, depth // 4
    sizes = [size for _, size in bands(half)]
    vm = pl.BlockSpec(memory_space=pltpu.VMEM)
    hbm = pl.BlockSpec(memory_space=pl.ANY)
    states = pltpu.VMEM((heads, NS, PS), bf16)
    by_token = pltpu.VMEM((tokens, NS), f32)
    by_state = pltpu.VMEM((NS, tokens), f32)
    square = pltpu.VMEM((tokens, tokens), f32)
    two_parts = pltpu.VMEM((tokens, 2 * NS), bf16)

    def shape(left, color):
        dims = {"x_lo": 2, "z": 4, "y": 4, "x_hi": 2}
        return tuple(n for name, n in dims.items() if name[0] in left) + (sizes[color], lanes)

    def sem(n):
        return pltpu.SemaphoreType.DMA((n,))

    everyone = range(BANDS)
    one = [shape(ORDER_SUM[c][1:], c) for c in everyone]
    two = [shape(ORDER_SUM[c][2:], c) for c in everyone]
    end = [shape("", c) for c in everyone]
    whole = (2, 4, 4, 2, half, lanes)
    return pl.pallas_call(
        partial(layer_kernel, heads),
        out_shape=(
            jax.ShapeDtypeStruct(x.shape, bf16),
            jax.ShapeDtypeStruct(x.shape, bf16),
            jax.ShapeDtypeStruct(h.shape, bf16),
            jax.ShapeDtypeStruct((cols, depth), f32),
        ),
        in_specs=[pl.BlockSpec(memory_space=pltpu.SMEM), vm, vm, hbm, hbm, hbm],
        out_specs=(hbm, hbm, hbm, vm),
        scratch_shapes=[
            pltpu.VMEM((8, 2, tokens, depth), bf16),
            pltpu.VMEM(whole, bf16),
            pltpu.VMEM(x.shape, bf16),
            pltpu.VMEM(x.shape, bf16),
            pltpu.VMEM((2 * tokens, 3 * NS), f32),
            pltpu.VMEM((tokens, 3 * NS), f32),
            pltpu.VMEM((tokens, 3 * NS), f32),
            by_token, by_state, by_state, by_token, by_state, by_state,
            two_parts, two_parts, square,
            by_token, by_token, pltpu.VMEM((8, NS), f32), by_token, by_token, square,
            states, states, states, states,
            pltpu.VMEM((2, tokens, 3 * NS), bf16),
            pltpu.VMEM((2, 3 * NS, tokens), bf16),
            pltpu.VMEM(whole, f32),
            pltpu.VMEM(whole, bf16),
        ]
        + [pltpu.VMEM((3,) + s, bf16) for s in one]
        + [pltpu.VMEM(s, f32) for s in one]
        + [pltpu.VMEM(s, bf16) for s in one]
        + [pltpu.VMEM((3,) + s, bf16) for s in two]
        + [pltpu.VMEM(s, f32) for s in two]
        + [pltpu.VMEM((3,) + s, f32) for s in end]
        + [
            pltpu.VMEM((half, lanes), f32),
            pltpu.VMEM((2, 4, half, lanes), f32),
            pltpu.VMEM((8, 2, tokens, depth), bf16),
            sem(8), sem(2), sem(8), sem(8), sem(27), sem(27), sem(3), sem(3),
            sem(chunks), sem(chunks), sem(chunks), sem(chunks), sem(chunks), sem(chunks),
            sem(27), sem(27), sem(21), sem(21), sem(8), sem(8), sem(8),
        ],
        compiler_params=pltpu.CompilerParams(
            collective_id=0, has_side_effects=True, vmem_limit_bytes=58 * 2**20
        ),
    )(gain, head, weight_t, h, x, dy)


def shards(hidden_rows, inner_rows, weight_proj, decay_log, step_bias, skip_gain, grad_output):
    token_rows = hidden_rows.reshape(-1, hidden_rows.shape[-1])
    value_rows = inner_rows.reshape(-1, inner_rows.shape[-1])
    cotangent = grad_output.reshape(value_rows.shape)
    heads = decay_log.shape[0]
    head = jnp.pad(jnp.stack([step_bias, decay_log]), ((0, 6), (0, NS - heads)))
    output, grad_values, grad_tokens, grad_weight_t = layer(
        skip_gain, head, weight_proj.T, token_rows, value_rows, cotangent
    )
    return (
        output.reshape(inner_rows.shape),
        grad_values.reshape(inner_rows.shape),
        grad_tokens.reshape(hidden_rows.shape),
        grad_weight_t.T,
    )


def solution(mesh):
    rows = P("dp", "ctx", None)
    return jax.shard_map(
        shards,
        mesh=mesh,
        in_specs=(rows, rows, P("dp", None), P(), P(), P(), rows),
        out_specs=(rows, rows, rows, P("dp", None)),
        check_vma=False,
    )
```

```python
from functools import partial

import jax
import jax.numpy as jnp
from jax import lax
from jax.experimental import pallas as pl
from jax.experimental.pallas import tpu as pltpu
from jax.sharding import PartitionSpec as P

PS = 128
NS = 128
CHUNK = 2
LAG = 2
LAG_FAR = 4
MESH = pl.DeviceIdType.MESH
highest = lax.Precision.HIGHEST
f32 = jnp.float32
bf16 = jnp.bfloat16
NN = (((1,), (0,)), ((), ()))
NT = (((1,), (1,)), ((), ()))
TN = (((0,), (0,)), ((), ()))


def dot(a, b, dims=NN):
    return lax.dot_general(a, b, dims, preferred_element_type=f32)


def dot_high(a, b, dims=NN):
    return lax.dot_general(a, b, dims, preferred_element_type=f32, precision=highest)


def split(a):
    high = a.astype(bf16)
    return high, (a - high.astype(f32)).astype(bf16)

BANDS = 3
ORDER_SUM = ("zyx", "yxz", "xzy")
ORDER_GATHER = ("xyz", "zxy", "yzx")


def bands(half):
    third = half // 3 // 16 * 16
    return ((0, third), (third, third), (2 * third, half - 2 * third))


def remote(src, dst, send, recv, device):
    return pltpu.make_async_remote_copy(
        src_ref=src, dst_ref=dst, send_sem=send, recv_sem=recv,
        device_id=device, device_id_type=MESH,
    )


class Place:
    def __init__(self):
        dp, ctx = lax.axis_index("dp"), lax.axis_index("ctx")
        self.x_lo, self.z, self.core = dp // 8, lax.rem(dp // 2, 4), lax.rem(dp, 2)
        self.x_hi, self.y = ctx // 4, lax.rem(ctx, 4)
        self.x = self.x_hi * 2 + self.x_lo
        self.ctx = ctx

    def device(self, **other):
        at = {name: getattr(self, name) for name in ("x_lo", "z", "core", "x_hi", "y")}
        at.update(other)
        return {
            "dp": at["x_lo"] * 8 + at["z"] * 2 + at["core"],
            "ctx": at["x_hi"] * 4 + at["y"],
        }

    def along(self, axis, d):
        to = lax.rem(getattr(self, axis) + d, 4)
        return {"x_lo": lax.rem(to, 2), "x_hi": to // 2} if axis == "x" else {axis: to}

    def ring(self, axis, d):
        return self.device(**self.along(axis, d))

    def sibling(self):
        return self.device(core=1 - self.core)

    def piece(self, a, b):
        return self.device(x_hi=lax.rem(self.x_hi + a, 2), y=lax.rem(self.y + b, 4))

    def columns(self, s, side, depth):
        at = (s // 4) * 8 + lax.rem(s, 4) * 2 + side
        return pl.ds(pl.multiple_of(at * depth, depth), depth)


OTHERS = [(a, b) for a in range(2) for b in range(4) if a + b]


def loop(count, body):
    def step(i, carry):
        body(i)
        return carry

    lax.fori_loop(0, count, step, 0)


def gather_weights(me, w_ref, all_ref, send, recv):
    cols, depth = w_ref.shape
    half = cols // 2
    whole = slice(None)

    def region(color, have):
        off, size = bands(half)[color]
        return all_ref.at[
            whole if "x" in have else me.x_lo,
            whole if "z" in have else me.z,
            whole if "y" in have else me.y,
            whole if "x" in have else me.x_hi,
            pl.ds(off, size),
        ]

    def exchange(color, stage):
        axis = ORDER_GATHER[color][stage]
        part = region(color, ORDER_GATHER[color][:stage])
        copies = []
        for d in (1, 3, 2):
            n = color * 9 + stage * 3 + d - 1
            copies.append(remote(part, part, send.at[n], recv.at[n], me.ring(axis, d)))
            copies[-1].start()
        return copies

    pending = []
    current = [exchange(color, 0) for color in range(BANDS)]
    for stage in (1, 2, 3):
        for color in range(BANDS):
            for copy in current[color]:
                copy.wait_recv()
            pending += current[color]
            if stage < 3:
                current[color] = exchange(color, stage)
    return pending


def sum_start(me, low, slots, send, recv):
    return [sum_exchange(me, color, 0, low, "xzy", slots, send, recv) for color in range(BANDS)]


def pick(left, axis, place):
    at = []
    for name in ("x_lo", "z", "y", "x_hi"):
        if name[0] in left:
            at.append(place[name] if name[0] == axis else slice(None))
    return tuple(at)


def sum_exchange(me, color, stage, source, left, slots, send, recv):
    axis = ORDER_SUM[color][stage]
    off, size = bands(slots[0][2].shape[1] + slots[1][2].shape[1] + slots[2][2].shape[1])[color]
    window = (pl.ds(off, size),) if stage == 0 else ()
    copies = []
    for d in (1, 3, 2):
        n = color * 9 + stage * 3 + d - 1
        part = source.at[pick(left, axis, me.along(axis, d)) + window]
        copies.append(
            remote(part, slots[color][stage].at[d - 1], send.at[n], recv.at[n], me.ring(axis, d))
        )
        copies[-1].start()
    return copies


def sum_finish(me, current, own, slots, sums, lows, finals, final, gathered, out_ref, send, recv, ga_s, ga_r):
    half = final.shape[0]
    lanes = final.shape[1]
    pending = []

    def arrived(color, stage, source, left, window=()):
        axis = ORDER_SUM[color][stage]
        pending.extend(current[color])
        for copy in current[color]:
            copy.wait_recv()
        total = source[pick(left, axis, me.along(axis, 0)) + window]
        for d in range(3):
            total += slots[color][stage][d].astype(f32)
        return total

    for color in range(BANDS):
        off, size = bands(half)[color]
        total = arrived(color, 0, own, "xzy", (pl.ds(off, size),))
        sums[color][...] = total
        lows[color][...] = total.astype(bf16)
        left = ORDER_SUM[color][1:]
        current[color] = sum_exchange(me, color, 1, lows[color], left, slots, send, recv)
    for color in range(BANDS):
        finals[color][...] = arrived(color, 1, sums[color], ORDER_SUM[color][1:])
        left = ORDER_SUM[color][2:]
        current[color] = sum_exchange(me, color, 2, finals[color], left, slots, send, recv)
    gathers = []
    for color in range(BANDS):
        off, size = bands(half)[color]
        total = arrived(color, 2, finals[color], ORDER_SUM[color][2:])
        final[pl.ds(off, size)] = total.astype(bf16)
        for m, (a, b) in enumerate(OTHERS):
            n = color * 7 + m
            gathers.append(
                remote(
                    final.at[pl.ds(off, size)], gathered.at[me.x_hi, me.y, pl.ds(off, size)],
                    ga_s.at[n], ga_r.at[n], me.piece(a, b),
                )
            )
            gathers[-1].start()
    for copy in gathers:
        copy.wait_recv()
    for a in range(2):
        for b in range(4):
            mine = (me.x_hi == a) & (me.y == b)
            part = jnp.where(mine, final[...].astype(f32), gathered[a, b].astype(f32))
            out_ref[a * half : (a + 1) * half, b * lanes : (b + 1) * lanes] = part
    return pending + gathers


def layer_kernel(
    heads, gain_ref, decay_ref, bias_ref, w_ref, h_ref, x_hbm, dy_hbm,
    x_ref, dy_ref, hid_ref, gw_ref,
    h_all, w_all, part, proj_in, proj_ref,
    run, run_t, step_t, step_c, key_t, query_t, key_hl, query_hl, scores,
    acc_diff, acc_cross, acc_const, dq, dk, dscores,
    state_in, state_out, grad_in, grad_out, state_own, grad_own,
    g_all, gt_all, own, low,
    slot_a0, slot_a1, slot_a2, sum_a0, sum_a1, sum_a2, low_a0, low_a1, low_a2,
    slot_b0, slot_b1, slot_b2, sum_b0, sum_b1, sum_b2,
    slot_c0, slot_c1, slot_c2, final, gathered, hid,
    load_h, load_xy, hs, hr, ag_s, ag_r, one_s, one_r, sf, rf, sb, rb,
    st_s, st_r, ga_s, ga_r, hid_s, hid_r,
):
    me = Place()
    k = me.ctx
    pieces = lax.axis_size("ctx")
    last = pieces - 1
    tokens = proj_ref.shape[0]
    half = tokens // 2
    chunks = heads // CHUNK
    cols, depth = w_ref.shape
    band, lanes = cols // 2, depth // 4
    right = {"ctx": lax.rem(k + 1, pieces)}
    left = {"ctx": lax.rem(k + pieces - 1, pieces)}

    def widened(ref):
        return jnp.concatenate([ref[...], jnp.zeros((1, NS - heads), f32)], axis=1)

    barrier = pltpu.get_barrier_semaphore()
    peers = [me.sibling()]
    peers += [me.ring("z", d) for d in (1, 2, 3)]
    peers += [me.ring("x", d) for d in (1, 3)]
    peers += [me.piece(a, b) for a, b in OTHERS]
    for peer in peers:
        pl.semaphore_signal(barrier, inc=1, device_id=peer, device_id_type=MESH)

    def load(s):
        return pltpu.make_async_copy(
            h_ref.at[:, me.columns(s, me.core, depth)], h_all.at[s, me.core], load_h.at[s]
        )

    def lend(s):
        return remote(
            h_ref.at[:, me.columns(s, 1 - me.core, depth)], h_all.at[s, me.core],
            hs.at[s], hr.at[s], me.sibling(),
        )

    loop(8, lambda s: load(s).start())
    load_x = pltpu.make_async_copy(x_hbm, x_ref, load_xy.at[0])
    load_dy = pltpu.make_async_copy(dy_hbm, dy_ref, load_xy.at[1])
    for a in range(2):
        for b in range(4):
            @pl.when((me.x_hi == a) & (me.y == b))
            def _():
                w_all[me.x_lo, me.z, b, a] = w_ref[
                    a * band : (a + 1) * band, b * lanes : (b + 1) * lanes
                ]
    part[...] = jnp.zeros_like(part)
    pl.semaphore_wait(barrier, len(peers))
    loop(8, lambda s: lend(s).start())
    load_x.start()
    load_dy.start()

    @pl.when(k == 0)
    def _():
        state_in[...] = jnp.zeros_like(state_in)

    @pl.when(k == last)
    def _():
        grad_in[...] = jnp.zeros_like(grad_in)

    dq[...] = jnp.zeros_like(dq)
    dk[...] = jnp.zeros_like(dk)
    dscores[...] = jnp.zeros_like(dscores)
    acc_diff[...] = jnp.zeros_like(acc_diff)
    acc_cross[...] = jnp.zeros_like(acc_cross)
    acc_const[...] = jnp.zeros_like(acc_const)

    pending = gather_weights(me, w_ref, w_all, ag_s, ag_r)

    def weights(s):
        parts = [w_all[s // 4, lax.rem(s, 4), b].reshape(cols, lanes) for b in range(4)]
        return jnp.concatenate(parts, axis=1)

    def project(s):
        load(s).wait()
        lend(s).wait_recv()
        part[:, :cols] += dot(h_all[s].reshape(2 * tokens, depth), weights(s), NT)

    loop(8, project)
    mine = pl.ds(pl.multiple_of(me.core * tokens, tokens), tokens)
    theirs = pl.ds(pl.multiple_of((1 - me.core) * tokens, tokens), tokens)
    give = remote(part.at[theirs], proj_in, one_s.at[0], one_r.at[0], me.sibling())
    give.start()
    give.wait_recv()
    pending.append(give)
    proj_ref[...] = part[mine] + proj_in[...]

    rows = lax.broadcasted_iota(jnp.int32, (tokens, tokens), 0)
    columns_at = lax.broadcasted_iota(jnp.int32, (tokens, tokens), 1)
    key = proj_ref[:, :NS]
    query = proj_ref[:, NS : 2 * NS] * NS ** (-0.5)
    pre = proj_ref[:, 2 * NS :] + widened(bias_ref)
    rate = jnp.exp(widened(decay_ref))
    steps = jnp.maximum(pre, 0.0) + jnp.log1p(jnp.exp(-jnp.abs(pre)))
    running = dot_high((rows >= columns_at).astype(f32), -rate * steps)
    run[...] = running
    run_t[...] = running.T
    step_c[...] = steps
    step_t[...] = steps.T
    key_t[...] = key.T
    query_t[...] = query.T
    high, low_part = split(key)
    key_hl[:, :NS] = high
    key_hl[:, NS:] = low_part
    high, low_part = split(query)
    query_hl[:, :NS] = high
    query_hl[:, NS:] = low_part
    scores[...] = dot_high(query, key, NT)
    load_x.wait()
    load_dy.wait()

    def copy_fwd(h):
        return remote(state_out.at[h], state_in.at[h], sf.at[h], rf.at[h], right)

    def copy_bwd(h):
        return remote(grad_out.at[h], grad_in.at[h], sb.at[h], rb.at[h], left)

    def columns(h, count=1):
        return pl.ds(pl.multiple_of(h * PS, PS), count * PS)

    def prepare(j):
        made = []
        for u in range(CHUNK):
            h = j * CHUNK + u
            r_row = run_t[pl.ds(h, 1), :]
            r_end = r_row[:, tokens - 1 : tokens]
            high, low_part = split(key_t[...] * (jnp.exp(r_end - r_row) * step_t[pl.ds(h, 1), :]))
            x = x_ref[:, columns(h)]
            state = dot(high, x) + dot(low_part, x)
            high, low_part = split(query_t[...] * jnp.exp(r_row))
            dy = dy_ref[:, columns(h)]
            made.append((h, state, dot(high, dy) + dot(low_part, dy)))
        for h, state, grad in made:
            state_own[h] = state
            grad_own[h] = grad

    def decay_of(h):
        return jnp.exp(run_t[pl.ds(h, 1), :][:, tokens - 1 : tokens])

    def forward(j):
        for u in range(CHUNK):
            h = j * CHUNK + u

            @pl.when(k > 0)
            def _():
                copy_fwd(h).wait_recv()

            @pl.when(k < last)
            def _():
                carried = decay_of(h) * state_in[h].astype(f32)
                state_out[h] = (carried + state_own[h]).astype(bf16)
                copy_fwd(h).start()

    def backward(j):
        for u in range(CHUNK):
            h = j * CHUNK + u

            @pl.when(k < last)
            def _():
                copy_bwd(h).wait_recv()

            @pl.when(k > 0)
            def _():
                carried = decay_of(h) * grad_in[h].astype(f32)
                grad_out[h] = (carried + grad_own[h]).astype(bf16)
                copy_bwd(h).start()

    def one_head(h):
        lane = lax.broadcasted_iota(jnp.int32, (tokens, NS), 1)
        at_h = lane == h
        r_col = jnp.sum(jnp.where(at_h, run[...], 0.0), axis=1, keepdims=True)
        s_col = jnp.sum(jnp.where(at_h, step_c[...], 0.0), axis=1, keepdims=True)
        r_row = run_t[pl.ds(h, 1), :]
        s_row = step_t[pl.ds(h, 1), :]
        r_end = r_row[:, tokens - 1 : tokens]
        x = x_ref[:, columns(h)]
        dy = dy_ref[:, columns(h)]
        gain = gain_ref[h]

        def decays(begin, width):
            t = lax.broadcasted_iota(jnp.int32, (half, width), 0) + begin
            s = lax.broadcasted_iota(jnp.int32, (half, width), 1)
            gaps = r_col[begin : begin + half] - r_row[:, :width]
            return jnp.exp(jnp.where(t >= s, gaps, -1e30)) * s_row[:, :width]

        top = decays(0, half)
        bottom = decays(half, tokens)
        mix_top = (top * scores[:half, :half]).astype(bf16)
        mix_bottom = (bottom * scores[half:, :]).astype(bf16)
        ds_top = top * dot(dy[:half], x[:half], NT)
        ds_bottom = bottom * dot(dy[half:], x, NT)
        y = jnp.concatenate([dot(mix_top, x[:half]), dot(mix_bottom, x)], axis=0)
        dx = dot(mix_bottom, dy[half:], TN)
        dx = jnp.concatenate([dx[:half] + dot(mix_top, dy[:half], TN), dx[half:]], axis=0)

        state = state_in[h]
        grad = grad_in[h]
        from_start = jnp.exp(r_col)
        to_end = jnp.exp(r_end - r_col) * s_col
        y += from_start * dot(query_hl[...], jnp.concatenate([state, state], axis=0))
        carried = to_end * dot(key_hl[...], jnp.concatenate([grad, grad], axis=0))
        dx += carried
        dq_h = from_start * dot(dy, state, NT)
        dk_h = to_end * dot(x, grad, NT)
        xf = x.astype(f32)
        dyf = dy.astype(f32)
        y_out = (y + gain * xf).astype(bf16)
        dx_out = (dx + gain * dyf).astype(bf16)
        cross = xf * dx
        cross_h = jnp.sum(cross, axis=1, keepdims=True)
        diff_h = jnp.sum(dyf * y - cross, axis=1, keepdims=True)
        inner = jnp.sum(grad.astype(f32) * state.astype(f32), axis=0, keepdims=True)
        inner = jnp.sum(inner, axis=1, keepdims=True)
        outer = jnp.sum(jnp.sum(xf * carried, axis=0, keepdims=True), axis=1, keepdims=True)
        const_h = jnp.exp(r_end) * inner + outer
        return at_h, ds_top, ds_bottom, dq_h, dk_h, y_out, dx_out, cross_h, diff_h, const_h

    def compute(j):
        done = [one_head(j * CHUNK + u) for u in range(CHUNK)]
        ats, ds_tops, ds_bottoms, dqs, dks, ys, dxs, crosses, diffs, consts = zip(*done)
        dscores[:half, :half] += sum(ds_tops[1:], ds_tops[0])
        dscores[half:, :] += sum(ds_bottoms[1:], ds_bottoms[0])
        dq[...] += sum(dqs[1:], dqs[0])
        dk[...] += sum(dks[1:], dks[0])
        cross, diff, const = acc_cross[...], acc_diff[...], acc_const[...]
        for u in range(CHUNK):
            cross = jnp.where(ats[u], crosses[u], cross)
            diff = jnp.where(ats[u], diffs[u], diff)
            const = jnp.where(ats[u][:8], consts[u], const)
        acc_cross[...] = cross
        acc_diff[...] = diff
        acc_const[...] = const
        for u in range(CHUNK):
            x_ref[:, columns(j * CHUNK + u)] = ys[u]
            dy_ref[:, columns(j * CHUNK + u)] = dxs[u]

    extra = LAG_FAR - LAG
    start_f = LAG * k + extra * (k // 4)
    start_b = LAG * (last - k) + extra * ((last - k) // 4)
    start_c = jnp.maximum(start_f, start_b)

    def iteration(i):
        jf = i - start_f
        jb = i - start_b
        jc = i - start_c

        @pl.when(i < chunks)
        def _():
            prepare(i)

        @pl.when((jf >= 0) & (jf < chunks))
        def _():
            forward(jf)

        @pl.when((jb >= 0) & (jb < chunks))
        def _():
            backward(jb)

        @pl.when((jc >= 0) & (jc < chunks))
        def _():
            compute(jc)

    loop(chunks + LAG * last + extra, iteration)

    key = proj_ref[:, :NS]
    query = proj_ref[:, NS : 2 * NS] * NS ** (-0.5)
    pre = proj_ref[:, 2 * NS :] + widened(bias_ref)
    d_log = dot_high((columns_at >= rows).astype(f32), acc_diff[...]) + acc_const[0:1, :]
    slope = 1.0 / (1.0 + jnp.exp(-pre))
    ratio = jnp.where(pre < -20.0, 1.0, slope / step_c[...])
    dk_all = dk[...] + dot_high(dscores[...].T, query)
    dq_all = (dq[...] + dot_high(dscores[...], key)) * NS ** (-0.5)
    dz_all = acc_cross[...] * ratio - rate * d_log * slope
    g_mine = g_all.at[me.core]
    gt_mine = gt_all.at[me.core]
    for n, grads in enumerate((dk_all, dq_all, dz_all)):
        g_mine[:, n * NS : (n + 1) * NS] = grads.astype(bf16)
        gt_mine[n * NS : (n + 1) * NS, :] = grads.T.astype(bf16)
    give_t = remote(gt_mine, gt_mine, one_s.at[1], one_r.at[1], me.sibling())
    give_g = remote(g_mine, g_mine, one_s.at[2], one_r.at[2], me.sibling())
    give_t.start()
    give_g.start()
    pending += [give_t, give_g]

    def weight_grad(s, side, more):
        p = dot(gt_all[side, :cols], h_all[s, side])
        for b in range(4):
            for a in range(2):
                at = (s // 4, lax.rem(s, 4), b, a)
                block = p[a * band : (a + 1) * band, b * lanes : (b + 1) * lanes]
                if more:
                    block += own[at]
                    low[at] = block.astype(bf16)
                own[at] = block

    loop(8, lambda s: weight_grad(s, me.core, False))
    give_t.wait_recv()
    loop(8, lambda s: weight_grad(s, 1 - me.core, True))
    slots = (
        (slot_a0, slot_b0, slot_c0), (slot_a1, slot_b1, slot_c1), (slot_a2, slot_b2, slot_c2)
    )
    current = sum_start(me, low, slots, st_s, st_r)
    give_g.wait_recv()

    def give_hid(s):
        return remote(
            hid.at[s], hid_ref.at[:, me.columns(s, me.core, depth)],
            hid_s.at[s], hid_r.at[s], me.sibling(),
        )

    def hidden(s):
        theirs = g_all[1 - me.core]
        hid[s] = dot(theirs[:, :cols], weights(s)).astype(bf16)
        give_hid(s).start()
        hid_ref[:, me.columns(s, me.core, depth)] = dot(
            g_all[me.core, :, :cols], weights(s)
        ).astype(bf16)

    loop(8, hidden)
    pending += sum_finish(
        me, current, own, slots, (sum_a0, sum_a1, sum_a2), (low_a0, low_a1, low_a2),
        (sum_b0, sum_b1, sum_b2), final, gathered, gw_ref, st_s, st_r, ga_s, ga_r,
    )
    for copy in pending:
        copy.wait_send()

    def finish(s):
        lend(s).wait_send()
        give_hid(s).wait_send()
        give_hid(s).wait_recv()

    loop(8, finish)

    @pl.when(k < last)
    def _():
        loop(heads, lambda h: copy_fwd(h).wait_send())

    @pl.when(k > 0)
    def _():
        loop(heads, lambda h: copy_bwd(h).wait_send())


def layer(gain, decay, bias, weight_t, h, x, dy):
    tokens, width = x.shape
    heads = width // PS
    chunks = heads // CHUNK
    cols, depth = weight_t.shape
    half, lanes = cols // 2, depth // 4
    sizes = [size for _, size in bands(half)]
    vm = pl.BlockSpec(memory_space=pltpu.VMEM)
    hbm = pl.BlockSpec(memory_space=pl.ANY)
    states = pltpu.VMEM((heads, NS, PS), bf16)
    own_states = pltpu.VMEM((heads, NS, PS), f32)
    by_token = pltpu.VMEM((tokens, NS), f32)
    by_state = pltpu.VMEM((NS, tokens), f32)
    square = pltpu.VMEM((tokens, tokens), f32)
    two_parts = pltpu.VMEM((tokens, 2 * NS), bf16)

    def shape(left, color):
        dims = {"x_lo": 2, "z": 4, "y": 4, "x_hi": 2}
        return tuple(n for name, n in dims.items() if name[0] in left) + (sizes[color], lanes)

    def sem(n):
        return pltpu.SemaphoreType.DMA((n,))

    everyone = range(BANDS)
    one = [shape(ORDER_SUM[c][1:], c) for c in everyone]
    two = [shape(ORDER_SUM[c][2:], c) for c in everyone]
    end = [shape("", c) for c in everyone]
    whole = (2, 4, 4, 2, half, lanes)
    return pl.pallas_call(
        partial(layer_kernel, heads),
        out_shape=(
            pltpu.VMEM(x.shape, bf16),
            pltpu.VMEM(x.shape, bf16),
            pltpu.VMEM(h.shape, bf16),
            pltpu.VMEM((cols, depth), f32),
        ),
        in_specs=[pl.BlockSpec(memory_space=pltpu.SMEM), vm, vm, vm, hbm, hbm, hbm],
        out_specs=(vm, vm, vm, vm),
        scratch_shapes=[
            pltpu.VMEM((8, 2, tokens, depth), bf16),
            pltpu.VMEM(whole, bf16),
            pltpu.VMEM((2 * tokens, 3 * NS), f32),
            pltpu.VMEM((tokens, 3 * NS), f32),
            pltpu.VMEM((tokens, 3 * NS), f32),
            by_token, by_state, by_state, by_token, by_state, by_state,
            two_parts, two_parts, square,
            by_token, by_token, pltpu.VMEM((8, NS), f32), by_token, by_token, square,
            states, states, states, states, own_states, own_states,
            pltpu.VMEM((2, tokens, 3 * NS), bf16),
            pltpu.VMEM((2, 3 * NS, tokens), bf16),
            pltpu.VMEM(whole, f32),
            pltpu.VMEM(whole, bf16),
        ]
        + [pltpu.VMEM((3,) + s, bf16) for s in one]
        + [pltpu.VMEM(s, f32) for s in one]
        + [pltpu.VMEM(s, bf16) for s in one]
        + [pltpu.VMEM((3,) + s, bf16) for s in two]
        + [pltpu.VMEM(s, f32) for s in two]
        + [pltpu.VMEM((3,) + s, f32) for s in end]
        + [
            pltpu.VMEM((half, lanes), bf16),
            pltpu.VMEM((2, 4, half, lanes), bf16),
            pltpu.VMEM((8, tokens, depth), bf16),
            sem(8), sem(2), sem(8), sem(8), sem(27), sem(27), sem(3), sem(3),
            sem(heads), sem(heads), sem(heads), sem(heads),
            sem(27), sem(27), sem(21), sem(21), sem(8), sem(8),
        ],
        compiler_params=pltpu.CompilerParams(
            collective_id=0, has_side_effects=True, vmem_limit_bytes=46 * 2**20
        ),
    )(gain, decay, bias, weight_t, h, x, dy)


def store_kernel(*refs):
    sems = refs[8]
    copies = []
    for source, target in zip(refs[:4], refs[4:8]):
        rows = source.shape[0] // 2
        for part in range(2):
            at = pl.ds(part * rows, rows)
            copies.append(
                pltpu.make_async_copy(source.at[at], target.at[at], sems.at[len(copies)])
            )
            copies[-1].start()
    for copy in copies:
        copy.wait()


def store(*arrays):
    hbm = pl.BlockSpec(memory_space=pl.ANY)
    vm = pl.BlockSpec(memory_space=pltpu.VMEM)
    return pl.pallas_call(
        store_kernel,
        out_shape=tuple(jax.ShapeDtypeStruct(a.shape, a.dtype) for a in arrays),
        in_specs=[vm] * 4,
        out_specs=(hbm,) * 4,
        scratch_shapes=[pltpu.SemaphoreType.DMA((8,))],
        compiler_params=pltpu.CompilerParams(vmem_limit_bytes=16 * 2**20),
    )(*arrays)


def shards(hidden_rows, inner_rows, weight_proj, decay_log, step_bias, skip_gain, grad_output):
    token_rows = hidden_rows.reshape(-1, hidden_rows.shape[-1])
    value_rows = inner_rows.reshape(-1, inner_rows.shape[-1])
    cotangent = grad_output.reshape(value_rows.shape)
    output, grad_values, grad_tokens, grad_weight_t = layer(
        skip_gain, decay_log[None], step_bias[None], weight_proj.T, token_rows, value_rows, cotangent
    )
    output, grad_values, grad_tokens, grad_weight_t = store(
        output, grad_values, grad_tokens, grad_weight_t
    )
    return (
        output.reshape(inner_rows.shape),
        grad_values.reshape(inner_rows.shape),
        grad_tokens.reshape(hidden_rows.shape),
        grad_weight_t.T,
    )


def solution(mesh):
    rows = P("dp", "ctx", None)
    return jax.shard_map(
        shards,
        mesh=mesh,
        in_specs=(rows, rows, P("dp", None), P(), P(), P(), rows),
        out_specs=(rows, rows, rows, P("dp", None)),
        check_vma=False,
    )
```

```python
from functools import partial

import jax
import jax.numpy as jnp
from jax import lax
from jax.experimental import pallas as pl
from jax.experimental.pallas import tpu as pltpu
from jax.sharding import PartitionSpec as P

PS = 128
NS = 128
CHUNK = 2
LAG = 3
LAG_FAR = 5
MESH = pl.DeviceIdType.MESH
highest = lax.Precision.HIGHEST
f32 = jnp.float32
bf16 = jnp.bfloat16
NN = (((1,), (0,)), ((), ()))
NT = (((1,), (1,)), ((), ()))
TN = (((0,), (0,)), ((), ()))


def dot(a, b, dims=NN):
    return lax.dot_general(a, b, dims, preferred_element_type=f32)


def dot_high(a, b, dims=NN):
    return lax.dot_general(a, b, dims, preferred_element_type=f32, precision=highest)


def split(a):
    high = a.astype(bf16)
    return high, (a - high.astype(f32)).astype(bf16)

BANDS = 3
ORDER_SUM = ("zyx", "yxz", "xzy")
ORDER_GATHER = ("xyz", "zxy", "yzx")


def bands(half):
    third = half // 3 // 16 * 16
    first = half - 2 * third
    return ((0, first), (first, third), (first + third, third))


def remote(src, dst, send, recv, device):
    return pltpu.make_async_remote_copy(
        src_ref=src, dst_ref=dst, send_sem=send, recv_sem=recv,
        device_id=device, device_id_type=MESH,
    )


class Place:
    def __init__(self):
        dp, ctx = lax.axis_index("dp"), lax.axis_index("ctx")
        self.x_lo, self.z, self.core = dp // 8, lax.rem(dp // 2, 4), lax.rem(dp, 2)
        self.x_hi, self.y = ctx // 4, lax.rem(ctx, 4)
        self.x = self.x_hi * 2 + self.x_lo
        self.ctx = ctx

    def device(self, **other):
        at = {name: getattr(self, name) for name in ("x_lo", "z", "core", "x_hi", "y")}
        at.update(other)
        return {
            "dp": at["x_lo"] * 8 + at["z"] * 2 + at["core"],
            "ctx": at["x_hi"] * 4 + at["y"],
        }

    def along(self, axis, d):
        to = lax.rem(getattr(self, axis) + d, 4)
        return {"x_lo": lax.rem(to, 2), "x_hi": to // 2} if axis == "x" else {axis: to}

    def ring(self, axis, d):
        return self.device(**self.along(axis, d))

    def sibling(self):
        return self.device(core=1 - self.core)

    def piece(self, a, b):
        return self.device(x_hi=lax.rem(self.x_hi + a, 2), y=lax.rem(self.y + b, 4))

    def columns(self, s, side, depth):
        at = (s // 4) * 8 + lax.rem(s, 4) * 2 + side
        return pl.ds(pl.multiple_of(at * depth, depth), depth)


OTHERS = [(a, b) for a in range(2) for b in range(4) if a + b]


def loop(count, body):
    def step(i, carry):
        body(i)
        return carry

    lax.fori_loop(0, count, step, 0)


def gather_weights(me, w_ref, all_ref, send, recv):
    cols, depth = w_ref.shape
    half = cols // 2
    whole = slice(None)

    def region(color, have):
        off, size = bands(half)[color]
        return all_ref.at[
            whole if "x" in have else me.x_lo,
            whole if "z" in have else me.z,
            whole if "y" in have else me.y,
            whole if "x" in have else me.x_hi,
            pl.ds(off, size),
        ]

    def exchange(color, stage):
        axis = ORDER_GATHER[color][stage]
        part = region(color, ORDER_GATHER[color][:stage])
        copies = []
        for d in (2, 1, 3):
            n = color * 9 + stage * 3 + d - 1
            copies.append(remote(part, part, send.at[n], recv.at[n], me.ring(axis, d)))
            copies[-1].start()
        return copies

    pending = []
    current = [exchange(color, 0) for color in range(BANDS)]
    for stage in (1, 2, 3):
        for color in range(BANDS):
            for copy in current[color]:
                copy.wait_recv()
            pending += current[color]
            if stage < 3:
                current[color] = exchange(color, stage)
    return pending


def sum_start(me, low, slots, send, recv):
    return [sum_exchange(me, color, 0, low, "xzy", slots, send, recv) for color in range(BANDS)]


def pick(left, axis, place):
    at = []
    for name in ("x_lo", "z", "y", "x_hi"):
        if name[0] in left:
            at.append(place[name] if name[0] == axis else slice(None))
    return tuple(at)


def sum_exchange(me, color, stage, source, left, slots, send, recv):
    axis = ORDER_SUM[color][stage]
    off, size = bands(slots[0][2].shape[1] + slots[1][2].shape[1] + slots[2][2].shape[1])[color]
    window = (pl.ds(off, size),) if stage == 0 else ()
    copies = []
    for d in (2, 1, 3):
        n = color * 9 + stage * 3 + d - 1
        part = source.at[pick(left, axis, me.along(axis, d)) + window]
        copies.append(
            remote(part, slots[color][stage].at[d - 1], send.at[n], recv.at[n], me.ring(axis, d))
        )
        copies[-1].start()
    return copies


def sum_finish(me, current, own, slots, sums, lows, finals, final, gathered, out_ref, send, recv, ga_s, ga_r):
    half = final.shape[0]
    lanes = final.shape[1]
    pending = []

    def arrived(color, stage, source, left, window=()):
        axis = ORDER_SUM[color][stage]
        pending.extend(current[color])
        for copy in current[color]:
            copy.wait_recv()
        total = source[pick(left, axis, me.along(axis, 0)) + window]
        for d in range(3):
            total += slots[color][stage][d].astype(f32)
        return total

    for color in range(BANDS):
        off, size = bands(half)[color]
        total = arrived(color, 0, own, "xzy", (pl.ds(off, size),))
        sums[color][...] = total
        lows[color][...] = total.astype(bf16)
        left = ORDER_SUM[color][1:]
        current[color] = sum_exchange(me, color, 1, lows[color], left, slots, send, recv)
    for color in range(BANDS):
        finals[color][...] = arrived(color, 1, sums[color], ORDER_SUM[color][1:])
        left = ORDER_SUM[color][2:]
        current[color] = sum_exchange(me, color, 2, finals[color], left, slots, send, recv)
    gathers = []
    for color in range(BANDS):
        off, size = bands(half)[color]
        total = arrived(color, 2, finals[color], ORDER_SUM[color][2:])
        final[pl.ds(off, size)] = total.astype(bf16)
        for m, (a, b) in enumerate(OTHERS):
            n = color * 7 + m
            gathers.append(
                remote(
                    final.at[pl.ds(off, size)], gathered.at[me.x_hi, me.y, pl.ds(off, size)],
                    ga_s.at[n], ga_r.at[n], me.piece(a, b),
                )
            )
            gathers[-1].start()
    for copy in gathers:
        copy.wait_recv()
    for a in range(2):
        for b in range(4):
            mine = (me.x_hi == a) & (me.y == b)
            part = jnp.where(mine, final[...].astype(f32), gathered[a, b].astype(f32))
            out_ref[a * half : (a + 1) * half, b * lanes : (b + 1) * lanes] = part
    return pending + gathers


def layer_kernel(
    heads, gain_ref, decay_ref, bias_ref, w_ref, h_ref, x_hbm, dy_hbm,
    x_ref, dy_ref, hid_ref, gw_ref,
    h_all, w_all, part, proj_in, proj_ref,
    run, run_t, step_t, step_c, key_t, query_t, key_hl, query_hl, scores,
    acc_diff, acc_cross, acc_const, dq, dk, dscores,
    state_in, state_out, grad_in, grad_out, state_own, grad_own,
    g_all, gt_all, own, low,
    slot_a0, slot_a1, slot_a2, sum_a0, sum_a1, sum_a2, low_a0, low_a1, low_a2,
    slot_b0, slot_b1, slot_b2, sum_b0, sum_b1, sum_b2,
    slot_c0, slot_c1, slot_c2, final, gathered, hid,
    load_h, load_xy, hs, hr, ag_s, ag_r, one_s, one_r, sf, rf, sb, rb,
    st_s, st_r, ga_s, ga_r, hid_s, hid_r,
):
    me = Place()
    k = me.ctx
    pieces = lax.axis_size("ctx")
    last = pieces - 1
    tokens = proj_ref.shape[0]
    half = tokens // 2
    chunks = heads // CHUNK
    cols, depth = w_ref.shape
    band, lanes = cols // 2, depth // 4
    right = {"ctx": lax.rem(k + 1, pieces)}
    left = {"ctx": lax.rem(k + pieces - 1, pieces)}

    def widened(ref):
        return jnp.concatenate([ref[...], jnp.zeros((1, NS - heads), f32)], axis=1)

    barrier = pltpu.get_barrier_semaphore()
    peers = [me.sibling()]
    peers += [me.ring("z", d) for d in (1, 2, 3)]
    peers += [me.ring("x", d) for d in (1, 3)]
    peers += [me.piece(a, b) for a, b in OTHERS]
    for peer in peers:
        pl.semaphore_signal(barrier, inc=1, device_id=peer, device_id_type=MESH)

    def load(s):
        return pltpu.make_async_copy(
            h_ref.at[:, me.columns(s, me.core, depth)], h_all.at[s, me.core], load_h.at[s]
        )

    def lend(s):
        return remote(
            h_ref.at[:, me.columns(s, 1 - me.core, depth)], h_all.at[s, me.core],
            hs.at[s], hr.at[s], me.sibling(),
        )

    loop(8, lambda s: load(s).start())
    load_x = pltpu.make_async_copy(x_hbm, x_ref, load_xy.at[0])
    load_dy = pltpu.make_async_copy(dy_hbm, dy_ref, load_xy.at[1])
    for a in range(2):
        for b in range(4):
            @pl.when((me.x_hi == a) & (me.y == b))
            def _():
                w_all[me.x_lo, me.z, b, a] = w_ref[
                    a * band : (a + 1) * band, b * lanes : (b + 1) * lanes
                ]
    part[...] = jnp.zeros_like(part)
    pl.semaphore_wait(barrier, len(peers))
    loop(8, lambda s: lend(s).start())
    load_x.start()
    load_dy.start()

    @pl.when(k == 0)
    def _():
        state_in[...] = jnp.zeros_like(state_in)

    @pl.when(k == last)
    def _():
        grad_in[...] = jnp.zeros_like(grad_in)

    dq[...] = jnp.zeros_like(dq)
    dk[...] = jnp.zeros_like(dk)
    dscores[...] = jnp.zeros_like(dscores)
    acc_diff[...] = jnp.zeros_like(acc_diff)
    acc_cross[...] = jnp.zeros_like(acc_cross)
    acc_const[...] = jnp.zeros_like(acc_const)

    pending = gather_weights(me, w_ref, w_all, ag_s, ag_r)

    def weights(s):
        parts = [w_all[s // 4, lax.rem(s, 4), b].reshape(cols, lanes) for b in range(4)]
        return jnp.concatenate(parts, axis=1)

    def project(s, side):
        part[side, :, :cols] += dot(h_all[s, side], weights(s), NT)

    def project_theirs(s):
        lend(s).wait_recv()
        project(s, 1 - me.core)

    def project_mine(s):
        load(s).wait()
        project(s, me.core)

    loop(8, project_theirs)
    give = remote(part.at[1 - me.core], proj_in, one_s.at[0], one_r.at[0], me.sibling())
    give.start()
    loop(8, project_mine)
    give.wait_recv()
    pending.append(give)
    proj_ref[...] = part[me.core] + proj_in[...]

    rows = lax.broadcasted_iota(jnp.int32, (tokens, tokens), 0)
    columns_at = lax.broadcasted_iota(jnp.int32, (tokens, tokens), 1)
    key = proj_ref[:, :NS]
    query = proj_ref[:, NS : 2 * NS] * NS ** (-0.5)
    pre = proj_ref[:, 2 * NS :] + widened(bias_ref)
    rate = jnp.exp(widened(decay_ref))
    steps = jnp.maximum(pre, 0.0) + jnp.log1p(jnp.exp(-jnp.abs(pre)))
    running = dot_high((rows >= columns_at).astype(f32), -rate * steps)
    run[...] = running
    run_t[...] = running.T
    step_c[...] = steps
    step_t[...] = steps.T
    key_t[...] = key.T
    query_t[...] = query.T
    high, low_part = split(key)
    key_hl[:, :NS] = high
    key_hl[:, NS:] = low_part
    high, low_part = split(query)
    query_hl[:, :NS] = high
    query_hl[:, NS:] = low_part
    scores[...] = dot_high(query, key, NT)
    load_x.wait()
    load_dy.wait()

    def copy_fwd(h):
        return remote(state_out.at[h], state_in.at[h], sf.at[h], rf.at[h], right)

    def copy_bwd(h):
        return remote(grad_out.at[h], grad_in.at[h], sb.at[h], rb.at[h], left)

    def columns(h, count=1):
        return pl.ds(pl.multiple_of(h * PS, PS), count * PS)

    def prepare(j):
        made = []
        for u in range(CHUNK):
            h = j * CHUNK + u
            r_row = run_t[pl.ds(h, 1), :]
            r_end = r_row[:, tokens - 1 : tokens]
            high, low_part = split(key_t[...] * (jnp.exp(r_end - r_row) * step_t[pl.ds(h, 1), :]))
            x = x_ref[:, columns(h)]
            state = dot(high, x) + dot(low_part, x)
            high, low_part = split(query_t[...] * jnp.exp(r_row))
            dy = dy_ref[:, columns(h)]
            made.append((h, state, dot(high, dy) + dot(low_part, dy)))
        for h, state, grad in made:
            state_own[h] = state
            grad_own[h] = grad

    def decay_of(h):
        return jnp.exp(run_t[pl.ds(h, 1), :][:, tokens - 1 : tokens])

    def forward(j):
        for u in range(CHUNK):
            h = j * CHUNK + u

            @pl.when(k > 0)
            def _():
                copy_fwd(h).wait_recv()

            @pl.when(k < last)
            def _():
                carried = decay_of(h) * state_in[h].astype(f32)
                state_out[h] = (carried + state_own[h]).astype(bf16)
                copy_fwd(h).start()

    def backward(j):
        for u in range(CHUNK):
            h = j * CHUNK + u

            @pl.when(k < last)
            def _():
                copy_bwd(h).wait_recv()

            @pl.when(k > 0)
            def _():
                carried = decay_of(h) * grad_in[h].astype(f32)
                grad_out[h] = (carried + grad_own[h]).astype(bf16)
                copy_bwd(h).start()

    def one_head(h):
        lane = lax.broadcasted_iota(jnp.int32, (tokens, NS), 1)
        at_h = lane == h
        r_col = jnp.sum(jnp.where(at_h, run[...], 0.0), axis=1, keepdims=True)
        s_col = jnp.sum(jnp.where(at_h, step_c[...], 0.0), axis=1, keepdims=True)
        r_row = run_t[pl.ds(h, 1), :]
        s_row = step_t[pl.ds(h, 1), :]
        r_end = r_row[:, tokens - 1 : tokens]
        x = x_ref[:, columns(h)]
        dy = dy_ref[:, columns(h)]
        gain = gain_ref[h]

        def decays(begin, width):
            t = lax.broadcasted_iota(jnp.int32, (half, width), 0) + begin
            s = lax.broadcasted_iota(jnp.int32, (half, width), 1)
            gaps = r_col[begin : begin + half] - r_row[:, :width]
            return jnp.exp(jnp.where(t >= s, gaps, -1e30)) * s_row[:, :width]

        top = decays(0, half)
        bottom = decays(half, tokens)
        mix_top = (top * scores[:half, :half]).astype(bf16)
        mix_bottom = (bottom * scores[half:, :]).astype(bf16)
        ds_top = top * dot(dy[:half], x[:half], NT)
        ds_bottom = bottom * dot(dy[half:], x, NT)
        y = jnp.concatenate([dot(mix_top, x[:half]), dot(mix_bottom, x)], axis=0)
        dx = dot(mix_bottom, dy[half:], TN)
        dx = jnp.concatenate([dx[:half] + dot(mix_top, dy[:half], TN), dx[half:]], axis=0)

        state = state_in[h]
        grad = grad_in[h]
        from_start = jnp.exp(r_col)
        to_end = jnp.exp(r_end - r_col) * s_col
        y += from_start * dot(query_hl[...], jnp.concatenate([state, state], axis=0))
        carried = to_end * dot(key_hl[...], jnp.concatenate([grad, grad], axis=0))
        dx += carried
        dq_h = from_start * dot(dy, state, NT)
        dk_h = to_end * dot(x, grad, NT)
        xf = x.astype(f32)
        dyf = dy.astype(f32)
        y_out = (y + gain * xf).astype(bf16)
        dx_out = (dx + gain * dyf).astype(bf16)
        cross = xf * dx
        cross_h = jnp.sum(cross, axis=1, keepdims=True)
        diff_h = jnp.sum(dyf * y - cross, axis=1, keepdims=True)
        inner = jnp.sum(grad.astype(f32) * state.astype(f32), axis=0, keepdims=True)
        inner = jnp.sum(inner, axis=1, keepdims=True)
        outer = jnp.sum(jnp.sum(xf * carried, axis=0, keepdims=True), axis=1, keepdims=True)
        const_h = jnp.exp(r_end) * inner + outer
        return at_h, ds_top, ds_bottom, dq_h, dk_h, y_out, dx_out, cross_h, diff_h, const_h

    def compute(j):
        done = [one_head(j * CHUNK + u) for u in range(CHUNK)]
        ats, ds_tops, ds_bottoms, dqs, dks, ys, dxs, crosses, diffs, consts = zip(*done)
        dscores[:half, :half] += sum(ds_tops[1:], ds_tops[0])
        dscores[half:, :] += sum(ds_bottoms[1:], ds_bottoms[0])
        dq[...] += sum(dqs[1:], dqs[0])
        dk[...] += sum(dks[1:], dks[0])
        cross, diff, const = acc_cross[...], acc_diff[...], acc_const[...]
        for u in range(CHUNK):
            cross = jnp.where(ats[u], crosses[u], cross)
            diff = jnp.where(ats[u], diffs[u], diff)
            const = jnp.where(ats[u][:8], consts[u], const)
        acc_cross[...] = cross
        acc_diff[...] = diff
        acc_const[...] = const
        for u in range(CHUNK):
            x_ref[:, columns(j * CHUNK + u)] = ys[u]
            dy_ref[:, columns(j * CHUNK + u)] = dxs[u]

    extra = LAG_FAR - LAG
    start_f = LAG * k + extra * (k // 4)
    start_b = LAG * (last - k) + extra * ((last - k) // 4)
    start_c = LAG * last + extra

    def iteration(i):
        jf = i - start_f
        jb = i - start_b
        jc = i - start_c

        @pl.when(i < chunks)
        def _():
            prepare(i)

        @pl.when((jf >= 0) & (jf < chunks))
        def _():
            forward(jf)

        @pl.when((jb >= 0) & (jb < chunks))
        def _():
            backward(jb)

        @pl.when((jc >= 0) & (jc < chunks))
        def _():
            compute(jc)

    loop(chunks + LAG * last + extra, iteration)

    key = proj_ref[:, :NS]
    query = proj_ref[:, NS : 2 * NS] * NS ** (-0.5)
    pre = proj_ref[:, 2 * NS :] + widened(bias_ref)
    d_log = dot_high((columns_at >= rows).astype(f32), acc_diff[...]) + acc_const[0:1, :]
    slope = 1.0 / (1.0 + jnp.exp(-pre))
    ratio = jnp.where(pre < -20.0, 1.0, slope / step_c[...])
    dk_all = dk[...] + dot_high(dscores[...].T, query)
    dq_all = (dq[...] + dot_high(dscores[...], key)) * NS ** (-0.5)
    dz_all = acc_cross[...] * ratio - rate * d_log * slope
    g_mine = g_all.at[me.core]
    gt_mine = gt_all.at[me.core]
    for n, grads in enumerate((dk_all, dq_all, dz_all)):
        g_mine[:, n * NS : (n + 1) * NS] = grads.astype(bf16)
        gt_mine[n * NS : (n + 1) * NS, :] = grads.T.astype(bf16)
    give_t = remote(gt_mine, gt_mine, one_s.at[1], one_r.at[1], me.sibling())
    give_g = remote(g_mine, g_mine, one_s.at[2], one_r.at[2], me.sibling())
    give_t.start()
    give_g.start()
    pending += [give_t, give_g]

    def weight_grad(s, side, more):
        p = dot(gt_all[side, :cols], h_all[s, side])
        for b in range(4):
            for a in range(2):
                at = (s // 4, lax.rem(s, 4), b, a)
                block = p[a * band : (a + 1) * band, b * lanes : (b + 1) * lanes]
                if more:
                    block += own[at]
                    low[at] = block.astype(bf16)
                own[at] = block

    loop(8, lambda s: weight_grad(s, me.core, False))
    give_t.wait_recv()
    loop(8, lambda s: weight_grad(s, 1 - me.core, True))
    slots = (
        (slot_a0, slot_b0, slot_c0), (slot_a1, slot_b1, slot_c1), (slot_a2, slot_b2, slot_c2)
    )
    current = sum_start(me, low, slots, st_s, st_r)
    give_g.wait_recv()

    def give_hid(s):
        return remote(
            hid.at[s], hid_ref.at[:, me.columns(s, me.core, depth)],
            hid_s.at[s], hid_r.at[s], me.sibling(),
        )

    def hidden(s):
        theirs = g_all[1 - me.core]
        hid[s] = dot(theirs[:, :cols], weights(s)).astype(bf16)
        give_hid(s).start()
        hid_ref[:, me.columns(s, me.core, depth)] = dot(
            g_all[me.core, :, :cols], weights(s)
        ).astype(bf16)

    loop(8, hidden)
    pending += sum_finish(
        me, current, own, slots, (sum_a0, sum_a1, sum_a2), (low_a0, low_a1, low_a2),
        (sum_b0, sum_b1, sum_b2), final, gathered, gw_ref, st_s, st_r, ga_s, ga_r,
    )
    for copy in pending:
        copy.wait_send()

    def finish(s):
        lend(s).wait_send()
        give_hid(s).wait_send()
        give_hid(s).wait_recv()

    loop(8, finish)

    @pl.when(k < last)
    def _():
        loop(heads, lambda h: copy_fwd(h).wait_send())

    @pl.when(k > 0)
    def _():
        loop(heads, lambda h: copy_bwd(h).wait_send())


def layer(gain, decay, bias, weight_t, h, x, dy):
    tokens, width = x.shape
    heads = width // PS
    chunks = heads // CHUNK
    cols, depth = weight_t.shape
    half, lanes = cols // 2, depth // 4
    sizes = [size for _, size in bands(half)]
    vm = pl.BlockSpec(memory_space=pltpu.VMEM)
    hbm = pl.BlockSpec(memory_space=pl.ANY)
    states = pltpu.VMEM((heads, NS, PS), bf16)
    own_states = pltpu.VMEM((heads, NS, PS), f32)
    by_token = pltpu.VMEM((tokens, NS), f32)
    by_state = pltpu.VMEM((NS, tokens), f32)
    square = pltpu.VMEM((tokens, tokens), f32)
    two_parts = pltpu.VMEM((tokens, 2 * NS), bf16)

    def shape(left, color):
        dims = {"x_lo": 2, "z": 4, "y": 4, "x_hi": 2}
        return tuple(n for name, n in dims.items() if name[0] in left) + (sizes[color], lanes)

    def sem(n):
        return pltpu.SemaphoreType.DMA((n,))

    everyone = range(BANDS)
    one = [shape(ORDER_SUM[c][1:], c) for c in everyone]
    two = [shape(ORDER_SUM[c][2:], c) for c in everyone]
    end = [shape("", c) for c in everyone]
    whole = (2, 4, 4, 2, half, lanes)
    return pl.pallas_call(
        partial(layer_kernel, heads),
        out_shape=(
            pltpu.VMEM(x.shape, bf16),
            pltpu.VMEM(x.shape, bf16),
            pltpu.VMEM(h.shape, bf16),
            pltpu.VMEM((cols, depth), f32),
        ),
        in_specs=[pl.BlockSpec(memory_space=pltpu.SMEM), vm, vm, vm, hbm, hbm, hbm],
        out_specs=(vm, vm, vm, vm),
        scratch_shapes=[
            pltpu.VMEM((8, 2, tokens, depth), bf16),
            pltpu.VMEM(whole, bf16),
            pltpu.VMEM((2, tokens, 3 * NS), f32),
            pltpu.VMEM((tokens, 3 * NS), f32),
            pltpu.VMEM((tokens, 3 * NS), f32),
            by_token, by_state, by_state, by_token, by_state, by_state,
            two_parts, two_parts, square,
            by_token, by_token, pltpu.VMEM((8, NS), f32), by_token, by_token, square,
            states, states, states, states, own_states, own_states,
            pltpu.VMEM((2, tokens, 3 * NS), bf16),
            pltpu.VMEM((2, 3 * NS, tokens), bf16),
            pltpu.VMEM(whole, f32),
            pltpu.VMEM(whole, bf16),
        ]
        + [pltpu.VMEM((3,) + s, bf16) for s in one]
        + [pltpu.VMEM(s, f32) for s in one]
        + [pltpu.VMEM(s, bf16) for s in one]
        + [pltpu.VMEM((3,) + s, bf16) for s in two]
        + [pltpu.VMEM(s, f32) for s in two]
        + [pltpu.VMEM((3,) + s, f32) for s in end]
        + [
            pltpu.VMEM((half, lanes), bf16),
            pltpu.VMEM((2, 4, half, lanes), bf16),
            pltpu.VMEM((8, tokens, depth), bf16),
            sem(8), sem(2), sem(8), sem(8), sem(27), sem(27), sem(3), sem(3),
            sem(heads), sem(heads), sem(heads), sem(heads),
            sem(27), sem(27), sem(21), sem(21), sem(8), sem(8),
        ],
        compiler_params=pltpu.CompilerParams(
            collective_id=0, has_side_effects=True, vmem_limit_bytes=46 * 2**20
        ),
    )(gain, decay, bias, weight_t, h, x, dy)


def store_kernel(*refs):
    sems = refs[8]
    copies = []
    for source, target in zip(refs[:4], refs[4:8]):
        rows = source.shape[0] // 2
        for part in range(2):
            at = pl.ds(part * rows, rows)
            copies.append(
                pltpu.make_async_copy(source.at[at], target.at[at], sems.at[len(copies)])
            )
            copies[-1].start()
    for copy in copies:
        copy.wait()


def store(*arrays):
    hbm = pl.BlockSpec(memory_space=pl.ANY)
    vm = pl.BlockSpec(memory_space=pltpu.VMEM)
    return pl.pallas_call(
        store_kernel,
        out_shape=tuple(jax.ShapeDtypeStruct(a.shape, a.dtype) for a in arrays),
        in_specs=[vm] * 4,
        out_specs=(hbm,) * 4,
        scratch_shapes=[pltpu.SemaphoreType.DMA((8,))],
        compiler_params=pltpu.CompilerParams(vmem_limit_bytes=16 * 2**20),
    )(*arrays)


def shards(hidden_rows, inner_rows, weight_proj, decay_log, step_bias, skip_gain, grad_output):
    token_rows = hidden_rows.reshape(-1, hidden_rows.shape[-1])
    value_rows = inner_rows.reshape(-1, inner_rows.shape[-1])
    cotangent = grad_output.reshape(value_rows.shape)
    output, grad_values, grad_tokens, grad_weight_t = layer(
        skip_gain, decay_log[None], step_bias[None], weight_proj.T, token_rows, value_rows, cotangent
    )
    output, grad_values, grad_tokens, grad_weight_t = store(
        output, grad_values, grad_tokens, grad_weight_t
    )
    return (
        output.reshape(inner_rows.shape),
        grad_values.reshape(inner_rows.shape),
        grad_tokens.reshape(hidden_rows.shape),
        grad_weight_t.T,
    )


def solution(mesh):
    rows = P("dp", "ctx", None)
    return jax.shard_map(
        shards,
        mesh=mesh,
        in_specs=(rows, rows, P("dp", None), P(), P(), P(), rows),
        out_specs=(rows, rows, rows, P("dp", None)),
        check_vma=False,
    )
```

```python
from functools import partial

import jax
import jax.numpy as jnp
from jax import lax
from jax.experimental import pallas as pl
from jax.experimental.pallas import tpu as pltpu
from jax.sharding import PartitionSpec as P

PS = 128
NS = 128
CHUNK = 2
LAG = 3
LAG_FAR = 5
MESH = pl.DeviceIdType.MESH
highest = lax.Precision.HIGHEST
f32 = jnp.float32
bf16 = jnp.bfloat16
NN = (((1,), (0,)), ((), ()))
NT = (((1,), (1,)), ((), ()))
TN = (((0,), (0,)), ((), ()))


def dot(a, b, dims=NN):
    return lax.dot_general(a, b, dims, preferred_element_type=f32)


def dot_high(a, b, dims=NN):
    return lax.dot_general(a, b, dims, preferred_element_type=f32, precision=highest)


def split(a):
    high = a.astype(bf16)
    return high, (a - high.astype(f32)).astype(bf16)

BANDS = 3
ORDER_SUM = ("zyx", "yxz", "xzy")
ORDER_GATHER = ("xyz", "zxy", "yzx")


def bands(half):
    third = half // 3 // 16 * 16
    first = half - 2 * third
    return ((0, first), (first, third), (first + third, third))


def remote(src, dst, send, recv, device):
    return pltpu.make_async_remote_copy(
        src_ref=src, dst_ref=dst, send_sem=send, recv_sem=recv,
        device_id=device, device_id_type=MESH,
    )


class Place:
    def __init__(self):
        dp, ctx = lax.axis_index("dp"), lax.axis_index("ctx")
        self.x_lo, self.z, self.core = dp // 8, lax.rem(dp // 2, 4), lax.rem(dp, 2)
        self.x_hi, self.y = ctx // 4, lax.rem(ctx, 4)
        self.x = self.x_hi * 2 + self.x_lo
        self.ctx = ctx

    def device(self, **other):
        at = {name: getattr(self, name) for name in ("x_lo", "z", "core", "x_hi", "y")}
        at.update(other)
        return {
            "dp": at["x_lo"] * 8 + at["z"] * 2 + at["core"],
            "ctx": at["x_hi"] * 4 + at["y"],
        }

    def along(self, axis, d):
        to = lax.rem(getattr(self, axis) + d, 4)
        return {"x_lo": lax.rem(to, 2), "x_hi": to // 2} if axis == "x" else {axis: to}

    def ring(self, axis, d):
        return self.device(**self.along(axis, d))

    def sibling(self):
        return self.device(core=1 - self.core)

    def piece(self, a, b):
        return self.device(x_hi=lax.rem(self.x_hi + a, 2), y=lax.rem(self.y + b, 4))

    def columns(self, s, side, depth):
        at = (s // 4) * 8 + lax.rem(s, 4) * 2 + side
        return pl.ds(pl.multiple_of(at * depth, depth), depth)


OTHERS = [(a, b) for a in range(2) for b in range(4) if a + b]


def loop(count, body):
    def step(i, carry):
        body(i)
        return carry

    lax.fori_loop(0, count, step, 0)


def gather_weights(me, w_ref, all_ref, send, recv):
    cols, depth = w_ref.shape
    half = cols // 2
    whole = slice(None)

    def region(color, have):
        off, size = bands(half)[color]
        return all_ref.at[
            whole if "x" in have else me.x_lo,
            whole if "z" in have else me.z,
            whole if "y" in have else me.y,
            whole if "x" in have else me.x_hi,
            pl.ds(off, size),
        ]

    def exchange(color, stage):
        axis = ORDER_GATHER[color][stage]
        part = region(color, ORDER_GATHER[color][:stage])
        copies = []
        for d in (2, 1, 3):
            n = color * 9 + stage * 3 + d - 1
            copies.append(remote(part, part, send.at[n], recv.at[n], me.ring(axis, d)))
            copies[-1].start()
        return copies

    pending = []
    current = [exchange(color, 0) for color in range(BANDS)]
    for stage in (1, 2, 3):
        for color in range(BANDS):
            for copy in current[color]:
                copy.wait_recv()
            pending += current[color]
            if stage < 3:
                current[color] = exchange(color, stage)
    return pending


def sum_start(me, low, slots, send, recv):
    return [sum_exchange(me, color, 0, low, "xzy", slots, send, recv) for color in range(BANDS)]


def pick(left, axis, place):
    at = []
    for name in ("x_lo", "z", "y", "x_hi"):
        if name[0] in left:
            at.append(place[name] if name[0] == axis else slice(None))
    return tuple(at)


def sum_exchange(me, color, stage, source, left, slots, send, recv):
    axis = ORDER_SUM[color][stage]
    off, size = bands(slots[0][2].shape[1] + slots[1][2].shape[1] + slots[2][2].shape[1])[color]
    window = (pl.ds(off, size),) if stage == 0 else ()
    copies = []
    for d in (2, 1, 3):
        n = color * 9 + stage * 3 + d - 1
        part = source.at[pick(left, axis, me.along(axis, d)) + window]
        copies.append(
            remote(part, slots[color][stage].at[d - 1], send.at[n], recv.at[n], me.ring(axis, d))
        )
        copies[-1].start()
    return copies


def sum_finish(me, current, own, slots, sums, lows, finals, final, gathered, out_ref, send, recv, ga_s, ga_r):
    half = final.shape[0]
    lanes = final.shape[1]
    pending = []

    def arrived(color, stage, source, left, window=()):
        axis = ORDER_SUM[color][stage]
        pending.extend(current[color])
        for copy in current[color]:
            copy.wait_recv()
        total = source[pick(left, axis, me.along(axis, 0)) + window]
        for d in range(3):
            total += slots[color][stage][d].astype(f32)
        return total

    for color in range(BANDS):
        off, size = bands(half)[color]
        total = arrived(color, 0, own, "xzy", (pl.ds(off, size),))
        sums[color][...] = total
        lows[color][...] = total.astype(bf16)
        left = ORDER_SUM[color][1:]
        current[color] = sum_exchange(me, color, 1, lows[color], left, slots, send, recv)
    for color in range(BANDS):
        finals[color][...] = arrived(color, 1, sums[color], ORDER_SUM[color][1:])
        left = ORDER_SUM[color][2:]
        current[color] = sum_exchange(me, color, 2, finals[color], left, slots, send, recv)
    gathers = []
    for color in range(BANDS):
        off, size = bands(half)[color]
        total = arrived(color, 2, finals[color], ORDER_SUM[color][2:])
        final[pl.ds(off, size)] = total.astype(bf16)
        for m, (a, b) in enumerate(OTHERS):
            n = color * 7 + m
            gathers.append(
                remote(
                    final.at[pl.ds(off, size)], gathered.at[me.x_hi, me.y, pl.ds(off, size)],
                    ga_s.at[n], ga_r.at[n], me.piece(a, b),
                )
            )
            gathers[-1].start()
    for copy in gathers:
        copy.wait_recv()
    for a in range(2):
        for b in range(4):
            mine = (me.x_hi == a) & (me.y == b)
            part = jnp.where(mine, final[...].astype(f32), gathered[a, b].astype(f32))
            out_ref[a * half : (a + 1) * half, b * lanes : (b + 1) * lanes] = part
    return pending + gathers


def layer_kernel(
    heads, gain_ref, decay_ref, bias_ref, w_ref, h_ref, x_hbm, dy_hbm,
    x_ref, dy_ref, hid_ref, gw_ref,
    h_all, w_all, part, proj_in, proj_ref,
    run, run_t, step_t, step_c, key_t, query_t, key_hl, query_hl, scores,
    acc_diff, acc_cross, acc_const, dq, dk, dscores,
    state_in, state_out, grad_in, grad_out, state_own, grad_own,
    g_all, gt_all, own, low,
    slot_a0, slot_a1, slot_a2, sum_a0, sum_a1, sum_a2, low_a0, low_a1, low_a2,
    slot_b0, slot_b1, slot_b2, sum_b0, sum_b1, sum_b2,
    slot_c0, slot_c1, slot_c2, final, gathered, hid,
    load_h, load_xy, hs, hr, ag_s, ag_r, one_s, one_r, sf, rf, sb, rb,
    st_s, st_r, ga_s, ga_r, hid_s, hid_r,
):
    me = Place()
    k = me.ctx
    pieces = lax.axis_size("ctx")
    last = pieces - 1
    tokens = proj_ref.shape[0]
    half = tokens // 2
    chunks = heads // CHUNK
    cols, depth = w_ref.shape
    band, lanes = cols // 2, depth // 4
    right = {"ctx": lax.rem(k + 1, pieces)}
    left = {"ctx": lax.rem(k + pieces - 1, pieces)}

    def widened(ref):
        return jnp.concatenate([ref[...], jnp.zeros((1, NS - heads), f32)], axis=1)

    barrier = pltpu.get_barrier_semaphore()
    peers = [me.sibling()]
    peers += [me.ring("z", d) for d in (1, 2, 3)]
    peers += [me.ring("x", d) for d in (1, 3)]
    peers += [me.piece(a, b) for a, b in OTHERS]
    for peer in peers:
        pl.semaphore_signal(barrier, inc=1, device_id=peer, device_id_type=MESH)

    def load(s):
        return pltpu.make_async_copy(
            h_ref.at[:, me.columns(s, me.core, depth)], h_all.at[s, me.core], load_h.at[s]
        )

    def lend(s):
        return remote(
            h_ref.at[:, me.columns(s, 1 - me.core, depth)], h_all.at[s, me.core],
            hs.at[s], hr.at[s], me.sibling(),
        )

    load_x = pltpu.make_async_copy(x_hbm, x_ref, load_xy.at[0])
    load_dy = pltpu.make_async_copy(dy_hbm, dy_ref, load_xy.at[1])
    piece = pltpu.make_async_copy(
        w_ref.at[
            pl.ds(pl.multiple_of(me.x_hi * band, 16), band),
            pl.ds(pl.multiple_of(me.y * lanes, lanes), lanes),
        ],
        w_all.at[me.x_lo, me.z, me.y, me.x_hi],
        load_xy.at[2],
    )
    piece.start()
    loop(8, lambda s: load(s).start())
    part[...] = jnp.zeros_like(part)
    @pl.when(k == 0)
    def _():
        state_in[...] = jnp.zeros_like(state_in)

    @pl.when(k == last)
    def _():
        grad_in[...] = jnp.zeros_like(grad_in)

    dq[...] = jnp.zeros_like(dq)
    dk[...] = jnp.zeros_like(dk)
    dscores[...] = jnp.zeros_like(dscores)
    acc_diff[...] = jnp.zeros_like(acc_diff)
    acc_cross[...] = jnp.zeros_like(acc_cross)
    acc_const[...] = jnp.zeros_like(acc_const)

    piece.wait()
    pl.semaphore_wait(barrier, len(peers))
    loop(8, lambda s: lend(s).start())
    load_x.start()
    load_dy.start()

    pending = gather_weights(me, w_ref, w_all, ag_s, ag_r)

    def weights(s):
        parts = [w_all[s // 4, lax.rem(s, 4), b].reshape(cols, lanes) for b in range(4)]
        return jnp.concatenate(parts, axis=1)

    def project(s, side):
        part[side, :, :cols] += dot(h_all[s, side], weights(s), NT)

    def project_theirs(s):
        lend(s).wait_recv()
        project(s, 1 - me.core)

    def project_mine(s):
        load(s).wait()
        project(s, me.core)

    loop(8, project_theirs)
    give = remote(part.at[1 - me.core], proj_in, one_s.at[0], one_r.at[0], me.sibling())
    give.start()
    loop(8, project_mine)
    give.wait_recv()
    pending.append(give)
    proj_ref[...] = part[me.core] + proj_in[...]

    rows = lax.broadcasted_iota(jnp.int32, (tokens, tokens), 0)
    columns_at = lax.broadcasted_iota(jnp.int32, (tokens, tokens), 1)
    key = proj_ref[:, :NS]
    query = proj_ref[:, NS : 2 * NS] * NS ** (-0.5)
    pre = proj_ref[:, 2 * NS :] + widened(bias_ref)
    rate = jnp.exp(widened(decay_ref))
    steps = jnp.maximum(pre, 0.0) + jnp.log1p(jnp.exp(-jnp.abs(pre)))
    running = dot_high((rows >= columns_at).astype(f32), -rate * steps)
    run[...] = running
    run_t[...] = running.T
    step_c[...] = steps
    step_t[...] = steps.T
    key_t[...] = key.T
    query_t[...] = query.T
    high, low_part = split(key)
    key_hl[:, :NS] = high
    key_hl[:, NS:] = low_part
    high, low_part = split(query)
    query_hl[:, :NS] = high
    query_hl[:, NS:] = low_part
    scores[...] = dot_high(query, key, NT)
    load_x.wait()
    load_dy.wait()

    def copy_fwd(h):
        return remote(state_out.at[h], state_in.at[h], sf.at[h], rf.at[h], right)

    def copy_bwd(h):
        return remote(grad_out.at[h], grad_in.at[h], sb.at[h], rb.at[h], left)

    def columns(h, count=1):
        return pl.ds(pl.multiple_of(h * PS, PS), count * PS)

    def prepare(j):
        made = []
        for u in range(CHUNK):
            h = j * CHUNK + u
            r_row = run_t[pl.ds(h, 1), :]
            r_end = r_row[:, tokens - 1 : tokens]
            high, low_part = split(key_t[...] * (jnp.exp(r_end - r_row) * step_t[pl.ds(h, 1), :]))
            x = x_ref[:, columns(h)]
            state = dot(high, x) + dot(low_part, x)
            high, low_part = split(query_t[...] * jnp.exp(r_row))
            dy = dy_ref[:, columns(h)]
            made.append((h, state, dot(high, dy) + dot(low_part, dy)))
        for h, state, grad in made:
            state_own[h] = state
            grad_own[h] = grad

    def decay_of(h):
        return jnp.exp(run_t[pl.ds(h, 1), :][:, tokens - 1 : tokens])

    def forward(j):
        for u in range(CHUNK):
            h = j * CHUNK + u

            @pl.when(k > 0)
            def _():
                copy_fwd(h).wait_recv()

            @pl.when(k < last)
            def _():
                carried = decay_of(h) * state_in[h].astype(f32)
                state_out[h] = (carried + state_own[h]).astype(bf16)
                copy_fwd(h).start()

    def backward(j):
        for u in range(CHUNK):
            h = j * CHUNK + u

            @pl.when(k < last)
            def _():
                copy_bwd(h).wait_recv()

            @pl.when(k > 0)
            def _():
                carried = decay_of(h) * grad_in[h].astype(f32)
                grad_out[h] = (carried + grad_own[h]).astype(bf16)
                copy_bwd(h).start()

    def one_head(h):
        lane = lax.broadcasted_iota(jnp.int32, (tokens, NS), 1)
        at_h = lane == h
        r_col = jnp.sum(jnp.where(at_h, run[...], 0.0), axis=1, keepdims=True)
        s_col = jnp.sum(jnp.where(at_h, step_c[...], 0.0), axis=1, keepdims=True)
        r_row = run_t[pl.ds(h, 1), :]
        s_row = step_t[pl.ds(h, 1), :]
        r_end = r_row[:, tokens - 1 : tokens]
        x = x_ref[:, columns(h)]
        dy = dy_ref[:, columns(h)]
        gain = gain_ref[h]

        def decays(begin, width):
            t = lax.broadcasted_iota(jnp.int32, (half, width), 0) + begin
            s = lax.broadcasted_iota(jnp.int32, (half, width), 1)
            gaps = r_col[begin : begin + half] - r_row[:, :width]
            return jnp.exp(jnp.where(t >= s, gaps, -1e30)) * s_row[:, :width]

        top = decays(0, half)
        bottom = decays(half, tokens)
        mix_top = (top * scores[:half, :half]).astype(bf16)
        mix_bottom = (bottom * scores[half:, :]).astype(bf16)
        ds_top = top * dot(dy[:half], x[:half], NT)
        ds_bottom = bottom * dot(dy[half:], x, NT)
        y = jnp.concatenate([dot(mix_top, x[:half]), dot(mix_bottom, x)], axis=0)
        dx = dot(mix_bottom, dy[half:], TN)
        dx = jnp.concatenate([dx[:half] + dot(mix_top, dy[:half], TN), dx[half:]], axis=0)

        state = state_in[h]
        grad = grad_in[h]
        from_start = jnp.exp(r_col)
        to_end = jnp.exp(r_end - r_col) * s_col
        y += from_start * dot(query_hl[...], jnp.concatenate([state, state], axis=0))
        carried = to_end * dot(key_hl[...], jnp.concatenate([grad, grad], axis=0))
        dx += carried
        dq_h = from_start * dot(dy, state, NT)
        dk_h = to_end * dot(x, grad, NT)
        xf = x.astype(f32)
        dyf = dy.astype(f32)
        y_out = (y + gain * xf).astype(bf16)
        dx_out = (dx + gain * dyf).astype(bf16)
        cross = xf * dx
        cross_h = jnp.sum(cross, axis=1, keepdims=True)
        diff_h = jnp.sum(dyf * y - cross, axis=1, keepdims=True)
        inner = jnp.sum(grad.astype(f32) * state.astype(f32), axis=0, keepdims=True)
        inner = jnp.sum(inner, axis=1, keepdims=True)
        outer = jnp.sum(jnp.sum(xf * carried, axis=0, keepdims=True), axis=1, keepdims=True)
        const_h = jnp.exp(r_end) * inner + outer
        return at_h, ds_top, ds_bottom, dq_h, dk_h, y_out, dx_out, cross_h, diff_h, const_h

    def compute(j):
        done = [one_head(j * CHUNK + u) for u in range(CHUNK)]
        ats, ds_tops, ds_bottoms, dqs, dks, ys, dxs, crosses, diffs, consts = zip(*done)
        dscores[:half, :half] += sum(ds_tops[1:], ds_tops[0])
        dscores[half:, :] += sum(ds_bottoms[1:], ds_bottoms[0])
        dq[...] += sum(dqs[1:], dqs[0])
        dk[...] += sum(dks[1:], dks[0])
        cross, diff, const = acc_cross[...], acc_diff[...], acc_const[...]
        for u in range(CHUNK):
            cross = jnp.where(ats[u], crosses[u], cross)
            diff = jnp.where(ats[u], diffs[u], diff)
            const = jnp.where(ats[u][:8], consts[u], const)
        acc_cross[...] = cross
        acc_diff[...] = diff
        acc_const[...] = const
        for u in range(CHUNK):
            x_ref[:, columns(j * CHUNK + u)] = ys[u]
            dy_ref[:, columns(j * CHUNK + u)] = dxs[u]

    extra = LAG_FAR - LAG
    start_f = LAG * k + extra * (k // 4)
    start_b = LAG * (last - k) + extra * ((last - k) // 4)
    start_c = LAG * last + extra

    def iteration(i):
        jf = i - start_f
        jb = i - start_b
        jc = i - start_c

        @pl.when(i < chunks)
        def _():
            prepare(i)

        @pl.when((jf >= 0) & (jf < chunks))
        def _():
            forward(jf)

        @pl.when((jb >= 0) & (jb < chunks))
        def _():
            backward(jb)

        @pl.when((jc >= 0) & (jc < chunks))
        def _():
            compute(jc)

    loop(chunks + LAG * last + extra, iteration)

    key = proj_ref[:, :NS]
    query = proj_ref[:, NS : 2 * NS] * NS ** (-0.5)
    pre = proj_ref[:, 2 * NS :] + widened(bias_ref)
    d_log = dot_high((columns_at >= rows).astype(f32), acc_diff[...]) + acc_const[0:1, :]
    slope = 1.0 / (1.0 + jnp.exp(-pre))
    ratio = jnp.where(pre < -20.0, 1.0, slope / step_c[...])
    dk_all = dk[...] + dot_high(dscores[...].T, query)
    dq_all = (dq[...] + dot_high(dscores[...], key)) * NS ** (-0.5)
    dz_all = acc_cross[...] * ratio - rate * d_log * slope
    g_mine = g_all.at[me.core]
    gt_mine = gt_all.at[me.core]
    for n, grads in enumerate((dk_all, dq_all, dz_all)):
        g_mine[:, n * NS : (n + 1) * NS] = grads.astype(bf16)
        gt_mine[n * NS : (n + 1) * NS, :] = grads.T.astype(bf16)
    give_t = remote(gt_mine, gt_mine, one_s.at[1], one_r.at[1], me.sibling())
    give_g = remote(g_mine, g_mine, one_s.at[2], one_r.at[2], me.sibling())
    give_t.start()
    give_g.start()
    pending += [give_t, give_g]

    def weight_grad(s, side, more):
        p = dot(gt_all[side, :cols], h_all[s, side])
        for b in range(4):
            for a in range(2):
                at = (s // 4, lax.rem(s, 4), b, a)
                block = p[a * band : (a + 1) * band, b * lanes : (b + 1) * lanes]
                if more:
                    block += own[at]
                    low[at] = block.astype(bf16)
                own[at] = block

    loop(8, lambda s: weight_grad(s, me.core, False))
    give_t.wait_recv()
    loop(8, lambda s: weight_grad(s, 1 - me.core, True))
    slots = (
        (slot_a0, slot_b0, slot_c0), (slot_a1, slot_b1, slot_c1), (slot_a2, slot_b2, slot_c2)
    )
    current = sum_start(me, low, slots, st_s, st_r)
    give_g.wait_recv()

    def give_hid(s):
        return remote(
            hid.at[s], hid_ref.at[:, me.columns(s, me.core, depth)],
            hid_s.at[s], hid_r.at[s], me.sibling(),
        )

    def hidden(s):
        theirs = g_all[1 - me.core]
        hid[s] = dot(theirs[:, :cols], weights(s)).astype(bf16)
        give_hid(s).start()
        hid_ref[:, me.columns(s, me.core, depth)] = dot(
            g_all[me.core, :, :cols], weights(s)
        ).astype(bf16)

    loop(8, hidden)
    pending += sum_finish(
        me, current, own, slots, (sum_a0, sum_a1, sum_a2), (low_a0, low_a1, low_a2),
        (sum_b0, sum_b1, sum_b2), final, gathered, gw_ref, st_s, st_r, ga_s, ga_r,
    )
    for copy in pending:
        copy.wait_send()

    def finish(s):
        lend(s).wait_send()
        give_hid(s).wait_send()
        give_hid(s).wait_recv()

    loop(8, finish)

    @pl.when(k < last)
    def _():
        loop(heads, lambda h: copy_fwd(h).wait_send())

    @pl.when(k > 0)
    def _():
        loop(heads, lambda h: copy_bwd(h).wait_send())


def layer(gain, decay, bias, weight_t, h, x, dy):
    tokens, width = x.shape
    heads = width // PS
    chunks = heads // CHUNK
    cols, depth = weight_t.shape
    half, lanes = cols // 2, depth // 4
    sizes = [size for _, size in bands(half)]
    vm = pl.BlockSpec(memory_space=pltpu.VMEM)
    hbm = pl.BlockSpec(memory_space=pl.ANY)
    states = pltpu.VMEM((heads, NS, PS), bf16)
    own_states = pltpu.VMEM((heads, NS, PS), f32)
    by_token = pltpu.VMEM((tokens, NS), f32)
    by_state = pltpu.VMEM((NS, tokens), f32)
    square = pltpu.VMEM((tokens, tokens), f32)
    two_parts = pltpu.VMEM((tokens, 2 * NS), bf16)

    def shape(left, color):
        dims = {"x_lo": 2, "z": 4, "y": 4, "x_hi": 2}
        return tuple(n for name, n in dims.items() if name[0] in left) + (sizes[color], lanes)

    def sem(n):
        return pltpu.SemaphoreType.DMA((n,))

    everyone = range(BANDS)
    one = [shape(ORDER_SUM[c][1:], c) for c in everyone]
    two = [shape(ORDER_SUM[c][2:], c) for c in everyone]
    end = [shape("", c) for c in everyone]
    whole = (2, 4, 4, 2, half, lanes)
    return pl.pallas_call(
        partial(layer_kernel, heads),
        out_shape=(
            pltpu.VMEM(x.shape, bf16),
            pltpu.VMEM(x.shape, bf16),
            pltpu.VMEM(h.shape, bf16),
            pltpu.VMEM((cols, depth), f32),
        ),
        in_specs=[pl.BlockSpec(memory_space=pltpu.SMEM), vm, vm, hbm, hbm, hbm, hbm],
        out_specs=(vm, vm, vm, vm),
        scratch_shapes=[
            pltpu.VMEM((8, 2, tokens, depth), bf16),
            pltpu.VMEM(whole, bf16),
            pltpu.VMEM((2, tokens, 3 * NS), f32),
            pltpu.VMEM((tokens, 3 * NS), f32),
            pltpu.VMEM((tokens, 3 * NS), f32),
            by_token, by_state, by_state, by_token, by_state, by_state,
            two_parts, two_parts, square,
            by_token, by_token, pltpu.VMEM((8, NS), f32), by_token, by_token, square,
            states, states, states, states, own_states, own_states,
            pltpu.VMEM((2, tokens, 3 * NS), bf16),
            pltpu.VMEM((2, 3 * NS, tokens), bf16),
            pltpu.VMEM(whole, f32),
            pltpu.VMEM(whole, bf16),
        ]
        + [pltpu.VMEM((3,) + s, bf16) for s in one]
        + [pltpu.VMEM(s, f32) for s in one]
        + [pltpu.VMEM(s, bf16) for s in one]
        + [pltpu.VMEM((3,) + s, bf16) for s in two]
        + [pltpu.VMEM(s, f32) for s in two]
        + [pltpu.VMEM((3,) + s, f32) for s in end]
        + [
            pltpu.VMEM((half, lanes), bf16),
            pltpu.VMEM((2, 4, half, lanes), bf16),
            pltpu.VMEM((8, tokens, depth), bf16),
            sem(8), sem(3), sem(8), sem(8), sem(27), sem(27), sem(3), sem(3),
            sem(heads), sem(heads), sem(heads), sem(heads),
            sem(27), sem(27), sem(21), sem(21), sem(8), sem(8),
        ],
        compiler_params=pltpu.CompilerParams(
            collective_id=0, has_side_effects=True, vmem_limit_bytes=46 * 2**20
        ),
    )(gain, decay, bias, weight_t, h, x, dy)


def store_kernel(*refs):
    sems = refs[8]
    copies = []
    for source, target in zip(refs[:4], refs[4:8]):
        rows = source.shape[0] // 4
        for part in range(4):
            at = pl.ds(part * rows, rows)
            copies.append(
                pltpu.make_async_copy(source.at[at], target.at[at], sems.at[len(copies)])
            )
            copies[-1].start()
    for copy in copies:
        copy.wait()


def store(*arrays):
    hbm = pl.BlockSpec(memory_space=pl.ANY)
    vm = pl.BlockSpec(memory_space=pltpu.VMEM)
    return pl.pallas_call(
        store_kernel,
        out_shape=tuple(jax.ShapeDtypeStruct(a.shape, a.dtype) for a in arrays),
        in_specs=[vm] * 4,
        out_specs=(hbm,) * 4,
        scratch_shapes=[pltpu.SemaphoreType.DMA((16,))],
        compiler_params=pltpu.CompilerParams(vmem_limit_bytes=16 * 2**20),
    )(*arrays)


def shards(hidden_rows, inner_rows, weight_proj, decay_log, step_bias, skip_gain, grad_output):
    token_rows = hidden_rows.reshape(-1, hidden_rows.shape[-1])
    value_rows = inner_rows.reshape(-1, inner_rows.shape[-1])
    cotangent = grad_output.reshape(value_rows.shape)
    output, grad_values, grad_tokens, grad_weight_t = layer(
        skip_gain, decay_log[None], step_bias[None], weight_proj.T, token_rows, value_rows, cotangent
    )
    output, grad_values, grad_tokens, grad_weight_t = store(
        output, grad_values, grad_tokens, grad_weight_t
    )
    return (
        output.reshape(inner_rows.shape),
        grad_values.reshape(inner_rows.shape),
        grad_tokens.reshape(hidden_rows.shape),
        grad_weight_t.T,
    )


def solution(mesh):
    rows = P("dp", "ctx", None)
    return jax.shard_map(
        shards,
        mesh=mesh,
        in_specs=(rows, rows, P("dp", None), P(), P(), P(), rows),
        out_specs=(rows, rows, rows, P("dp", None)),
        check_vma=False,
    )
```

```python
from functools import partial

import jax
import jax.numpy as jnp
from jax import lax
from jax.experimental import pallas as pl
from jax.experimental.pallas import tpu as pltpu
from jax.sharding import PartitionSpec as P

PS = 128
NS = 128
CHUNK = 2
LAG = 3
LAG_FAR = 4
MESH = pl.DeviceIdType.MESH
highest = lax.Precision.HIGHEST
f32 = jnp.float32
bf16 = jnp.bfloat16
NN = (((1,), (0,)), ((), ()))
NT = (((1,), (1,)), ((), ()))
TN = (((0,), (0,)), ((), ()))


def dot(a, b, dims=NN):
    return lax.dot_general(a, b, dims, preferred_element_type=f32)


def dot_high(a, b, dims=NN):
    return lax.dot_general(a, b, dims, preferred_element_type=f32, precision=highest)


def split(a):
    high = a.astype(bf16)
    return high, (a - high.astype(f32)).astype(bf16)

BANDS = 3
ORDER_SUM = ("zyx", "yxz", "xzy")
ORDER_GATHER = ("xyz", "zxy", "yzx")


def bands(half):
    third = half // 3 // 16 * 16
    first = half - 2 * third
    return ((0, first), (first, third), (first + third, third))


def remote(src, dst, send, recv, device):
    return pltpu.make_async_remote_copy(
        src_ref=src, dst_ref=dst, send_sem=send, recv_sem=recv,
        device_id=device, device_id_type=MESH,
    )


class Place:
    def __init__(self):
        dp, ctx = lax.axis_index("dp"), lax.axis_index("ctx")
        self.x_lo, self.z, self.core = dp // 8, lax.rem(dp // 2, 4), lax.rem(dp, 2)
        self.x_hi, self.y = ctx // 4, lax.rem(ctx, 4)
        self.x = self.x_hi * 2 + self.x_lo
        self.ctx = ctx

    def device(self, **other):
        at = {name: getattr(self, name) for name in ("x_lo", "z", "core", "x_hi", "y")}
        at.update(other)
        return {
            "dp": at["x_lo"] * 8 + at["z"] * 2 + at["core"],
            "ctx": at["x_hi"] * 4 + at["y"],
        }

    def along(self, axis, d):
        to = lax.rem(getattr(self, axis) + d, 4)
        return {"x_lo": lax.rem(to, 2), "x_hi": to // 2} if axis == "x" else {axis: to}

    def ring(self, axis, d):
        return self.device(**self.along(axis, d))

    def sibling(self):
        return self.device(core=1 - self.core)

    def piece(self, a, b):
        return self.device(x_hi=lax.rem(self.x_hi + a, 2), y=lax.rem(self.y + b, 4))

    def columns(self, s, side, depth):
        at = (s // 4) * 8 + lax.rem(s, 4) * 2 + side
        return pl.ds(pl.multiple_of(at * depth, depth), depth)


OTHERS = [(a, b) for a in range(2) for b in range(4) if a + b]


def loop(count, body):
    def step(i, carry):
        body(i)
        return carry

    lax.fori_loop(0, count, step, 0)


def gather_weights(me, w_ref, all_ref, send, recv):
    cols, depth = w_ref.shape
    half = cols // 2
    whole = slice(None)

    def region(color, have):
        off, size = bands(half)[color]
        return all_ref.at[
            whole if "x" in have else me.x_lo,
            whole if "z" in have else me.z,
            whole if "y" in have else me.y,
            whole if "x" in have else me.x_hi,
            pl.ds(off, size),
        ]

    def exchange(color, stage):
        axis = ORDER_GATHER[color][stage]
        part = region(color, ORDER_GATHER[color][:stage])
        copies = []
        for d in (2, 1, 3):
            n = color * 9 + stage * 3 + d - 1
            copies.append(remote(part, part, send.at[n], recv.at[n], me.ring(axis, d)))
            copies[-1].start()
        return copies

    pending = []
    current = [exchange(color, 0) for color in range(BANDS)]
    for stage in (1, 2, 3):
        for color in range(BANDS):
            for copy in current[color]:
                copy.wait_recv()
            pending += current[color]
            if stage < 3:
                current[color] = exchange(color, stage)
    return pending


def sum_start(me, low, slots, send, recv):
    return [sum_exchange(me, color, 0, low, "xzy", slots, send, recv) for color in range(BANDS)]


def pick(left, axis, place):
    at = []
    for name in ("x_lo", "z", "y", "x_hi"):
        if name[0] in left:
            at.append(place[name] if name[0] == axis else slice(None))
    return tuple(at)


def sum_exchange(me, color, stage, source, left, slots, send, recv):
    axis = ORDER_SUM[color][stage]
    off, size = bands(slots[0][2].shape[1] + slots[1][2].shape[1] + slots[2][2].shape[1])[color]
    window = (pl.ds(off, size),) if stage == 0 else ()
    copies = []
    for d in (2, 1, 3):
        n = color * 9 + stage * 3 + d - 1
        part = source.at[pick(left, axis, me.along(axis, d)) + window]
        copies.append(
            remote(part, slots[color][stage].at[d - 1], send.at[n], recv.at[n], me.ring(axis, d))
        )
        copies[-1].start()
    return copies


def sum_finish(me, current, own, slots, sums, lows, finals, final, gathered, out_ref, send, recv, ga_s, ga_r):
    half = final.shape[0]
    lanes = final.shape[1]
    pending = []

    def arrived(color, stage, source, left, window=()):
        axis = ORDER_SUM[color][stage]
        pending.extend(current[color])
        for copy in current[color]:
            copy.wait_recv()
        total = source[pick(left, axis, me.along(axis, 0)) + window]
        for d in range(3):
            total += slots[color][stage][d].astype(f32)
        return total

    for color in range(BANDS):
        off, size = bands(half)[color]
        total = arrived(color, 0, own, "xzy", (pl.ds(off, size),))
        sums[color][...] = total
        lows[color][...] = total.astype(bf16)
        left = ORDER_SUM[color][1:]
        current[color] = sum_exchange(me, color, 1, lows[color], left, slots, send, recv)
    for color in range(BANDS):
        finals[color][...] = arrived(color, 1, sums[color], ORDER_SUM[color][1:])
        left = ORDER_SUM[color][2:]
        current[color] = sum_exchange(me, color, 2, finals[color], left, slots, send, recv)
    gathers = []
    for color in range(BANDS):
        off, size = bands(half)[color]
        total = arrived(color, 2, finals[color], ORDER_SUM[color][2:])
        final[pl.ds(off, size)] = total.astype(bf16)
        for m, (a, b) in enumerate(OTHERS):
            n = color * 7 + m
            gathers.append(
                remote(
                    final.at[pl.ds(off, size)], gathered.at[me.x_hi, me.y, pl.ds(off, size)],
                    ga_s.at[n], ga_r.at[n], me.piece(a, b),
                )
            )
            gathers[-1].start()
    for copy in gathers:
        copy.wait_recv()
    for a in range(2):
        for b in range(4):
            mine = (me.x_hi == a) & (me.y == b)
            part = jnp.where(mine, final[...].astype(f32), gathered[a, b].astype(f32))
            out_ref[a * half : (a + 1) * half, b * lanes : (b + 1) * lanes] = part
    return pending + gathers


def layer_kernel(
    heads, gain_ref, decay_ref, bias_ref, w_ref, h_ref, x_hbm, dy_hbm,
    x_ref, dy_ref, hid_ref, gw_ref,
    h_all, w_all, part, proj_in, proj_ref,
    run, run_t, step_t, step_c, key_t, query_t, key_hl, query_hl, scores,
    acc_diff, acc_cross, acc_const, dq, dk, dscores,
    state_in, state_out, grad_in, grad_out, state_own, grad_own,
    g_all, gt_all, own, low,
    slot_a0, slot_a1, slot_a2, sum_a0, sum_a1, sum_a2, low_a0, low_a1, low_a2,
    slot_b0, slot_b1, slot_b2, sum_b0, sum_b1, sum_b2,
    slot_c0, slot_c1, slot_c2, final, gathered, hid,
    load_h, load_xy, hs, hr, ag_s, ag_r, one_s, one_r, sf, rf, sb, rb,
    st_s, st_r, ga_s, ga_r, hid_s, hid_r,
):
    me = Place()
    k = me.ctx
    pieces = lax.axis_size("ctx")
    last = pieces - 1
    tokens = proj_ref.shape[0]
    half = tokens // 2
    chunks = heads // CHUNK
    cols, depth = w_ref.shape
    band, lanes = cols // 2, depth // 4
    right = {"ctx": lax.rem(k + 1, pieces)}
    left = {"ctx": lax.rem(k + pieces - 1, pieces)}

    def widened(ref):
        return jnp.concatenate([ref[...], jnp.zeros((1, NS - heads), f32)], axis=1)

    barrier = pltpu.get_barrier_semaphore()
    peers = [me.sibling()]
    peers += [me.ring("z", d) for d in (1, 2, 3)]
    peers += [me.ring("x", d) for d in (1, 3)]
    peers += [me.piece(a, b) for a, b in OTHERS]
    for peer in peers:
        pl.semaphore_signal(barrier, inc=1, device_id=peer, device_id_type=MESH)

    def load(s):
        return pltpu.make_async_copy(
            h_ref.at[:, me.columns(s, me.core, depth)], h_all.at[s, me.core], load_h.at[s]
        )

    def lend(s):
        return remote(
            h_ref.at[:, me.columns(s, 1 - me.core, depth)], h_all.at[s, me.core],
            hs.at[s], hr.at[s], me.sibling(),
        )

    load_x = pltpu.make_async_copy(x_hbm, x_ref, load_xy.at[0])
    load_dy = pltpu.make_async_copy(dy_hbm, dy_ref, load_xy.at[1])
    piece = pltpu.make_async_copy(
        w_ref.at[
            pl.ds(pl.multiple_of(me.x_hi * band, 16), band),
            pl.ds(pl.multiple_of(me.y * lanes, lanes), lanes),
        ],
        w_all.at[me.x_lo, me.z, me.y, me.x_hi],
        load_xy.at[2],
    )
    piece.start()
    loop(8, lambda s: load(s).start())
    part[...] = jnp.zeros_like(part)
    @pl.when(k == 0)
    def _():
        state_in[...] = jnp.zeros_like(state_in)

    @pl.when(k == last)
    def _():
        grad_in[...] = jnp.zeros_like(grad_in)

    dq[...] = jnp.zeros_like(dq)
    dk[...] = jnp.zeros_like(dk)
    dscores[...] = jnp.zeros_like(dscores)
    acc_diff[...] = jnp.zeros_like(acc_diff)
    acc_cross[...] = jnp.zeros_like(acc_cross)
    acc_const[...] = jnp.zeros_like(acc_const)

    piece.wait()
    pl.semaphore_wait(barrier, len(peers))
    loop(8, lambda s: lend(s).start())
    load_x.start()
    load_dy.start()

    pending = gather_weights(me, w_ref, w_all, ag_s, ag_r)

    def weights(s):
        parts = [w_all[s // 4, lax.rem(s, 4), b].reshape(cols, lanes) for b in range(4)]
        return jnp.concatenate(parts, axis=1)

    def project(s, side):
        part[side, :, :cols] += dot(h_all[s, side], weights(s), NT)

    def project_theirs(s):
        lend(s).wait_recv()
        project(s, 1 - me.core)

    def project_mine(s):
        load(s).wait()
        project(s, me.core)

    loop(8, project_theirs)
    give = remote(part.at[1 - me.core], proj_in, one_s.at[0], one_r.at[0], me.sibling())
    give.start()
    loop(8, project_mine)
    give.wait_recv()
    pending.append(give)
    proj_ref[...] = part[me.core] + proj_in[...]

    rows = lax.broadcasted_iota(jnp.int32, (tokens, tokens), 0)
    columns_at = lax.broadcasted_iota(jnp.int32, (tokens, tokens), 1)
    key = proj_ref[:, :NS]
    query = proj_ref[:, NS : 2 * NS] * NS ** (-0.5)
    pre = proj_ref[:, 2 * NS :] + widened(bias_ref)
    rate = jnp.exp(widened(decay_ref))
    steps = jnp.maximum(pre, 0.0) + jnp.log1p(jnp.exp(-jnp.abs(pre)))
    running = dot_high((rows >= columns_at).astype(f32), -rate * steps)
    run[...] = running
    run_t[...] = running.T
    step_c[...] = steps
    step_t[...] = steps.T
    key_t[...] = key.T
    query_t[...] = query.T
    high, low_part = split(key)
    key_hl[:, :NS] = high
    key_hl[:, NS:] = low_part
    high, low_part = split(query)
    query_hl[:, :NS] = high
    query_hl[:, NS:] = low_part
    scores[...] = dot_high(query, key, NT)
    load_x.wait()
    load_dy.wait()

    def copy_fwd(h):
        return remote(state_out.at[h], state_in.at[h], sf.at[h], rf.at[h], right)

    def copy_bwd(h):
        return remote(grad_out.at[h], grad_in.at[h], sb.at[h], rb.at[h], left)

    def columns(h, count=1):
        return pl.ds(pl.multiple_of(h * PS, PS), count * PS)

    def prepare(j):
        made = []
        for u in range(CHUNK):
            h = j * CHUNK + u
            r_row = run_t[pl.ds(h, 1), :]
            r_end = r_row[:, tokens - 1 : tokens]
            high, low_part = split(key_t[...] * (jnp.exp(r_end - r_row) * step_t[pl.ds(h, 1), :]))
            x = x_ref[:, columns(h)]
            state = dot(high, x) + dot(low_part, x)
            high, low_part = split(query_t[...] * jnp.exp(r_row))
            dy = dy_ref[:, columns(h)]
            made.append((h, state, dot(high, dy) + dot(low_part, dy)))
        for h, state, grad in made:
            state_own[h] = state
            grad_own[h] = grad

    def decay_of(h):
        return jnp.exp(run_t[pl.ds(h, 1), :][:, tokens - 1 : tokens])

    def forward(j):
        for u in range(CHUNK):
            h = j * CHUNK + u

            @pl.when(k > 0)
            def _():
                copy_fwd(h).wait_recv()

            @pl.when(k < last)
            def _():
                carried = decay_of(h) * state_in[h].astype(f32)
                state_out[h] = (carried + state_own[h]).astype(bf16)
                copy_fwd(h).start()

    def backward(j):
        for u in range(CHUNK):
            h = j * CHUNK + u

            @pl.when(k < last)
            def _():
                copy_bwd(h).wait_recv()

            @pl.when(k > 0)
            def _():
                carried = decay_of(h) * grad_in[h].astype(f32)
                grad_out[h] = (carried + grad_own[h]).astype(bf16)
                copy_bwd(h).start()

    def one_head(h):
        lane = lax.broadcasted_iota(jnp.int32, (tokens, NS), 1)
        at_h = lane == h
        r_col = jnp.sum(jnp.where(at_h, run[...], 0.0), axis=1, keepdims=True)
        s_col = jnp.sum(jnp.where(at_h, step_c[...], 0.0), axis=1, keepdims=True)
        r_row = run_t[pl.ds(h, 1), :]
        s_row = step_t[pl.ds(h, 1), :]
        r_end = r_row[:, tokens - 1 : tokens]
        x = x_ref[:, columns(h)]
        dy = dy_ref[:, columns(h)]
        gain = gain_ref[h]

        def decays(begin, width):
            t = lax.broadcasted_iota(jnp.int32, (half, width), 0) + begin
            s = lax.broadcasted_iota(jnp.int32, (half, width), 1)
            gaps = r_col[begin : begin + half] - r_row[:, :width]
            return jnp.exp(jnp.where(t >= s, gaps, -1e30)) * s_row[:, :width]

        top = decays(0, half)
        bottom = decays(half, tokens)
        mix_top = (top * scores[:half, :half]).astype(bf16)
        mix_bottom = (bottom * scores[half:, :]).astype(bf16)
        ds_top = top * dot(dy[:half], x[:half], NT)
        ds_bottom = bottom * dot(dy[half:], x, NT)
        y = jnp.concatenate([dot(mix_top, x[:half]), dot(mix_bottom, x)], axis=0)
        dx = dot(mix_bottom, dy[half:], TN)
        dx = jnp.concatenate([dx[:half] + dot(mix_top, dy[:half], TN), dx[half:]], axis=0)

        state = state_in[h]
        grad = grad_in[h]
        from_start = jnp.exp(r_col)
        to_end = jnp.exp(r_end - r_col) * s_col
        y += from_start * dot(query_hl[...], jnp.concatenate([state, state], axis=0))
        carried = to_end * dot(key_hl[...], jnp.concatenate([grad, grad], axis=0))
        dx += carried
        dq_h = from_start * dot(dy, state, NT)
        dk_h = to_end * dot(x, grad, NT)
        xf = x.astype(f32)
        dyf = dy.astype(f32)
        y_out = (y + gain * xf).astype(bf16)
        dx_out = (dx + gain * dyf).astype(bf16)
        cross = xf * dx
        cross_h = jnp.sum(cross, axis=1, keepdims=True)
        diff_h = jnp.sum(dyf * y - cross, axis=1, keepdims=True)
        inner = jnp.sum(grad.astype(f32) * state.astype(f32), axis=0, keepdims=True)
        inner = jnp.sum(inner, axis=1, keepdims=True)
        outer = jnp.sum(jnp.sum(xf * carried, axis=0, keepdims=True), axis=1, keepdims=True)
        const_h = jnp.exp(r_end) * inner + outer
        return at_h, ds_top, ds_bottom, dq_h, dk_h, y_out, dx_out, cross_h, diff_h, const_h

    def compute(j):
        done = [one_head(j * CHUNK + u) for u in range(CHUNK)]
        ats, ds_tops, ds_bottoms, dqs, dks, ys, dxs, crosses, diffs, consts = zip(*done)
        dscores[:half, :half] += sum(ds_tops[1:], ds_tops[0])
        dscores[half:, :] += sum(ds_bottoms[1:], ds_bottoms[0])
        dq[...] += sum(dqs[1:], dqs[0])
        dk[...] += sum(dks[1:], dks[0])
        cross, diff, const = acc_cross[...], acc_diff[...], acc_const[...]
        for u in range(CHUNK):
            cross = jnp.where(ats[u], crosses[u], cross)
            diff = jnp.where(ats[u], diffs[u], diff)
            const = jnp.where(ats[u][:8], consts[u], const)
        acc_cross[...] = cross
        acc_diff[...] = diff
        acc_const[...] = const
        for u in range(CHUNK):
            x_ref[:, columns(j * CHUNK + u)] = ys[u]
            dy_ref[:, columns(j * CHUNK + u)] = dxs[u]

    extra = LAG_FAR - LAG
    start_f = LAG * k + extra * (k // 4)
    start_b = LAG * (last - k) + extra * ((last - k) // 4)
    start_c = LAG * last + extra

    def iteration(i):
        jf = i - start_f
        jb = i - start_b
        jc = i - start_c

        @pl.when(i < chunks)
        def _():
            prepare(i)

        @pl.when((jf >= 0) & (jf < chunks))
        def _():
            forward(jf)

        @pl.when((jb >= 0) & (jb < chunks))
        def _():
            backward(jb)

        @pl.when((jc >= 0) & (jc < chunks))
        def _():
            compute(jc)

    loop(chunks + LAG * last + extra, iteration)

    key = proj_ref[:, :NS]
    query = proj_ref[:, NS : 2 * NS] * NS ** (-0.5)
    pre = proj_ref[:, 2 * NS :] + widened(bias_ref)
    d_log = dot_high((columns_at >= rows).astype(f32), acc_diff[...]) + acc_const[0:1, :]
    slope = 1.0 / (1.0 + jnp.exp(-pre))
    ratio = jnp.where(pre < -20.0, 1.0, slope / step_c[...])
    dk_all = dk[...] + dot_high(dscores[...].T, query)
    dq_all = (dq[...] + dot_high(dscores[...], key)) * NS ** (-0.5)
    dz_all = acc_cross[...] * ratio - rate * d_log * slope
    g_mine = g_all.at[me.core]
    gt_mine = gt_all.at[me.core]
    for n, grads in enumerate((dk_all, dq_all, dz_all)):
        g_mine[:, n * NS : (n + 1) * NS] = grads.astype(bf16)
        gt_mine[n * NS : (n + 1) * NS, :] = grads.T.astype(bf16)
    give_t = remote(gt_mine, gt_mine, one_s.at[1], one_r.at[1], me.sibling())
    give_g = remote(g_mine, g_mine, one_s.at[2], one_r.at[2], me.sibling())
    give_t.start()
    give_g.start()
    pending += [give_t, give_g]

    def weight_grad(s, side, more):
        p = dot(gt_all[side, :cols], h_all[s, side])
        for b in range(4):
            for a in range(2):
                at = (s // 4, lax.rem(s, 4), b, a)
                block = p[a * band : (a + 1) * band, b * lanes : (b + 1) * lanes]
                if more:
                    block += own[at]
                    low[at] = block.astype(bf16)
                own[at] = block

    loop(8, lambda s: weight_grad(s, me.core, False))
    give_t.wait_recv()
    loop(8, lambda s: weight_grad(s, 1 - me.core, True))
    slots = (
        (slot_a0, slot_b0, slot_c0), (slot_a1, slot_b1, slot_c1), (slot_a2, slot_b2, slot_c2)
    )
    current = sum_start(me, low, slots, st_s, st_r)
    give_g.wait_recv()

    def give_hid(s):
        return remote(
            hid.at[s], hid_ref.at[:, me.columns(s, me.core, depth)],
            hid_s.at[s], hid_r.at[s], me.sibling(),
        )

    def hidden(s):
        theirs = g_all[1 - me.core]
        hid[s] = dot(theirs[:, :cols], weights(s)).astype(bf16)
        give_hid(s).start()
        hid_ref[:, me.columns(s, me.core, depth)] = dot(
            g_all[me.core, :, :cols], weights(s)
        ).astype(bf16)

    loop(8, hidden)
    pending += sum_finish(
        me, current, own, slots, (sum_a0, sum_a1, sum_a2), (low_a0, low_a1, low_a2),
        (sum_b0, sum_b1, sum_b2), final, gathered, gw_ref, st_s, st_r, ga_s, ga_r,
    )
    for copy in pending:
        copy.wait_send()

    def finish(s):
        lend(s).wait_send()
        give_hid(s).wait_send()
        give_hid(s).wait_recv()

    loop(8, finish)

    @pl.when(k < last)
    def _():
        loop(heads, lambda h: copy_fwd(h).wait_send())

    @pl.when(k > 0)
    def _():
        loop(heads, lambda h: copy_bwd(h).wait_send())


def layer(gain, decay, bias, weight_t, h, x, dy):
    tokens, width = x.shape
    heads = width // PS
    chunks = heads // CHUNK
    cols, depth = weight_t.shape
    half, lanes = cols // 2, depth // 4
    sizes = [size for _, size in bands(half)]
    vm = pl.BlockSpec(memory_space=pltpu.VMEM)
    hbm = pl.BlockSpec(memory_space=pl.ANY)
    states = pltpu.VMEM((heads, NS, PS), bf16)
    own_states = pltpu.VMEM((heads, NS, PS), f32)
    by_token = pltpu.VMEM((tokens, NS), f32)
    by_state = pltpu.VMEM((NS, tokens), f32)
    square = pltpu.VMEM((tokens, tokens), f32)
    two_parts = pltpu.VMEM((tokens, 2 * NS), bf16)

    def shape(left, color):
        dims = {"x_lo": 2, "z": 4, "y": 4, "x_hi": 2}
        return tuple(n for name, n in dims.items() if name[0] in left) + (sizes[color], lanes)

    def sem(n):
        return pltpu.SemaphoreType.DMA((n,))

    everyone = range(BANDS)
    one = [shape(ORDER_SUM[c][1:], c) for c in everyone]
    two = [shape(ORDER_SUM[c][2:], c) for c in everyone]
    end = [shape("", c) for c in everyone]
    whole = (2, 4, 4, 2, half, lanes)
    return pl.pallas_call(
        partial(layer_kernel, heads),
        out_shape=(
            pltpu.VMEM(x.shape, bf16),
            pltpu.VMEM(x.shape, bf16),
            pltpu.VMEM(h.shape, bf16),
            pltpu.VMEM((cols, depth), f32),
        ),
        in_specs=[pl.BlockSpec(memory_space=pltpu.SMEM), vm, vm, hbm, hbm, hbm, hbm],
        out_specs=(vm, vm, vm, vm),
        scratch_shapes=[
            pltpu.VMEM((8, 2, tokens, depth), bf16),
            pltpu.VMEM(whole, bf16),
            pltpu.VMEM((2, tokens, 3 * NS), f32),
            pltpu.VMEM((tokens, 3 * NS), f32),
            pltpu.VMEM((tokens, 3 * NS), f32),
            by_token, by_state, by_state, by_token, by_state, by_state,
            two_parts, two_parts, square,
            by_token, by_token, pltpu.VMEM((8, NS), f32), by_token, by_token, square,
            states, states, states, states, own_states, own_states,
            pltpu.VMEM((2, tokens, 3 * NS), bf16),
            pltpu.VMEM((2, 3 * NS, tokens), bf16),
            pltpu.VMEM(whole, f32),
            pltpu.VMEM(whole, bf16),
        ]
        + [pltpu.VMEM((3,) + s, bf16) for s in one]
        + [pltpu.VMEM(s, f32) for s in one]
        + [pltpu.VMEM(s, bf16) for s in one]
        + [pltpu.VMEM((3,) + s, bf16) for s in two]
        + [pltpu.VMEM(s, f32) for s in two]
        + [pltpu.VMEM((3,) + s, f32) for s in end]
        + [
            pltpu.VMEM((half, lanes), bf16),
            pltpu.VMEM((2, 4, half, lanes), bf16),
            pltpu.VMEM((8, tokens, depth), bf16),
            sem(8), sem(3), sem(8), sem(8), sem(27), sem(27), sem(3), sem(3),
            sem(heads), sem(heads), sem(heads), sem(heads),
            sem(27), sem(27), sem(21), sem(21), sem(8), sem(8),
        ],
        compiler_params=pltpu.CompilerParams(
            collective_id=0, has_side_effects=True, vmem_limit_bytes=46 * 2**20
        ),
    )(gain, decay, bias, weight_t, h, x, dy)


def store_kernel(*refs):
    sems = refs[8]
    copies = []
    for source, target in zip(refs[:4], refs[4:8]):
        rows = source.shape[0] // 4
        for part in range(4):
            at = pl.ds(part * rows, rows)
            copies.append(
                pltpu.make_async_copy(source.at[at], target.at[at], sems.at[len(copies)])
            )
            copies[-1].start()
    for copy in copies:
        copy.wait()


def store(*arrays):
    hbm = pl.BlockSpec(memory_space=pl.ANY)
    vm = pl.BlockSpec(memory_space=pltpu.VMEM)
    return pl.pallas_call(
        store_kernel,
        out_shape=tuple(jax.ShapeDtypeStruct(a.shape, a.dtype) for a in arrays),
        in_specs=[vm] * 4,
        out_specs=(hbm,) * 4,
        scratch_shapes=[pltpu.SemaphoreType.DMA((16,))],
        compiler_params=pltpu.CompilerParams(vmem_limit_bytes=16 * 2**20),
    )(*arrays)


def shards(hidden_rows, inner_rows, weight_proj, decay_log, step_bias, skip_gain, grad_output):
    token_rows = hidden_rows.reshape(-1, hidden_rows.shape[-1])
    value_rows = inner_rows.reshape(-1, inner_rows.shape[-1])
    cotangent = grad_output.reshape(value_rows.shape)
    output, grad_values, grad_tokens, grad_weight_t = layer(
        skip_gain, decay_log[None], step_bias[None], weight_proj.T, token_rows, value_rows, cotangent
    )
    output, grad_values, grad_tokens, grad_weight_t = store(
        output, grad_values, grad_tokens, grad_weight_t
    )
    return (
        output.reshape(inner_rows.shape),
        grad_values.reshape(inner_rows.shape),
        grad_tokens.reshape(hidden_rows.shape),
        grad_weight_t.T,
    )


def solution(mesh):
    rows = P("dp", "ctx", None)
    return jax.shard_map(
        shards,
        mesh=mesh,
        in_specs=(rows, rows, P("dp", None), P(), P(), P(), rows),
        out_specs=(rows, rows, rows, P("dp", None)),
        check_vma=False,
    )
```
